32 devices in a mesh: dp: 4 (over y, core), ctx: 8 (over z, x).
Axes of the slice: x: 2, y: 2, z: 4, core: 2. Of those that a mesh axis runs over, the one named last changes fastest.
Arguments:
- tokens: bfloat16 [4, 1024, 1024], P('dp', 'ctx'), may hold values from -6 to 6
- w_qkv: bfloat16 [1024, 3072], P(('dp', 'ctx')), may hold values from -0.1875 to 0.1875
- b_query: bfloat16 [1024], P(('dp', 'ctx')), may hold values from -3 to 3
- b_value: bfloat16 [1024], P(('dp', 'ctx')), may hold values from -3 to 3
- w_out: bfloat16 [1024, 1024], P(('dp', 'ctx')), may hold values from -3 to 3
- b_out: bfloat16 [1024], P(('dp', 'ctx')), may hold values from -3 to 3
- ln1_gain: bfloat16 [1024], P(('dp', 'ctx')), may hold values from 0.25 to 1.75
- ln1_bias: bfloat16 [1024], P(('dp', 'ctx')), may hold values from -3 to 3
- w_up: bfloat16 [1024, 4096], P(('dp', 'ctx')), may hold values from -0.1875 to 0.1875
- b_up: bfloat16 [4096], P(('dp', 'ctx')), may hold values from -3 to 3
- w_down: bfloat16 [4096, 1024], P(('dp', 'ctx')), may hold values from -0.09375 to 0.09375
- b_down: bfloat16 [1024], P(('dp', 'ctx')), may hold values from -3 to 3
- ln2_gain: bfloat16 [1024], P(('dp', 'ctx')), may hold values from 0.25 to 1.75
- ln2_bias: bfloat16 [1024], P(('dp', 'ctx')), may hold values from -3 to 3
- segment_ids: int32 [4, 1024], P('dp', 'ctx'), may hold values from 0 to 3, as said below
- pad_mask: int32 [4, 1024], P('dp', 'ctx'), may hold values 0 or 1
- cotangent: bfloat16 [4, 1024, 1024], P('dp', 'ctx'), may hold values from -6 to 6
Outputs:
- layer_out: bfloat16 [4, 1024, 1024], P('dp', 'ctx')
- input_grad: bfloat16 [4, 1024, 1024], P('dp', 'ctx')
- grad_w_qkv: float32 [1024, 3072], P(('dp', 'ctx'))
- grad_b_query: float32 [1024], P(('dp', 'ctx'))
- grad_b_value: float32 [1024], P(('dp', 'ctx'))
- grad_w_out: float32 [1024, 1024], P(('dp', 'ctx'))
- grad_b_out: float32 [1024], P(('dp', 'ctx'))
- grad_ln1_gain: float32 [1024], P(('dp', 'ctx'))
- grad_ln1_bias: float32 [1024], P(('dp', 'ctx'))
- grad_w_up: float32 [1024, 4096], P(('dp', 'ctx'))
- grad_b_up: float32 [4096], P(('dp', 'ctx'))
- grad_w_down: float32 [4096, 1024], P(('dp', 'ctx'))
- grad_b_down: float32 [1024], P(('dp', 'ctx'))
- grad_ln2_gain: float32 [1024], P(('dp', 'ctx'))
- grad_ln2_bias: float32 [1024], P(('dp', 'ctx'))
The draws below stay inside these ranges and needn't reach their ends.
Inputs may be any that keep to these rules, and one draw needn't show every extreme that they name: `segment_ids`: along each sequence the document numbers never fall, and each of 0 to 3 appears.
All inputs are finite; a program needn't handle non-finite values. No bound on the sum of `pad_mask` on one device may be relied on, other than what follows from the above.
Results may differ from the reference program's by a relative error of at most 0.015.
Values may be sent and summed in bfloat16 or wider, within the bound.
No kernel may reach another device: no remote copies, remote signals or barrier semaphores. Data moves between devices by JAX's collectives and lax.ppermute only.
A program may use at most 320 MiB of HBM per device.

```python
import jax
import jax.numpy as jnp
from jax import lax

D = 1024
HEADS = 16
HEAD = 64
FF = 4096
WINDOW = 1024
DOCS = 4
LENGTH = 1024
SEQS = 4


def draw_segment_ids(key, part):
    key = jax.random.fold_in(key, 11)

    def one_sequence(sequence_key):
        shuffled = jax.random.permutation(sequence_key, LENGTH - 1) + 1
        boundaries = shuffled[:DOCS - 1]
        positions = jnp.arange(LENGTH, dtype=jnp.int32)
        return jnp.sum((positions[:, None] >= boundaries[None, :]).astype(jnp.int32), axis=1).astype(jnp.int32)
    return jax.vmap(one_sequence)(jax.random.split(key, SEQS))


def touch_ends(values, rng, smallest, largest):
    shape = values.shape
    spot = [jax.random.randint(jax.random.fold_in(rng, axis), (), 0, shape[axis]) for axis in range(len(shape))]
    values = values.at[tuple(spot)].set(smallest)
    longest = shape.index(max(shape))
    spot[longest] = (spot[longest] + 1) % shape[longest]
    return values.at[tuple(spot)].set(largest)


def raised(array, stream_key, source, target, shards_of, factor):
    owner, partner = [(jnp.arange(array.shape[dim]) // (array.shape[dim] // shards_of)).reshape([-1 if axis == dim else 1 for axis in range(array.ndim)]) for dim in (source, target)]
    chosen = jax.random.permutation(stream_key, shards_of)[partner]
    strong = (owner == chosen) | (owner == (partner + shards_of // 2) % shards_of)
    return jnp.where(strong, factor * array, array)


def levels(own_key, shape, cuts, low, high):
    gain = 1.0
    for dim, blocks in cuts:
        draws = jax.random.uniform(jax.random.fold_in(jax.random.fold_in(own_key, 6), dim), (blocks,), jnp.float32, low / len(cuts), high / len(cuts))
        gain = gain * jnp.repeat(jnp.exp(draws), shape[dim] // blocks).reshape((-1,) + (1,) * (len(shape) - 1 - dim))
    return gain


def bell_draw(key, extent, scale, limit, cuts=(), kind=jnp.bfloat16):
    array = scale * jax.random.normal(key, extent, jnp.float32)
    if cuts:
        array = array * levels(key, extent, cuts, -0.22, 0.18)
    return jnp.clip(array, -limit, limit).astype(kind)


def heavy_noise(stream_key, dims, scale, most, shards, heavy, kind=jnp.bfloat16):
    array = scale * jax.random.normal(stream_key, dims, jnp.float32)
    if shards:
        array = array * levels(stream_key, dims, shards, -0.22, 0.18)
    return jnp.clip(raised(array, jax.random.fold_in(stream_key, 3), *heavy), -most, most).astype(kind)


def setup_inputs(seed: int = 0) -> dict:
    key_list = jax.random.split(jax.random.key(seed), 18)
    tokens = heavy_noise(key_list[0], (SEQS, LENGTH, D), 1.0, 6.0, ((0, 4), (1, 8)), (1, 2, 8, 2.0))
    w_qkv = bell_draw(key_list[1], (D, 3 * D), D ** -0.5, 0.1875, ((0, 32),))
    b_query = bell_draw(key_list[2], (D,), 0.5, 3.0, ((0, 32),))
    b_value = bell_draw(key_list[3], (D,), 0.5, 3.0, ((0, 32),))
    w_out = bell_draw(key_list[4], (D, D), (max(D // 256, 1)) ** -0.5, 3.0, ((0, 32),))
    b_out = bell_draw(key_list[5], (D,), 0.5, 3.0, ((0, 32),))
    ln1_gain = jnp.clip(1.0 + 0.15 * jax.random.normal(key_list[6], (D,), jnp.float32), 0.25, 1.75).astype(jnp.bfloat16)
    ln1_bias = bell_draw(key_list[7], (D,), 0.5, 3.0, ((0, 32),))
    w_up = bell_draw(key_list[8], (D, FF), D ** -0.5, 0.1875, ((0, 32),))
    b_up = bell_draw(key_list[9], (FF,), 0.5, 3.0, ((0, 32),))
    w_down = bell_draw(key_list[10], (FF, D), FF ** -0.5, 0.09375, ((0, 32),))
    b_down = bell_draw(key_list[11], (D,), 0.5, 3.0, ((0, 32),))
    ln2_gain = jnp.clip(1.0 + 0.15 * jax.random.normal(key_list[12], (D,), jnp.float32), 0.25, 1.75).astype(jnp.bfloat16)
    ln2_bias = bell_draw(key_list[13], (D,), 0.5, 3.0, ((0, 32),))
    segment_ids = draw_segment_ids(jax.random.fold_in(key_list[17], 71), 0)
    pad_mask = touch_ends((jax.random.randint(key_list[15], (SEQS, LENGTH), 0, 8) < 7).astype(jnp.int32), jax.random.fold_in(key_list[15], 1), 0, 1)
    cotangent = bell_draw(key_list[16], (SEQS, LENGTH, D), 1.0, 6.0, ((0, 4), (1, 8)))
    return dict(tokens=tokens, w_qkv=w_qkv, b_query=b_query, b_value=b_value, w_out=w_out, b_out=b_out, ln1_gain=ln1_gain, ln1_bias=ln1_bias, w_up=w_up, b_up=b_up, w_down=w_down, b_down=b_down, ln2_gain=ln2_gain, ln2_bias=ln2_bias, segment_ids=segment_ids, pad_mask=pad_mask, cotangent=cotangent)


MASKED = -1e+30
EPSILON = 1e-05

@jax.custom_vjp
def low(v):
    return lax.optimization_barrier(v.astype(jnp.bfloat16)).astype(jnp.float32)

@jax.custom_vjp
def low_back(v):
    return v

def low_keep(v):
    return (low(v), None)

def low_pass(kept, grad):
    return (grad,)

def back_keep(v):
    return (v, None)

def back_low(kept, grad):
    return (low(grad),)
low.defvjp(low_keep, low_pass)
low_back.defvjp(back_keep, back_low)

def product(left, right):
    return jnp.dot(left, right, precision=lax.Precision.HIGHEST, preferred_element_type=jnp.float32)

def layer_norm(values, scales, offsets):
    average = lax.optimization_barrier(jnp.mean(values, axis=-1, keepdims=True))
    centred = values - average
    variance = lax.optimization_barrier(jnp.mean(centred * centred, axis=-1, keepdims=True))
    return centred * lax.rsqrt(variance + EPSILON) * scales + offsets

def allowed_keys(query_tags, query_place, key_tags, key_place):
    same_doc = query_tags[:, None] // 2 == key_tags[None, :] // 2
    distance = jnp.abs(query_place[:, None] - key_place[None, :])
    usable = (key_tags[None, :] % 2 == 1) | (distance == 0)
    return same_doc & (distance <= WINDOW // 2) & usable

def attend_sequence(queries, keys, values, token_tags):
    seq_length = queries.shape[0]
    margin = WINDOW // 2
    block_rows = min(512, seq_length)
    key_rows = block_rows + 2 * margin
    padding = jnp.zeros((margin, HEADS, HEAD), jnp.float32)
    keys_padded = jnp.concatenate([padding, keys, padding], axis=0)
    values_padded = jnp.concatenate([padding, values, padding], axis=0)
    tag_padding = jnp.zeros((margin,), jnp.int32)
    tags_padded = jnp.concatenate([tag_padding, token_tags, tag_padding], axis=0)

    def one_block(block_index):
        first_row = (block_index * block_rows).astype(jnp.int32)
        query_block = lax.dynamic_slice_in_dim(queries, first_row, block_rows, 0)
        key_block = lax.dynamic_slice_in_dim(keys_padded, first_row, key_rows, 0)
        value_block = lax.dynamic_slice_in_dim(values_padded, first_row, key_rows, 0)
        query_tags = lax.dynamic_slice_in_dim(token_tags, first_row, block_rows, 0)
        key_tags = lax.dynamic_slice_in_dim(tags_padded, first_row, key_rows, 0)
        query_place = first_row + jnp.arange(block_rows, dtype=jnp.int32)
        key_place = first_row - margin + jnp.arange(key_rows, dtype=jnp.int32)
        allowed = allowed_keys(query_tags, query_place, key_tags, key_place)
        raw = jnp.einsum('qhd,khd->hqk', query_block, key_block, precision=lax.Precision.HIGHEST) * 0.125
        raw = low_back(raw)
        scores = jnp.where(allowed[None], raw, MASKED)
        totals = jax.nn.logsumexp(scores, axis=2, keepdims=True)
        probs = low(jnp.exp(scores - totals))
        return jnp.einsum('hqk,khd->qhd', probs, value_block, precision=lax.Precision.HIGHEST)
    blocks = lax.map(jax.checkpoint(one_block), jnp.arange(seq_length // block_rows, dtype=jnp.int32))
    return blocks.reshape(seq_length, HEADS * HEAD)

def layer(params, inputs, token_tags):
    w_qkv, b_query, b_value, w_out, b_out, ln1_gain, ln1_bias, w_up, b_up, w_down, b_down, ln2_gain, ln2_bias = params
    model_width = inputs.shape[2]
    results = []
    for sequence in range(inputs.shape[0]):
        tokens = inputs[sequence]
        seq_length = tokens.shape[0]
        mixed = product(tokens, w_qkv)
        queries = low(low_back(mixed[:, :model_width] + b_query))
        keys = low(low_back(mixed[:, model_width:2 * model_width]))
        values = low(low_back(mixed[:, 2 * model_width:] + b_value))
        attended = attend_sequence(queries.reshape(seq_length, HEADS, HEAD), keys.reshape(seq_length, HEADS, HEAD), values.reshape(seq_length, HEADS, HEAD), token_tags[sequence])
        attended = low(low_back(attended))
        branch = low_back(product(attended, w_out) + b_out)
        normed = layer_norm(tokens + branch, ln1_gain, ln1_bias)
        hidden = low_back(product(low(normed), w_up) + b_up)
        active = low(jax.nn.gelu(hidden, approximate=False))
        outcome = low_back(product(active, w_down) + b_down)
        results.append(layer_norm(normed + outcome, ln2_gain, ln2_bias))
    return jnp.stack(results)

def reference(tokens, w_qkv, b_query, b_value, w_out, b_out, ln1_gain, ln1_bias, w_up, b_up, w_down, b_down, ln2_gain, ln2_bias, segment_ids, pad_mask, cotangent):
    token_tags = (2 * (segment_ids + 1) + pad_mask).astype(jnp.int32)
    params = tuple((weight.astype(jnp.float32) for weight in (w_qkv, b_query, b_value, w_out, b_out, ln1_gain, ln1_bias, w_up, b_up, w_down, b_down, ln2_gain, ln2_bias)))
    inputs = tokens.astype(jnp.float32)
    result, pull_back = jax.vjp(lambda weights, values: layer(weights, values, token_tags), params, inputs)
    grad_params, grad_inputs = pull_back(cotangent.astype(jnp.float32))
    return (result.astype(jnp.bfloat16), grad_inputs.astype(jnp.bfloat16), grad_params[0], grad_params[1], grad_params[2], grad_params[3], grad_params[4], grad_params[5], grad_params[6], grad_params[7], grad_params[8], grad_params[9], grad_params[10], grad_params[11], grad_params[12])
```

```python
from functools import partial

import jax
import jax.numpy as jnp
from jax import lax
from jax.sharding import Mesh
from jax.sharding import PartitionSpec as P

HEADS = 16
HEAD = 64
WINDOW = 1024


MASKED = -1e30
EPSILON = 1e-05


def layer_norm(values, scales, offsets):
    average = jnp.mean(values, axis=-1, keepdims=True)
    centred = values - average
    variance = jnp.mean(centred * centred, axis=-1, keepdims=True)
    return centred * lax.rsqrt(variance + EPSILON) * scales + offsets


def matmul(left, right):
    return jnp.dot(left, right, preferred_element_type=jnp.float32)


def rows_product(left, right):
    return lax.dot_general(
        left, right, (((0,), (0,)), ((), ())), preferred_element_type=jnp.float32
    )


def cols_product(left, right):
    return lax.dot_general(
        left, right, (((1,), (1,)), ((), ())), preferred_element_type=jnp.float32
    )


def split_heads(matrix):
    return matrix.reshape(matrix.shape[0], HEADS, HEAD)


def allowed_keys(query_tags, query_place, key_tags, key_place):
    same_doc = query_tags[:, None] // 2 == key_tags[None, :] // 2
    distance = jnp.abs(query_place[:, None] - key_place[None, :])
    usable = (key_tags[None, :] % 2 == 1) | (distance == 0)
    return same_doc & (distance <= WINDOW // 2) & usable


def masked_scores(query_block, key_heads, query_tags, query_place, key_tags, key_place):
    raw = (
        jnp.einsum("qhd,khd->hqk", query_block, key_heads, preferred_element_type=jnp.float32)
        * 0.125
    )
    return jnp.where(allowed_keys(query_tags, query_place, key_tags, key_place)[None], raw, MASKED)


def attend_forward(
    query_heads, key_heads, value_heads, query_tags, query_place, key_tags, key_place
):
    row_count = query_heads.shape[0]
    block_rows = min(row_count, 512)

    def one_block(block_index):
        scores = masked_scores(query_heads, key_heads, query_tags, query_place, key_tags, key_place)
        totals = jax.nn.logsumexp(scores, axis=2)
        probs = jnp.exp(scores - totals[:, :, None]).astype(jnp.bfloat16)
        output = jnp.einsum("hqk,khd->qhd", probs, value_heads, preferred_element_type=jnp.float32)
        return (output, totals)

    outputs, totals = lax.map(one_block, jnp.arange(row_count // block_rows, dtype=jnp.int32))
    return (outputs.reshape(row_count, HEADS * HEAD), totals)


def attend_backward(
    query_heads,
    key_heads,
    value_heads,
    grad_heads,
    deltas,
    totals,
    query_tags,
    query_place,
    key_tags,
    key_place,
):
    row_count = query_heads.shape[0]
    block_rows = min(row_count, 512)

    def one_block(running, block_index):
        key_grad, value_grad = running
        scores = masked_scores(query_heads, key_heads, query_tags, query_place, key_tags, key_place)
        probs = jnp.exp(scores - totals[block_index][:, :, None])
        dprobs = jnp.einsum(
            "qhd,khd->hqk", grad_heads, value_heads, preferred_element_type=jnp.float32
        )
        dscores = (probs * (dprobs - deltas[:, :, None])).astype(jnp.bfloat16)
        query_grad = (
            jnp.einsum("hqk,khd->qhd", dscores, key_heads, preferred_element_type=jnp.float32)
            * 0.125
        )
        key_grad = (
            key_grad
            + jnp.einsum("hqk,qhd->khd", dscores, query_heads, preferred_element_type=jnp.float32)
            * 0.125
        )
        value_grad = value_grad + jnp.einsum(
            "hqk,qhd->khd",
            probs.astype(jnp.bfloat16),
            grad_heads,
            preferred_element_type=jnp.float32,
        )
        return ((key_grad, value_grad), query_grad)

    zeros = jnp.zeros(key_heads.shape, jnp.float32)
    (key_grad, value_grad), query_grads = lax.scan(
        one_block, (zeros, zeros), jnp.arange(row_count // block_rows, dtype=jnp.int32)
    )
    key_count = key_heads.shape[0]
    return (
        query_grads.reshape(row_count, HEADS * HEAD),
        key_grad.reshape(key_count, HEADS * HEAD),
        value_grad.reshape(key_count, HEADS * HEAD),
    )


def clip_window(whole, rows_here, seq_length, own_index):
    neighbours = (WINDOW // 2 + rows_here - 1) // rows_here
    key_span = min((2 * neighbours + 1) * rows_here, seq_length)
    first_key = jnp.clip((own_index - neighbours) * rows_here, 0, seq_length - key_span)
    window = tuple((lax.dynamic_slice_in_dim(member, first_key, key_span, 0) for member in whole))
    return (window, first_key)


def window_keys(items, rows_here, seq_length, own_index):
    whole = (
        lax.all_gather(items[0], "ctx", axis=0, tiled=True),
        lax.all_gather(items[1], "ctx", axis=0, tiled=True),
        lax.all_gather(items[2], "ctx", axis=0, tiled=True),
    )
    return clip_window(whole, rows_here, seq_length, own_index)


def window_keys_again(items, rows_here, seq_length, own_index):
    whole = (
        lax.all_gather(items[0], "ctx", axis=0, tiled=True),
        lax.all_gather(items[1], "ctx", axis=0, tiled=True),
        lax.all_gather(items[2], "ctx", axis=0, tiled=True),
    )
    return clip_window(whole, rows_here, seq_length, own_index)


def return_key_grads(key_grad, value_grad, rows_here, first_key):
    width = key_grad.shape[1]
    joined = jnp.concatenate([key_grad, value_grad], axis=1)
    key_span = joined.shape[0]
    count = rows_here * lax.axis_size("ctx")
    padding = jnp.zeros((count, 2 * width), jnp.float32)
    padded = jnp.concatenate([padding, joined, padding], axis=0)
    offset = jnp.clip(jnp.int32(0) - first_key + count, 0, key_span + count)
    summed = lax.psum_scatter(
        lax.dynamic_slice_in_dim(padded, offset, count, 0), "ctx", scatter_dimension=0, tiled=True
    )
    return (summed[:, :width], summed[:, width:])


def general_body(
    tokens,
    w_qkv,
    b_query,
    b_value,
    w_out,
    b_out,
    ln1_gain,
    ln1_bias,
    w_up,
    b_up,
    w_down,
    b_down,
    ln2_gain,
    ln2_bias,
    segment_ids,
    pad_mask,
    cotangent,
):
    weight_shards = (
        w_qkv,
        b_query,
        b_value,
        w_out,
        b_out,
        ln1_gain,
        ln1_bias,
        w_up,
        b_up,
        w_down,
        b_down,
        ln2_gain,
        ln2_bias,
    )
    gathered = (
        lax.all_gather(weight_shards[0], ("dp", "ctx"), axis=0, tiled=True),
        lax.all_gather(weight_shards[1], ("dp", "ctx"), axis=0, tiled=True),
        lax.all_gather(weight_shards[2], ("dp", "ctx"), axis=0, tiled=True),
        lax.all_gather(weight_shards[3], ("dp", "ctx"), axis=0, tiled=True),
        lax.all_gather(weight_shards[4], ("dp", "ctx"), axis=0, tiled=True),
        lax.all_gather(weight_shards[5], ("dp", "ctx"), axis=0, tiled=True),
        lax.all_gather(weight_shards[6], ("dp", "ctx"), axis=0, tiled=True),
        lax.all_gather(weight_shards[7], ("dp", "ctx"), axis=0, tiled=True),
        lax.all_gather(weight_shards[8], ("dp", "ctx"), axis=0, tiled=True),
        lax.all_gather(weight_shards[9], ("dp", "ctx"), axis=0, tiled=True),
        lax.all_gather(weight_shards[10], ("dp", "ctx"), axis=0, tiled=True),
        lax.all_gather(weight_shards[11], ("dp", "ctx"), axis=0, tiled=True),
        lax.all_gather(weight_shards[12], ("dp", "ctx"), axis=0, tiled=True),
    )
    (
        full_qkv,
        full_bquery,
        full_bvalue,
        full_out,
        full_bout,
        full_gain_one,
        full_bias_one,
        full_up,
        full_bup,
        full_down,
        full_bdown,
        full_gain_two,
        full_bias_two,
    ) = gathered
    rows_here = tokens.shape[1]
    seq_length = rows_here * lax.axis_size("ctx")
    own_index = lax.axis_index("ctx")
    inputs = tokens[0]
    inputs_wide = inputs.astype(jnp.float32)
    model_width = inputs.shape[1]
    token_tags = 2 * (segment_ids[0] + 1) + pad_mask[0]
    query_place = own_index * rows_here + jnp.arange(rows_here, dtype=jnp.int32)
    mixed = matmul(inputs, full_qkv)
    queries = (mixed[:, :model_width] + full_bquery.astype(jnp.float32)).astype(jnp.bfloat16)
    keys = mixed[:, model_width : 2 * model_width].astype(jnp.bfloat16)
    values = (mixed[:, 2 * model_width :] + full_bvalue.astype(jnp.float32)).astype(jnp.bfloat16)
    (key_window, value_window, tag_window), first_key = window_keys(
        (keys, values, token_tags), rows_here, seq_length, own_index
    )
    key_place = first_key + jnp.arange(key_window.shape[0], dtype=jnp.int32)
    attended, totals = attend_forward(
        split_heads(queries),
        split_heads(key_window),
        split_heads(value_window),
        token_tags,
        query_place,
        tag_window,
        key_place,
    )
    attended_low = attended.astype(jnp.bfloat16)
    first = inputs_wide + matmul(attended_low, full_out) + full_bout.astype(jnp.float32)
    normed, first_pull = jax.vjp(
        layer_norm, first, full_gain_one.astype(jnp.float32), full_bias_one.astype(jnp.float32)
    )
    normed_low = normed.astype(jnp.bfloat16)
    hidden = matmul(normed_low, full_up) + full_bup.astype(jnp.float32)
    active, gelu_pull = jax.vjp(partial(jax.nn.gelu, approximate=False), hidden)
    active_low = active.astype(jnp.bfloat16)
    second = normed + matmul(active_low, full_down) + full_bdown.astype(jnp.float32)
    result, second_pull = jax.vjp(
        layer_norm, second, full_gain_two.astype(jnp.float32), full_bias_two.astype(jnp.float32)
    )
    gathered = (
        lax.all_gather(weight_shards[0], ("dp", "ctx"), axis=0, tiled=True),
        lax.all_gather(weight_shards[1], ("dp", "ctx"), axis=0, tiled=True),
        lax.all_gather(weight_shards[2], ("dp", "ctx"), axis=0, tiled=True),
        lax.all_gather(weight_shards[3], ("dp", "ctx"), axis=0, tiled=True),
        lax.all_gather(weight_shards[4], ("dp", "ctx"), axis=0, tiled=True),
        lax.all_gather(weight_shards[5], ("dp", "ctx"), axis=0, tiled=True),
        lax.all_gather(weight_shards[6], ("dp", "ctx"), axis=0, tiled=True),
        lax.all_gather(weight_shards[7], ("dp", "ctx"), axis=0, tiled=True),
        lax.all_gather(weight_shards[8], ("dp", "ctx"), axis=0, tiled=True),
        lax.all_gather(weight_shards[9], ("dp", "ctx"), axis=0, tiled=True),
        lax.all_gather(weight_shards[10], ("dp", "ctx"), axis=0, tiled=True),
        lax.all_gather(weight_shards[11], ("dp", "ctx"), axis=0, tiled=True),
        lax.all_gather(weight_shards[12], ("dp", "ctx"), axis=0, tiled=True),
    )
    back_qkv = gathered[0]
    back_out = gathered[3]
    back_up = gathered[7]
    back_down = gathered[9]
    grad_second, grad_gain_two, grad_bias_two = second_pull(cotangent[0].astype(jnp.float32))
    grad_outcome = grad_second.astype(jnp.bfloat16)
    grad_wdown = rows_product(active_low, grad_outcome)
    grad_bdown = jnp.sum(grad_outcome.astype(jnp.float32), axis=0)
    (grad_active,) = gelu_pull(cols_product(grad_outcome, back_down))
    grad_hidden = grad_active.astype(jnp.bfloat16)
    grad_wup = rows_product(normed_low, grad_hidden)
    grad_bup = jnp.sum(grad_hidden.astype(jnp.float32), axis=0)
    grad_normed = grad_second + cols_product(grad_hidden, back_up)
    grad_first, grad_gain_one, grad_bias_one = first_pull(grad_normed)
    grad_branch = grad_first.astype(jnp.bfloat16)
    grad_wout = rows_product(attended_low, grad_branch)
    grad_bout = jnp.sum(grad_branch.astype(jnp.float32), axis=0)
    grad_attended = cols_product(grad_branch, back_out).astype(jnp.bfloat16)
    deltas = jnp.sum(
        (grad_attended.astype(jnp.float32) * attended).reshape(rows_here, HEADS, HEAD), axis=2
    ).T
    (key_again, value_again, tag_again), first_again = window_keys_again(
        (keys, values, token_tags), rows_here, seq_length, own_index
    )
    place_again = first_again + jnp.arange(key_again.shape[0], dtype=jnp.int32)
    grad_queries, key_grad, value_grad = attend_backward(
        split_heads(queries),
        split_heads(key_again),
        split_heads(value_again),
        split_heads(grad_attended),
        deltas,
        totals,
        token_tags,
        query_place,
        tag_again,
        place_again,
    )
    key_total, value_total = return_key_grads(key_grad, value_grad, rows_here, first_again)
    grad_query_low = grad_queries.astype(jnp.bfloat16)
    grad_value_low = value_total.astype(jnp.bfloat16)
    grad_mixed = jnp.concatenate(
        [grad_query_low, key_total.astype(jnp.bfloat16), grad_value_low], axis=1
    )
    grad_wqkv = rows_product(inputs, grad_mixed)
    grad_bquery = jnp.sum(grad_query_low.astype(jnp.float32), axis=0)
    grad_bvalue = jnp.sum(grad_value_low.astype(jnp.float32), axis=0)
    grad_inputs = grad_first + cols_product(grad_mixed, back_qkv)
    summed = (
        lax.psum_scatter(grad_wqkv, ("dp", "ctx"), scatter_dimension=0, tiled=True),
        lax.psum_scatter(grad_bquery, ("dp", "ctx"), scatter_dimension=0, tiled=True),
        lax.psum_scatter(grad_bvalue, ("dp", "ctx"), scatter_dimension=0, tiled=True),
        lax.psum_scatter(grad_wout, ("dp", "ctx"), scatter_dimension=0, tiled=True),
        lax.psum_scatter(grad_bout, ("dp", "ctx"), scatter_dimension=0, tiled=True),
        lax.psum_scatter(grad_gain_one, ("dp", "ctx"), scatter_dimension=0, tiled=True),
        lax.psum_scatter(grad_bias_one, ("dp", "ctx"), scatter_dimension=0, tiled=True),
        lax.psum_scatter(grad_wup, ("dp", "ctx"), scatter_dimension=0, tiled=True),
        lax.psum_scatter(grad_bup, ("dp", "ctx"), scatter_dimension=0, tiled=True),
        lax.psum_scatter(grad_wdown, ("dp", "ctx"), scatter_dimension=0, tiled=True),
        lax.psum_scatter(grad_bdown, ("dp", "ctx"), scatter_dimension=0, tiled=True),
        lax.psum_scatter(grad_gain_two, ("dp", "ctx"), scatter_dimension=0, tiled=True),
        lax.psum_scatter(grad_bias_two, ("dp", "ctx"), scatter_dimension=0, tiled=True),
    )
    return (
        result.astype(jnp.bfloat16)[None],
        grad_inputs.astype(jnp.bfloat16)[None],
        summed[0],
        summed[1],
        summed[2],
        summed[3],
        summed[4],
        summed[5],
        summed[6],
        summed[7],
        summed[8],
        summed[9],
        summed[10],
        summed[11],
        summed[12],
    )


def swap(member, axes, code):
    count = 1
    for axis in axes:
        count *= lax.axis_size(axis)
    return lax.ppermute(member, axes, [(place, place ^ code) for place in range(count)])


GROUP = ("y", "core", "x")
CTX = ("z", "x")
DP = ("y", "core")
EVERY = ("y", "core", "z", "x")


def group_gather(block):
    plane = [block] + [swap(block, ("y", "x"), code) for code in range(1, 4)]
    return plane + [swap(member, ("core",), 1) for member in plane]


def group_scatter(parts):
    near = [
        parts[code] + swap(parts[code + 4].astype(jnp.bfloat16), ("core",), 1).astype(jnp.float32)
        for code in range(4)
    ]
    total = near[0]
    for code in range(1, 4):
        total = total + swap(near[code].astype(jnp.bfloat16), ("y", "x"), code).astype(jnp.float32)
    return total


def exchange_sum(parts, axes):
    moved = lax.all_to_all(parts.astype(jnp.bfloat16), axes, 0, 0, tiled=True)
    count = 1
    for axis in axes:
        count *= lax.axis_size(axis)
    moved = moved.reshape((count, moved.shape[0] // count) + moved.shape[1:])
    return jnp.sum(moved.astype(jnp.float32), axis=0)


def heads_body(
    tokens,
    w_qkv,
    b_query,
    b_value,
    w_out,
    b_out,
    ln1_gain,
    ln1_bias,
    w_up,
    b_up,
    w_down,
    b_down,
    ln2_gain,
    ln2_bias,
    segment_ids,
    pad_mask,
    cotangent,
):
    bf16, f32 = jnp.bfloat16, jnp.float32
    inputs = tokens[0]
    rows, width = inputs.shape
    n_ctx = lax.axis_size(CTX)
    n_z = lax.axis_size("z")
    length = rows * n_ctx
    heads_here = HEADS // n_ctx
    cols = heads_here * HEAD
    shard = w_qkv.shape[0]
    units = w_down.shape[0]
    ff = w_up.shape[1]
    own_ctx = lax.axis_index(CTX)
    own_dp = lax.axis_index(DP)

    tags_here = (2 * (segment_ids[0] + 1) + pad_mask[0]).astype(bf16)
    packed = jnp.concatenate(
        [b_query, b_value, b_out, ln1_gain, ln1_bias, b_down, ln2_gain, ln2_bias, b_up, tags_here]
    )
    small = lax.all_gather(packed[None], EVERY, axis=0, tiled=True)
    vectors = [small[:, i * shard : (i + 1) * shard].reshape(width).astype(f32) for i in range(8)]
    bquery, bvalue, bout, gain_one, bias_one, bdown, gain_two, bias_two = vectors
    n_dp = lax.axis_size(DP)
    up_parts = small[:, 8 * shard : 8 * shard + units].reshape(n_dp, n_z, 2, units)
    bup = lax.dynamic_slice(
        up_parts, (own_dp, 0, lax.axis_index("x"), 0), (1, n_z, 1, units)
    ).reshape(n_z * units).astype(f32)
    tags = lax.dynamic_slice(
        small[:, 8 * shard + units :].reshape(n_dp, length), (own_dp, 0), (1, length)
    )[0].astype(jnp.int32)

    qkv = w_qkv.reshape(shard, 3, n_ctx, cols).transpose(2, 0, 1, 3).reshape(n_ctx * shard, 3 * cols)
    qkv = lax.all_to_all(qkv, CTX, 0, 0, tiled=True)
    qkv = lax.all_gather(qkv, DP, axis=0, tiled=True)
    whole = lax.all_gather(inputs, CTX, axis=0, tiled=True)
    full_out = lax.all_gather(w_out, EVERY, axis=0, tiled=True)

    up = w_up.reshape(shard, 2, 2, n_z, 2, units).transpose(1, 2, 4, 0, 3, 5)
    up = lax.all_to_all(up.reshape(8 * shard, n_z * units), GROUP, 0, 0, tiled=True)
    up = lax.all_gather(up, "z", axis=0, tiled=True)
    up = up.reshape(n_z, 2, 2, 2, shard, n_z * units).transpose(1, 2, 0, 3, 4, 5)
    up = up.reshape(width, n_z * units)
    down = lax.all_gather(w_down, "z", axis=0, tiled=True)

    mixed = matmul(whole, qkv)
    query_bias = lax.dynamic_slice(bquery, (own_ctx * cols,), (cols,))
    value_bias = lax.dynamic_slice(bvalue, (own_ctx * cols,), (cols,))
    queries = (mixed[:, :cols] + query_bias).astype(bf16).reshape(length, heads_here, HEAD)
    keys = mixed[:, cols : 2 * cols].astype(bf16).reshape(length, heads_here, HEAD)
    values = (mixed[:, 2 * cols :] + value_bias).astype(bf16).reshape(length, heads_here, HEAD)
    place = jnp.arange(length, dtype=jnp.int32)
    scores = masked_scores(queries, keys, tags, place, tags, place)
    totals = jax.nn.logsumexp(scores, axis=2)
    probs = jnp.exp(scores - totals[:, :, None])
    probs_low = probs.astype(bf16)
    attended = jnp.einsum("hqk,khd->qhd", probs_low, values, preferred_element_type=f32)
    moved = lax.all_to_all(attended.reshape(length, cols).astype(bf16), CTX, 0, 0, tiled=True)
    attended_low = moved.reshape(n_ctx, rows, cols).transpose(1, 0, 2).reshape(rows, width)

    first = inputs.astype(f32) + matmul(attended_low, full_out) + bout
    normed, first_pull = jax.vjp(layer_norm, first, gain_one, bias_one)
    normed_all = jnp.concatenate(group_gather(normed.astype(bf16)), axis=0)
    hidden = matmul(normed_all, up) + bup
    active, gelu_pull = jax.vjp(partial(jax.nn.gelu, approximate=False), hidden)
    active_low = active.astype(bf16)
    outcome = matmul(active_low, down)
    second = normed + group_scatter(jnp.split(outcome, 8)) + bdown
    result, second_pull = jax.vjp(layer_norm, second, gain_two, bias_two)

    grad_second, grad_gain_two, grad_bias_two = second_pull(cotangent[0].astype(f32))
    grad_z = grad_second.astype(bf16)
    grad_bdown = jnp.sum(grad_z.astype(f32), axis=0)
    grad_z_all = jnp.concatenate(group_gather(grad_z), axis=0)
    (grad_active,) = gelu_pull(cols_product(grad_z_all, down))
    grad_hidden = grad_active.astype(bf16)
    back = cols_product(grad_hidden, up)
    grad_normed = grad_second + group_scatter(jnp.split(back, 8))
    grad_wdown = rows_product(active_low, grad_z_all)
    grad_bup = jnp.sum(grad_hidden.astype(f32), axis=0)
    down_parts = jnp.concatenate(
        [grad_wdown, jnp.broadcast_to(grad_bup[:, None], (n_z * units, 128))], axis=1
    )
    down_sum = exchange_sum(down_parts, ("z",))
    grad_wdown_out, grad_bup_out = down_sum[:, :width], down_sum[:, width]
    grad_wup = rows_product(normed_all, grad_hidden)
    up_sum = exchange_sum(
        grad_wup.reshape(2, 2, n_z, 2, shard, n_z * units)
        .transpose(2, 0, 1, 3, 4, 5)
        .reshape(n_z, 8 * shard, n_z * units)
        .reshape(n_z * 8 * shard, n_z * units),
        ("z",),
    )
    up_sum = lax.all_to_all(up_sum, GROUP, 0, 0, tiled=True)
    grad_wup_out = (
        up_sum.reshape(2, 2, 2, shard, n_z, units).transpose(3, 0, 1, 4, 2, 5).reshape(shard, ff)
    )

    grad_first, grad_gain_one, grad_bias_one = first_pull(grad_normed)
    grad_branch = grad_first.astype(bf16)
    grad_bout = jnp.sum(grad_branch.astype(f32), axis=0)
    grad_attended = cols_product(grad_branch, full_out).astype(bf16)
    moved = grad_attended.reshape(rows, n_ctx, cols).transpose(1, 0, 2).reshape(length, cols)
    moved = lax.all_to_all(moved, CTX, 0, 0, tiled=True)
    grad_heads = moved.reshape(length, heads_here, HEAD)

    grad_wout = rows_product(attended_low, grad_branch)
    extra = jnp.stack(
        [grad_bout, grad_gain_one, grad_bias_one, grad_bdown, grad_gain_two, grad_bias_two], axis=1
    )
    extra = jnp.pad(extra, ((0, 0), (0, 122)))
    out_parts = jnp.concatenate([grad_wout, extra], axis=1)
    out_sum = exchange_sum(out_parts, EVERY)
    grad_wout_out = out_sum[:, :width]
    thin = out_sum[:, width:]

    deltas = jnp.sum(
        grad_heads.astype(f32) * attended.reshape(length, heads_here, HEAD), axis=2
    ).T
    dprobs = jnp.einsum("qhd,khd->hqk", grad_heads, values, preferred_element_type=f32)
    dscores = (probs * (dprobs - deltas[:, :, None])).astype(bf16)
    grad_queries = jnp.einsum("hqk,khd->qhd", dscores, keys, preferred_element_type=f32) * 0.125
    grad_keys = jnp.einsum("hqk,qhd->khd", dscores, queries, preferred_element_type=f32) * 0.125
    grad_values = jnp.einsum("hqk,qhd->khd", probs_low, grad_heads, preferred_element_type=f32)
    grad_mixed = jnp.concatenate(
        [v.astype(bf16).reshape(length, cols) for v in (grad_queries, grad_keys, grad_values)],
        axis=1,
    )
    grad_bias = jnp.sum(grad_mixed.astype(f32), axis=0)
    grad_qkv = rows_product(whole, grad_mixed)
    grad_qkv = jnp.concatenate(
        [
            grad_qkv.reshape(n_dp, n_ctx * shard, 3 * cols),
            jnp.broadcast_to(grad_bias, (n_dp, 16, 3 * cols)),
        ],
        axis=1,
    ).reshape(-1, 3 * cols)
    qkv_sum = exchange_sum(grad_qkv, DP)
    qkv_rows = qkv_sum[: n_ctx * shard].reshape(n_ctx, shard, 3 * cols)
    qkv_bias = jnp.broadcast_to(qkv_sum[n_ctx * shard :][:8], (n_ctx, 8, 3 * cols))
    qkv_sum = jnp.concatenate([qkv_rows, qkv_bias], axis=1).reshape(-1, 3 * cols)
    qkv_sum = lax.all_to_all(qkv_sum, CTX, 0, 0, tiled=True).reshape(n_ctx, shard + 8, 3, cols)
    grad_wqkv_out = qkv_sum[:, :shard].transpose(1, 2, 0, 3).reshape(shard, 3 * width)
    bias_sum = qkv_sum[:, shard].transpose(1, 0, 2).reshape(3, width)
    first_own = (own_dp * n_ctx + own_ctx) * shard
    bias_own = lax.dynamic_slice(bias_sum, (0, first_own), (3, shard))

    input_parts = cols_product(grad_mixed, qkv)
    grad_inputs = grad_first + exchange_sum(input_parts, CTX)
    return (
        result.astype(bf16)[None],
        grad_inputs.astype(bf16)[None],
        grad_wqkv_out,
        bias_own[0],
        bias_own[2],
        grad_wout_out,
        thin[:, 0],
        thin[:, 1],
        thin[:, 2],
        grad_wup_out,
        grad_bup_out,
        grad_wdown_out,
        thin[:, 3],
        thin[:, 4],
        thin[:, 5],
    )


def call_heads(mesh, *arrays):
    grid = Mesh(mesh.devices.reshape(2, 2, 4, 2), EVERY)
    rows, lone, block = P(EVERY, None), P(EVERY), P(DP, CTX, None)
    in_specs = (
        block, rows, lone, lone, rows, lone, lone, lone, rows, lone, rows, lone, lone, lone,
        P(DP, CTX), P(DP, CTX), block,
    )
    out_specs = (
        block, block, rows, lone, lone, rows, lone, lone, lone, rows, lone, rows, lone, lone, lone,
    )
    return jax.shard_map(
        heads_body, mesh=grid, in_specs=in_specs, out_specs=out_specs, check_vma=False
    )(*arrays)


def call(mesh, *arrays):
    if mesh.shape["dp"] == 4 and mesh.shape["ctx"] == 8 and arrays[0].shape[1] <= 1024:
        return call_heads(mesh, *arrays)
    return general_call(mesh)(*arrays)


def general_call(mesh):
    in_specs = (
        P("dp", "ctx", None),
        P(("dp", "ctx"), None),
        P(("dp", "ctx")),
        P(("dp", "ctx")),
        P(("dp", "ctx"), None),
        P(("dp", "ctx")),
        P(("dp", "ctx")),
        P(("dp", "ctx")),
        P(("dp", "ctx"), None),
        P(("dp", "ctx")),
        P(("dp", "ctx"), None),
        P(("dp", "ctx")),
        P(("dp", "ctx")),
        P(("dp", "ctx")),
        P("dp", "ctx"),
        P("dp", "ctx"),
        P("dp", "ctx", None),
    )
    out_specs = (
        P("dp", "ctx", None),
        P("dp", "ctx", None),
        P(("dp", "ctx"), None),
        P(("dp", "ctx")),
        P(("dp", "ctx")),
        P(("dp", "ctx"), None),
        P(("dp", "ctx")),
        P(("dp", "ctx")),
        P(("dp", "ctx")),
        P(("dp", "ctx"), None),
        P(("dp", "ctx")),
        P(("dp", "ctx"), None),
        P(("dp", "ctx")),
        P(("dp", "ctx")),
        P(("dp", "ctx")),
    )
    return jax.shard_map(general_body, mesh=mesh, in_specs=in_specs, out_specs=out_specs, check_vma=False)


def solution(mesh):
    return partial(call, mesh)
```

```python
from functools import partial

import jax
import jax.numpy as jnp
from jax import lax
from jax.sharding import Mesh
from jax.sharding import PartitionSpec as P

HEADS = 16
HEAD = 64
WINDOW = 1024


MASKED = -1e30
EPSILON = 1e-05


def layer_norm(values, scales, offsets):
    average = jnp.mean(values, axis=-1, keepdims=True)
    centred = values - average
    variance = jnp.mean(centred * centred, axis=-1, keepdims=True)
    return centred * lax.rsqrt(variance + EPSILON) * scales + offsets


def matmul(left, right):
    return jnp.dot(left, right, preferred_element_type=jnp.float32)


def rows_product(left, right):
    return lax.dot_general(
        left, right, (((0,), (0,)), ((), ())), preferred_element_type=jnp.float32
    )


def cols_product(left, right):
    return lax.dot_general(
        left, right, (((1,), (1,)), ((), ())), preferred_element_type=jnp.float32
    )


def split_heads(matrix):
    return matrix.reshape(matrix.shape[0], HEADS, HEAD)


def allowed_keys(query_tags, query_place, key_tags, key_place):
    same_doc = query_tags[:, None] // 2 == key_tags[None, :] // 2
    distance = jnp.abs(query_place[:, None] - key_place[None, :])
    usable = (key_tags[None, :] % 2 == 1) | (distance == 0)
    return same_doc & (distance <= WINDOW // 2) & usable


def masked_scores(query_block, key_heads, query_tags, query_place, key_tags, key_place):
    raw = (
        jnp.einsum("qhd,khd->hqk", query_block, key_heads, preferred_element_type=jnp.float32)
        * 0.125
    )
    return jnp.where(allowed_keys(query_tags, query_place, key_tags, key_place)[None], raw, MASKED)


def attend_forward(
    query_heads, key_heads, value_heads, query_tags, query_place, key_tags, key_place
):
    row_count = query_heads.shape[0]
    block_rows = min(row_count, 512)

    def one_block(block_index):
        scores = masked_scores(query_heads, key_heads, query_tags, query_place, key_tags, key_place)
        totals = jax.nn.logsumexp(scores, axis=2)
        probs = jnp.exp(scores - totals[:, :, None]).astype(jnp.bfloat16)
        output = jnp.einsum("hqk,khd->qhd", probs, value_heads, preferred_element_type=jnp.float32)
        return (output, totals)

    outputs, totals = lax.map(one_block, jnp.arange(row_count // block_rows, dtype=jnp.int32))
    return (outputs.reshape(row_count, HEADS * HEAD), totals)


def attend_backward(
    query_heads,
    key_heads,
    value_heads,
    grad_heads,
    deltas,
    totals,
    query_tags,
    query_place,
    key_tags,
    key_place,
):
    row_count = query_heads.shape[0]
    block_rows = min(row_count, 512)

    def one_block(running, block_index):
        key_grad, value_grad = running
        scores = masked_scores(query_heads, key_heads, query_tags, query_place, key_tags, key_place)
        probs = jnp.exp(scores - totals[block_index][:, :, None])
        dprobs = jnp.einsum(
            "qhd,khd->hqk", grad_heads, value_heads, preferred_element_type=jnp.float32
        )
        dscores = (probs * (dprobs - deltas[:, :, None])).astype(jnp.bfloat16)
        query_grad = (
            jnp.einsum("hqk,khd->qhd", dscores, key_heads, preferred_element_type=jnp.float32)
            * 0.125
        )
        key_grad = (
            key_grad
            + jnp.einsum("hqk,qhd->khd", dscores, query_heads, preferred_element_type=jnp.float32)
            * 0.125
        )
        value_grad = value_grad + jnp.einsum(
            "hqk,qhd->khd",
            probs.astype(jnp.bfloat16),
            grad_heads,
            preferred_element_type=jnp.float32,
        )
        return ((key_grad, value_grad), query_grad)

    zeros = jnp.zeros(key_heads.shape, jnp.float32)
    (key_grad, value_grad), query_grads = lax.scan(
        one_block, (zeros, zeros), jnp.arange(row_count // block_rows, dtype=jnp.int32)
    )
    key_count = key_heads.shape[0]
    return (
        query_grads.reshape(row_count, HEADS * HEAD),
        key_grad.reshape(key_count, HEADS * HEAD),
        value_grad.reshape(key_count, HEADS * HEAD),
    )


def clip_window(whole, rows_here, seq_length, own_index):
    neighbours = (WINDOW // 2 + rows_here - 1) // rows_here
    key_span = min((2 * neighbours + 1) * rows_here, seq_length)
    first_key = jnp.clip((own_index - neighbours) * rows_here, 0, seq_length - key_span)
    window = tuple((lax.dynamic_slice_in_dim(member, first_key, key_span, 0) for member in whole))
    return (window, first_key)


def window_keys(items, rows_here, seq_length, own_index):
    whole = (
        lax.all_gather(items[0], "ctx", axis=0, tiled=True),
        lax.all_gather(items[1], "ctx", axis=0, tiled=True),
        lax.all_gather(items[2], "ctx", axis=0, tiled=True),
    )
    return clip_window(whole, rows_here, seq_length, own_index)


def window_keys_again(items, rows_here, seq_length, own_index):
    whole = (
        lax.all_gather(items[0], "ctx", axis=0, tiled=True),
        lax.all_gather(items[1], "ctx", axis=0, tiled=True),
        lax.all_gather(items[2], "ctx", axis=0, tiled=True),
    )
    return clip_window(whole, rows_here, seq_length, own_index)


def return_key_grads(key_grad, value_grad, rows_here, first_key):
    width = key_grad.shape[1]
    joined = jnp.concatenate([key_grad, value_grad], axis=1)
    key_span = joined.shape[0]
    count = rows_here * lax.axis_size("ctx")
    padding = jnp.zeros((count, 2 * width), jnp.float32)
    padded = jnp.concatenate([padding, joined, padding], axis=0)
    offset = jnp.clip(jnp.int32(0) - first_key + count, 0, key_span + count)
    summed = lax.psum_scatter(
        lax.dynamic_slice_in_dim(padded, offset, count, 0), "ctx", scatter_dimension=0, tiled=True
    )
    return (summed[:, :width], summed[:, width:])


def general_body(
    tokens,
    w_qkv,
    b_query,
    b_value,
    w_out,
    b_out,
    ln1_gain,
    ln1_bias,
    w_up,
    b_up,
    w_down,
    b_down,
    ln2_gain,
    ln2_bias,
    segment_ids,
    pad_mask,
    cotangent,
):
    weight_shards = (
        w_qkv,
        b_query,
        b_value,
        w_out,
        b_out,
        ln1_gain,
        ln1_bias,
        w_up,
        b_up,
        w_down,
        b_down,
        ln2_gain,
        ln2_bias,
    )
    gathered = (
        lax.all_gather(weight_shards[0], ("dp", "ctx"), axis=0, tiled=True),
        lax.all_gather(weight_shards[1], ("dp", "ctx"), axis=0, tiled=True),
        lax.all_gather(weight_shards[2], ("dp", "ctx"), axis=0, tiled=True),
        lax.all_gather(weight_shards[3], ("dp", "ctx"), axis=0, tiled=True),
        lax.all_gather(weight_shards[4], ("dp", "ctx"), axis=0, tiled=True),
        lax.all_gather(weight_shards[5], ("dp", "ctx"), axis=0, tiled=True),
        lax.all_gather(weight_shards[6], ("dp", "ctx"), axis=0, tiled=True),
        lax.all_gather(weight_shards[7], ("dp", "ctx"), axis=0, tiled=True),
        lax.all_gather(weight_shards[8], ("dp", "ctx"), axis=0, tiled=True),
        lax.all_gather(weight_shards[9], ("dp", "ctx"), axis=0, tiled=True),
        lax.all_gather(weight_shards[10], ("dp", "ctx"), axis=0, tiled=True),
        lax.all_gather(weight_shards[11], ("dp", "ctx"), axis=0, tiled=True),
        lax.all_gather(weight_shards[12], ("dp", "ctx"), axis=0, tiled=True),
    )
    (
        full_qkv,
        full_bquery,
        full_bvalue,
        full_out,
        full_bout,
        full_gain_one,
        full_bias_one,
        full_up,
        full_bup,
        full_down,
        full_bdown,
        full_gain_two,
        full_bias_two,
    ) = gathered
    rows_here = tokens.shape[1]
    seq_length = rows_here * lax.axis_size("ctx")
    own_index = lax.axis_index("ctx")
    inputs = tokens[0]
    inputs_wide = inputs.astype(jnp.float32)
    model_width = inputs.shape[1]
    token_tags = 2 * (segment_ids[0] + 1) + pad_mask[0]
    query_place = own_index * rows_here + jnp.arange(rows_here, dtype=jnp.int32)
    mixed = matmul(inputs, full_qkv)
    queries = (mixed[:, :model_width] + full_bquery.astype(jnp.float32)).astype(jnp.bfloat16)
    keys = mixed[:, model_width : 2 * model_width].astype(jnp.bfloat16)
    values = (mixed[:, 2 * model_width :] + full_bvalue.astype(jnp.float32)).astype(jnp.bfloat16)
    (key_window, value_window, tag_window), first_key = window_keys(
        (keys, values, token_tags), rows_here, seq_length, own_index
    )
    key_place = first_key + jnp.arange(key_window.shape[0], dtype=jnp.int32)
    attended, totals = attend_forward(
        split_heads(queries),
        split_heads(key_window),
        split_heads(value_window),
        token_tags,
        query_place,
        tag_window,
        key_place,
    )
    attended_low = attended.astype(jnp.bfloat16)
    first = inputs_wide + matmul(attended_low, full_out) + full_bout.astype(jnp.float32)
    normed, first_pull = jax.vjp(
        layer_norm, first, full_gain_one.astype(jnp.float32), full_bias_one.astype(jnp.float32)
    )
    normed_low = normed.astype(jnp.bfloat16)
    hidden = matmul(normed_low, full_up) + full_bup.astype(jnp.float32)
    active, gelu_pull = jax.vjp(partial(jax.nn.gelu, approximate=False), hidden)
    active_low = active.astype(jnp.bfloat16)
    second = normed + matmul(active_low, full_down) + full_bdown.astype(jnp.float32)
    result, second_pull = jax.vjp(
        layer_norm, second, full_gain_two.astype(jnp.float32), full_bias_two.astype(jnp.float32)
    )
    gathered = (
        lax.all_gather(weight_shards[0], ("dp", "ctx"), axis=0, tiled=True),
        lax.all_gather(weight_shards[1], ("dp", "ctx"), axis=0, tiled=True),
        lax.all_gather(weight_shards[2], ("dp", "ctx"), axis=0, tiled=True),
        lax.all_gather(weight_shards[3], ("dp", "ctx"), axis=0, tiled=True),
        lax.all_gather(weight_shards[4], ("dp", "ctx"), axis=0, tiled=True),
        lax.all_gather(weight_shards[5], ("dp", "ctx"), axis=0, tiled=True),
        lax.all_gather(weight_shards[6], ("dp", "ctx"), axis=0, tiled=True),
        lax.all_gather(weight_shards[7], ("dp", "ctx"), axis=0, tiled=True),
        lax.all_gather(weight_shards[8], ("dp", "ctx"), axis=0, tiled=True),
        lax.all_gather(weight_shards[9], ("dp", "ctx"), axis=0, tiled=True),
        lax.all_gather(weight_shards[10], ("dp", "ctx"), axis=0, tiled=True),
        lax.all_gather(weight_shards[11], ("dp", "ctx"), axis=0, tiled=True),
        lax.all_gather(weight_shards[12], ("dp", "ctx"), axis=0, tiled=True),
    )
    back_qkv = gathered[0]
    back_out = gathered[3]
    back_up = gathered[7]
    back_down = gathered[9]
    grad_second, grad_gain_two, grad_bias_two = second_pull(cotangent[0].astype(jnp.float32))
    grad_outcome = grad_second.astype(jnp.bfloat16)
    grad_wdown = rows_product(active_low, grad_outcome)
    grad_bdown = jnp.sum(grad_outcome.astype(jnp.float32), axis=0)
    (grad_active,) = gelu_pull(cols_product(grad_outcome, back_down))
    grad_hidden = grad_active.astype(jnp.bfloat16)
    grad_wup = rows_product(normed_low, grad_hidden)
    grad_bup = jnp.sum(grad_hidden.astype(jnp.float32), axis=0)
    grad_normed = grad_second + cols_product(grad_hidden, back_up)
    grad_first, grad_gain_one, grad_bias_one = first_pull(grad_normed)
    grad_branch = grad_first.astype(jnp.bfloat16)
    grad_wout = rows_product(attended_low, grad_branch)
    grad_bout = jnp.sum(grad_branch.astype(jnp.float32), axis=0)
    grad_attended = cols_product(grad_branch, back_out).astype(jnp.bfloat16)
    deltas = jnp.sum(
        (grad_attended.astype(jnp.float32) * attended).reshape(rows_here, HEADS, HEAD), axis=2
    ).T
    (key_again, value_again, tag_again), first_again = window_keys_again(
        (keys, values, token_tags), rows_here, seq_length, own_index
    )
    place_again = first_again + jnp.arange(key_again.shape[0], dtype=jnp.int32)
    grad_queries, key_grad, value_grad = attend_backward(
        split_heads(queries),
        split_heads(key_again),
        split_heads(value_again),
        split_heads(grad_attended),
        deltas,
        totals,
        token_tags,
        query_place,
        tag_again,
        place_again,
    )
    key_total, value_total = return_key_grads(key_grad, value_grad, rows_here, first_again)
    grad_query_low = grad_queries.astype(jnp.bfloat16)
    grad_value_low = value_total.astype(jnp.bfloat16)
    grad_mixed = jnp.concatenate(
        [grad_query_low, key_total.astype(jnp.bfloat16), grad_value_low], axis=1
    )
    grad_wqkv = rows_product(inputs, grad_mixed)
    grad_bquery = jnp.sum(grad_query_low.astype(jnp.float32), axis=0)
    grad_bvalue = jnp.sum(grad_value_low.astype(jnp.float32), axis=0)
    grad_inputs = grad_first + cols_product(grad_mixed, back_qkv)
    summed = (
        lax.psum_scatter(grad_wqkv, ("dp", "ctx"), scatter_dimension=0, tiled=True),
        lax.psum_scatter(grad_bquery, ("dp", "ctx"), scatter_dimension=0, tiled=True),
        lax.psum_scatter(grad_bvalue, ("dp", "ctx"), scatter_dimension=0, tiled=True),
        lax.psum_scatter(grad_wout, ("dp", "ctx"), scatter_dimension=0, tiled=True),
        lax.psum_scatter(grad_bout, ("dp", "ctx"), scatter_dimension=0, tiled=True),
        lax.psum_scatter(grad_gain_one, ("dp", "ctx"), scatter_dimension=0, tiled=True),
        lax.psum_scatter(grad_bias_one, ("dp", "ctx"), scatter_dimension=0, tiled=True),
        lax.psum_scatter(grad_wup, ("dp", "ctx"), scatter_dimension=0, tiled=True),
        lax.psum_scatter(grad_bup, ("dp", "ctx"), scatter_dimension=0, tiled=True),
        lax.psum_scatter(grad_wdown, ("dp", "ctx"), scatter_dimension=0, tiled=True),
        lax.psum_scatter(grad_bdown, ("dp", "ctx"), scatter_dimension=0, tiled=True),
        lax.psum_scatter(grad_gain_two, ("dp", "ctx"), scatter_dimension=0, tiled=True),
        lax.psum_scatter(grad_bias_two, ("dp", "ctx"), scatter_dimension=0, tiled=True),
    )
    return (
        result.astype(jnp.bfloat16)[None],
        grad_inputs.astype(jnp.bfloat16)[None],
        summed[0],
        summed[1],
        summed[2],
        summed[3],
        summed[4],
        summed[5],
        summed[6],
        summed[7],
        summed[8],
        summed[9],
        summed[10],
        summed[11],
        summed[12],
    )


def swap(member, axes, code):
    count = 1
    for axis in axes:
        count *= lax.axis_size(axis)
    return lax.ppermute(member, axes, [(place, place ^ code) for place in range(count)])


GROUP = ("y", "core", "x")
CTX = ("z", "x")
DP = ("y", "core")
EVERY = ("y", "core", "z", "x")


def group_gather(block):
    plane = [block] + [swap(block, ("y", "x"), code) for code in range(1, 4)]
    return plane + [swap(member, ("core",), 1) for member in plane]


def group_scatter(parts):
    near = [
        parts[code] + swap(parts[code + 4].astype(jnp.bfloat16), ("core",), 1).astype(jnp.float32)
        for code in range(4)
    ]
    total = near[0]
    for code in range(1, 4):
        total = total + swap(near[code].astype(jnp.bfloat16), ("y", "x"), code).astype(jnp.float32)
    return total


def sum_over_z(parts):
    total = parts[0]
    for code in range(1, 4):
        total = total + swap(parts[code].astype(jnp.bfloat16), ("z",), code).astype(jnp.float32)
    return total


def relative(blocks, own):
    return jnp.take(blocks, own ^ jnp.arange(blocks.shape[0]), axis=0)


def ctx_gather(block):
    line = [block] + [swap(block, ("z",), code) for code in range(1, 4)]
    return [piece for member in line for piece in (member, swap(member, ("x",), 1))]


def ctx_exchange(blocks):
    rows = blocks[0].shape[0]
    crossed = swap(jnp.concatenate(blocks[1::2], axis=0), ("x",), 1)
    crossed = jnp.split(crossed, 4)
    out = [blocks[0], crossed[0]]
    for code in range(1, 4):
        both = swap(jnp.concatenate([blocks[2 * code], crossed[code]], axis=0), ("z",), code)
        out += [both[:rows], both[rows:]]
    return out


def ctx_sum(parts):
    line = [None] * 4
    for code in (3, 2, 1, 0):
        crossed = swap(parts[2 * code + 1].astype(jnp.bfloat16), ("x",), 1)
        line[code] = parts[2 * code] + crossed.astype(jnp.float32)
    return sum_over_z(line)


def dp_gather(block):
    pair = jnp.stack([block, swap(block, ("y",), 1)])
    four = jnp.concatenate([pair, swap(pair, ("core",), 1)])
    place = lax.axis_index("core") * 2 + lax.axis_index("y")
    return relative(four, place)[jnp.array([0, 2, 1, 3])]


def dp_sum(parts):
    crossed = jnp.concatenate([parts[1], parts[3]], axis=0).astype(jnp.bfloat16)
    crossed = swap(crossed, ("core",), 1).astype(jnp.float32)
    rows = parts[0].shape[0]
    near, far = parts[0] + crossed[:rows], parts[2] + crossed[rows:]
    return near + swap(far.astype(jnp.bfloat16), ("y",), 1).astype(jnp.float32)


def gather_every(block):
    blocks = block[None]
    for axis, code in (("x", 1), ("z", 1), ("z", 2), ("core", 1), ("y", 1)):
        blocks = jnp.concatenate([blocks, swap(blocks, (axis,), code)], axis=0)
    place = lax.axis_index(EVERY)
    hot = (jnp.arange(32)[:, None] == (jnp.arange(32) ^ place)[None, :]).astype(block.dtype)
    return jnp.einsum("ij,j...->i...", hot, blocks, preferred_element_type=jnp.float32)


def gather_out(block, own_ctx):
    line = jnp.stack([block] + [swap(block, ("z",), code) for code in range(1, 4)])
    both = jnp.stack([line, swap(line, ("y",), 1)])
    plane = jnp.stack([both, swap(both, ("x",), 1)])
    every = jnp.stack([plane, swap(plane, ("core",), 1)])
    rows, width = block.shape
    every = every.reshape(32, rows, width)
    group = (own_ctx ^ jnp.arange(8))[:, None] * 4 + jnp.arange(4)[None, :]
    place = group.reshape(32) ^ lax.axis_index(EVERY)
    y, core, z, x = place // 16, place // 8 % 2, place // 2 % 4, place % 2
    index = core * 16 + x * 8 + y * 4 + z
    return jnp.take(every, index, axis=0).reshape(8, 4 * rows, width)


def own_ctx_rows(block, own_ctx):
    return (block // 4 ^ own_ctx) * 4 + block % 4


def heads_body(
    tokens,
    w_qkv,
    b_query,
    b_value,
    w_out,
    b_out,
    ln1_gain,
    ln1_bias,
    w_up,
    b_up,
    w_down,
    b_down,
    ln2_gain,
    ln2_bias,
    segment_ids,
    pad_mask,
    cotangent,
):
    bf16, f32 = jnp.bfloat16, jnp.float32
    inputs = tokens[0]
    rows, width = inputs.shape
    n_ctx = lax.axis_size(CTX)
    n_z = lax.axis_size("z")
    length = rows * n_ctx
    heads_here = HEADS // n_ctx
    cols = heads_here * HEAD
    shard = w_qkv.shape[0]
    units = w_down.shape[0]
    ff = w_up.shape[1]
    own_ctx = lax.axis_index(CTX)
    own_dp = lax.axis_index(DP)

    tags_here = (2 * (segment_ids[0] + 1) + pad_mask[0]).astype(bf16)
    packed = jnp.concatenate(
        [b_query, b_value, b_out, ln1_gain, ln1_bias, b_down, ln2_gain, ln2_bias, b_up, tags_here]
    )
    small = gather_every(packed)
    vectors = [small[:, i * shard : (i + 1) * shard].reshape(width) for i in range(8)]
    bquery, bvalue, bout, gain_one, bias_one, bdown, gain_two, bias_two = vectors
    n_dp = lax.axis_size(DP)
    up_parts = small[:, 8 * shard : 8 * shard + units].reshape(n_dp, n_z, 2, units)
    bup = lax.dynamic_slice(
        up_parts, (own_dp, 0, lax.axis_index("x"), 0), (1, n_z, 1, units)
    ).reshape(n_z * units)
    tags = lax.dynamic_slice(
        small[:, 8 * shard + units :].reshape(n_dp, length), (own_dp, 0), (1, length)
    )[0].astype(jnp.int32)
    tags = relative(tags.reshape(n_ctx, rows), own_ctx).reshape(length)

    qkv = w_qkv.reshape(shard, 3, n_ctx, cols).transpose(2, 0, 1, 3).reshape(n_ctx * shard, 3 * cols)
    qkv = lax.all_to_all(qkv, CTX, 0, 0, tiled=True)
    qkv = dp_gather(qkv).reshape(width, 3 * cols)
    whole = jnp.concatenate(ctx_gather(inputs), axis=0)
    full_out = gather_out(w_out, own_ctx)

    up = w_up.reshape(shard, 2, 2, n_z, 2, units).transpose(1, 2, 4, 0, 3, 5)
    up = lax.all_to_all(up.reshape(8 * shard, n_z * units), GROUP, 0, 0, tiled=True)
    up = lax.all_gather(up, "z", axis=0, tiled=True)
    up = up.reshape(n_z, 2, 2, 2, shard, n_z * units).transpose(1, 2, 0, 3, 4, 5)
    up = up.reshape(width, n_z * units)
    down = lax.all_gather(w_down, "z", axis=0, tiled=True)

    mixed = matmul(whole, qkv)
    query_bias = lax.dynamic_slice(bquery, (own_ctx * cols,), (cols,))
    value_bias = lax.dynamic_slice(bvalue, (own_ctx * cols,), (cols,))
    queries = (mixed[:, :cols] + query_bias).astype(bf16).reshape(length, heads_here, HEAD)
    keys = mixed[:, cols : 2 * cols].astype(bf16).reshape(length, heads_here, HEAD)
    values = (mixed[:, 2 * cols :] + value_bias).astype(bf16).reshape(length, heads_here, HEAD)
    order = own_ctx ^ jnp.arange(n_ctx, dtype=jnp.int32)
    place = (order[:, None] * rows + jnp.arange(rows, dtype=jnp.int32)[None, :]).reshape(length)
    scores = masked_scores(queries, keys, tags, place, tags, place)
    totals = jax.nn.logsumexp(scores, axis=2)
    probs = jnp.exp(scores - totals[:, :, None])
    probs_low = probs.astype(bf16)
    attended = jnp.einsum("hqk,khd->qhd", probs_low, values, preferred_element_type=f32)
    attended_blocks = ctx_exchange(jnp.split(attended.reshape(length, cols).astype(bf16), n_ctx))
    attended_low = jnp.concatenate(attended_blocks, axis=1)
    full_out = full_out.reshape(width, width)

    first = inputs.astype(f32) + matmul(attended_low, full_out) + bout
    normed, first_pull = jax.vjp(layer_norm, first, gain_one, bias_one)
    normed_all = jnp.concatenate(group_gather(normed.astype(bf16)), axis=0)
    hidden = matmul(normed_all, up) + bup
    active, gelu_pull = jax.vjp(partial(jax.nn.gelu, approximate=False), hidden)
    active_low = active.astype(bf16)
    outcome = matmul(active_low, down)
    second = normed + group_scatter(jnp.split(outcome, 8)) + bdown
    result, second_pull = jax.vjp(layer_norm, second, gain_two, bias_two)

    grad_second, grad_gain_two, grad_bias_two = second_pull(cotangent[0].astype(f32))
    grad_z = grad_second.astype(bf16)
    grad_bdown = jnp.sum(grad_z.astype(f32), axis=0)
    grad_z_all = jnp.concatenate(group_gather(grad_z), axis=0)
    (grad_active,) = gelu_pull(cols_product(grad_z_all, down))
    grad_hidden = grad_active.astype(bf16)
    back = cols_product(grad_hidden, up)
    grad_normed = grad_second + group_scatter(jnp.split(back, 8))
    grad_wdown = rows_product(active_low, grad_z_all)
    grad_bup = jnp.sum(grad_hidden.astype(f32), axis=0)
    down_parts = jnp.concatenate(
        [grad_wdown, jnp.broadcast_to(grad_bup[:, None], (n_z * units, 128))], axis=1
    ).reshape(n_z, units, width + 128)
    own_z = lax.axis_index("z")
    down_sum = sum_over_z(list(relative(down_parts.astype(bf16), own_z)))
    grad_wdown_out, grad_bup_out = down_sum[:, :width], down_sum[:, width]
    grad_wup = rows_product(normed_all, grad_hidden)
    up_parts = grad_wup.astype(bf16).reshape(2, 2, n_z, 2, shard, n_z * units)
    up_parts = up_parts.transpose(2, 0, 1, 3, 4, 5).reshape(n_z, 8 * shard, n_z * units)
    up_sum = sum_over_z(list(relative(up_parts, own_z))).astype(bf16)
    up_sum = lax.all_to_all(up_sum, GROUP, 0, 0, tiled=True)
    grad_wup_out = (
        up_sum.reshape(2, 2, 2, shard, n_z, units)
        .astype(f32)
        .transpose(3, 0, 1, 4, 2, 5)
        .reshape(shard, ff)
    )

    grad_first, grad_gain_one, grad_bias_one = first_pull(grad_normed)
    grad_branch = grad_first.astype(bf16)
    grad_bout = jnp.sum(grad_branch.astype(f32), axis=0)
    grad_attended = cols_product(grad_branch, full_out).astype(bf16)
    moved = ctx_exchange(jnp.split(grad_attended, n_ctx, axis=1))
    grad_heads = jnp.concatenate(moved, axis=0).reshape(length, heads_here, HEAD)

    grad_wout = rows_product(attended_low, grad_branch).astype(bf16).reshape(32, shard, width)
    group = lax.axis_index(GROUP)
    parts = []
    for code in range(8):
        core, y, x = code // 4, code // 2 % 2, code % 2
        owner = group ^ (y * 4 + core * 2 + x)
        wanted = owner // 2 * 8 + jnp.arange(4) * 2 + owner % 2
        wanted = own_ctx_rows(wanted, own_ctx)
        parts.append(jnp.take(grad_wout, wanted, axis=0).reshape(4 * shard, width).astype(f32))
    out_line = group_scatter(parts).reshape(n_z, shard, width)
    grad_wout_out = sum_over_z(list(relative(out_line, own_z)))
    extra = jnp.stack(
        [grad_bout, grad_gain_one, grad_bias_one, grad_bdown, grad_gain_two, grad_bias_two]
    )
    extra = extra.reshape(6, 32, shard).transpose(1, 0, 2).reshape(32, 6 * shard)
    extra = jnp.pad(extra, ((0, 0), (0, 2 * shard)))
    thin = jnp.sum(lax.all_to_all(extra, EVERY, 0, 0, tiled=True), axis=0).reshape(8, shard)

    deltas = jnp.sum(
        grad_heads.astype(f32) * attended.reshape(length, heads_here, HEAD), axis=2
    ).T
    dprobs = jnp.einsum("qhd,khd->hqk", grad_heads, values, preferred_element_type=f32)
    dscores = (probs * (dprobs - deltas[:, :, None])).astype(bf16)
    grad_queries = jnp.einsum("hqk,khd->qhd", dscores, keys, preferred_element_type=f32) * 0.125
    grad_keys = jnp.einsum("hqk,qhd->khd", dscores, queries, preferred_element_type=f32) * 0.125
    grad_values = jnp.einsum("hqk,qhd->khd", probs_low, grad_heads, preferred_element_type=f32)
    grad_mixed = jnp.concatenate(
        [v.astype(bf16).reshape(length, cols) for v in (grad_queries, grad_keys, grad_values)],
        axis=1,
    )
    grad_bias = jnp.sum(grad_mixed.astype(f32), axis=0)
    grad_qkv = rows_product(whole, grad_mixed)
    grad_qkv = jnp.concatenate(
        [
            grad_qkv.reshape(n_dp, n_ctx * shard, 3 * cols),
            jnp.broadcast_to(grad_bias, (n_dp, 16, 3 * cols)),
        ],
        axis=1,
    )
    qkv_sum = dp_sum(list(relative(grad_qkv, own_dp)))
    qkv_rows = qkv_sum[: n_ctx * shard].reshape(n_ctx, shard, 3 * cols)
    qkv_bias = jnp.broadcast_to(qkv_sum[n_ctx * shard :][:8], (n_ctx, 8, 3 * cols))
    qkv_sum = jnp.concatenate([qkv_rows, qkv_bias], axis=1).reshape(-1, 3 * cols)
    qkv_sum = lax.all_to_all(qkv_sum.astype(bf16), CTX, 0, 0, tiled=True).reshape(n_ctx, shard + 8, 3, cols)
    grad_wqkv_out = qkv_sum[:, :shard].astype(f32).transpose(1, 2, 0, 3).reshape(shard, 3 * width)
    bias_sum = qkv_sum[:, shard].transpose(1, 0, 2).reshape(3, width)
    first_own = (own_dp * n_ctx + own_ctx) * shard
    bias_own = lax.dynamic_slice(bias_sum, (0, first_own), (3, shard)).astype(f32)

    input_parts = cols_product(grad_mixed, qkv)
    grad_inputs = grad_first + ctx_sum(jnp.split(input_parts, n_ctx))
    return (
        result.astype(bf16)[None],
        grad_inputs.astype(bf16)[None],
        grad_wqkv_out,
        bias_own[0],
        bias_own[2],
        grad_wout_out,
        thin[0],
        thin[1],
        thin[2],
        grad_wup_out,
        grad_bup_out,
        grad_wdown_out,
        thin[3],
        thin[4],
        thin[5],
    )


def call_heads(mesh, *arrays):
    grid = Mesh(mesh.devices.reshape(2, 2, 4, 2), EVERY)
    rows, lone, block = P(EVERY, None), P(EVERY), P(DP, CTX, None)
    in_specs = (
        block, rows, lone, lone, rows, lone, lone, lone, rows, lone, rows, lone, lone, lone,
        P(DP, CTX), P(DP, CTX), block,
    )
    out_specs = (
        block, block, rows, lone, lone, rows, lone, lone, lone, rows, lone, rows, lone, lone, lone,
    )
    return jax.shard_map(
        heads_body, mesh=grid, in_specs=in_specs, out_specs=out_specs, check_vma=False
    )(*arrays)


def call(mesh, *arrays):
    if mesh.shape["dp"] == 4 and mesh.shape["ctx"] == 8 and arrays[0].shape[1] <= 1024:
        return call_heads(mesh, *arrays)
    return general_call(mesh)(*arrays)


def general_call(mesh):
    in_specs = (
        P("dp", "ctx", None),
        P(("dp", "ctx"), None),
        P(("dp", "ctx")),
        P(("dp", "ctx")),
        P(("dp", "ctx"), None),
        P(("dp", "ctx")),
        P(("dp", "ctx")),
        P(("dp", "ctx")),
        P(("dp", "ctx"), None),
        P(("dp", "ctx")),
        P(("dp", "ctx"), None),
        P(("dp", "ctx")),
        P(("dp", "ctx")),
        P(("dp", "ctx")),
        P("dp", "ctx"),
        P("dp", "ctx"),
        P("dp", "ctx", None),
    )
    out_specs = (
        P("dp", "ctx", None),
        P("dp", "ctx", None),
        P(("dp", "ctx"), None),
        P(("dp", "ctx")),
        P(("dp", "ctx")),
        P(("dp", "ctx"), None),
        P(("dp", "ctx")),
        P(("dp", "ctx")),
        P(("dp", "ctx")),
        P(("dp", "ctx"), None),
        P(("dp", "ctx")),
        P(("dp", "ctx"), None),
        P(("dp", "ctx")),
        P(("dp", "ctx")),
        P(("dp", "ctx")),
    )
    return jax.shard_map(general_body, mesh=mesh, in_specs=in_specs, out_specs=out_specs, check_vma=False)


def solution(mesh):
    return partial(call, mesh)
```

```python
from functools import partial

import jax
import jax.numpy as jnp
from jax import lax
from jax.experimental import pallas as pl
from jax.experimental.pallas import tpu as pltpu
from jax.sharding import Mesh
from jax.sharding import PartitionSpec as P

HEADS = 16
HEAD = 64
WINDOW = 1024


MASKED = -1e30
EPSILON = 1e-05


def layer_norm(values, scales, offsets):
    average = jnp.mean(values, axis=-1, keepdims=True)
    centred = values - average
    variance = jnp.mean(centred * centred, axis=-1, keepdims=True)
    return centred * lax.rsqrt(variance + EPSILON) * scales + offsets


def matmul(left, right):
    return jnp.dot(left, right, preferred_element_type=jnp.float32)


def rows_product(left, right):
    return lax.dot_general(
        left, right, (((0,), (0,)), ((), ())), preferred_element_type=jnp.float32
    )


def cols_product(left, right):
    return lax.dot_general(
        left, right, (((1,), (1,)), ((), ())), preferred_element_type=jnp.float32
    )


def split_heads(matrix):
    return matrix.reshape(matrix.shape[0], HEADS, HEAD)


def allowed_keys(query_tags, query_place, key_tags, key_place):
    same_doc = query_tags[:, None] // 2 == key_tags[None, :] // 2
    distance = jnp.abs(query_place[:, None] - key_place[None, :])
    usable = (key_tags[None, :] % 2 == 1) | (distance == 0)
    return same_doc & (distance <= WINDOW // 2) & usable


def masked_scores(query_block, key_heads, query_tags, query_place, key_tags, key_place):
    raw = (
        jnp.einsum("qhd,khd->hqk", query_block, key_heads, preferred_element_type=jnp.float32)
        * 0.125
    )
    return jnp.where(allowed_keys(query_tags, query_place, key_tags, key_place)[None], raw, MASKED)


def attend_forward(
    query_heads, key_heads, value_heads, query_tags, query_place, key_tags, key_place
):
    row_count = query_heads.shape[0]
    block_rows = min(row_count, 512)

    def one_block(block_index):
        scores = masked_scores(query_heads, key_heads, query_tags, query_place, key_tags, key_place)
        totals = jax.nn.logsumexp(scores, axis=2)
        probs = jnp.exp(scores - totals[:, :, None]).astype(jnp.bfloat16)
        output = jnp.einsum("hqk,khd->qhd", probs, value_heads, preferred_element_type=jnp.float32)
        return (output, totals)

    outputs, totals = lax.map(one_block, jnp.arange(row_count // block_rows, dtype=jnp.int32))
    return (outputs.reshape(row_count, HEADS * HEAD), totals)


def attend_backward(
    query_heads,
    key_heads,
    value_heads,
    grad_heads,
    deltas,
    totals,
    query_tags,
    query_place,
    key_tags,
    key_place,
):
    row_count = query_heads.shape[0]
    block_rows = min(row_count, 512)

    def one_block(running, block_index):
        key_grad, value_grad = running
        scores = masked_scores(query_heads, key_heads, query_tags, query_place, key_tags, key_place)
        probs = jnp.exp(scores - totals[block_index][:, :, None])
        dprobs = jnp.einsum(
            "qhd,khd->hqk", grad_heads, value_heads, preferred_element_type=jnp.float32
        )
        dscores = (probs * (dprobs - deltas[:, :, None])).astype(jnp.bfloat16)
        query_grad = (
            jnp.einsum("hqk,khd->qhd", dscores, key_heads, preferred_element_type=jnp.float32)
            * 0.125
        )
        key_grad = (
            key_grad
            + jnp.einsum("hqk,qhd->khd", dscores, query_heads, preferred_element_type=jnp.float32)
            * 0.125
        )
        value_grad = value_grad + jnp.einsum(
            "hqk,qhd->khd",
            probs.astype(jnp.bfloat16),
            grad_heads,
            preferred_element_type=jnp.float32,
        )
        return ((key_grad, value_grad), query_grad)

    zeros = jnp.zeros(key_heads.shape, jnp.float32)
    (key_grad, value_grad), query_grads = lax.scan(
        one_block, (zeros, zeros), jnp.arange(row_count // block_rows, dtype=jnp.int32)
    )
    key_count = key_heads.shape[0]
    return (
        query_grads.reshape(row_count, HEADS * HEAD),
        key_grad.reshape(key_count, HEADS * HEAD),
        value_grad.reshape(key_count, HEADS * HEAD),
    )


def clip_window(whole, rows_here, seq_length, own_index):
    neighbours = (WINDOW // 2 + rows_here - 1) // rows_here
    key_span = min((2 * neighbours + 1) * rows_here, seq_length)
    first_key = jnp.clip((own_index - neighbours) * rows_here, 0, seq_length - key_span)
    window = tuple((lax.dynamic_slice_in_dim(member, first_key, key_span, 0) for member in whole))
    return (window, first_key)


def window_keys(items, rows_here, seq_length, own_index):
    whole = (
        lax.all_gather(items[0], "ctx", axis=0, tiled=True),
        lax.all_gather(items[1], "ctx", axis=0, tiled=True),
        lax.all_gather(items[2], "ctx", axis=0, tiled=True),
    )
    return clip_window(whole, rows_here, seq_length, own_index)


def window_keys_again(items, rows_here, seq_length, own_index):
    whole = (
        lax.all_gather(items[0], "ctx", axis=0, tiled=True),
        lax.all_gather(items[1], "ctx", axis=0, tiled=True),
        lax.all_gather(items[2], "ctx", axis=0, tiled=True),
    )
    return clip_window(whole, rows_here, seq_length, own_index)


def return_key_grads(key_grad, value_grad, rows_here, first_key):
    width = key_grad.shape[1]
    joined = jnp.concatenate([key_grad, value_grad], axis=1)
    key_span = joined.shape[0]
    count = rows_here * lax.axis_size("ctx")
    padding = jnp.zeros((count, 2 * width), jnp.float32)
    padded = jnp.concatenate([padding, joined, padding], axis=0)
    offset = jnp.clip(jnp.int32(0) - first_key + count, 0, key_span + count)
    summed = lax.psum_scatter(
        lax.dynamic_slice_in_dim(padded, offset, count, 0), "ctx", scatter_dimension=0, tiled=True
    )
    return (summed[:, :width], summed[:, width:])


def general_body(
    tokens,
    w_qkv,
    b_query,
    b_value,
    w_out,
    b_out,
    ln1_gain,
    ln1_bias,
    w_up,
    b_up,
    w_down,
    b_down,
    ln2_gain,
    ln2_bias,
    segment_ids,
    pad_mask,
    cotangent,
):
    weight_shards = (
        w_qkv,
        b_query,
        b_value,
        w_out,
        b_out,
        ln1_gain,
        ln1_bias,
        w_up,
        b_up,
        w_down,
        b_down,
        ln2_gain,
        ln2_bias,
    )
    gathered = (
        lax.all_gather(weight_shards[0], ("dp", "ctx"), axis=0, tiled=True),
        lax.all_gather(weight_shards[1], ("dp", "ctx"), axis=0, tiled=True),
        lax.all_gather(weight_shards[2], ("dp", "ctx"), axis=0, tiled=True),
        lax.all_gather(weight_shards[3], ("dp", "ctx"), axis=0, tiled=True),
        lax.all_gather(weight_shards[4], ("dp", "ctx"), axis=0, tiled=True),
        lax.all_gather(weight_shards[5], ("dp", "ctx"), axis=0, tiled=True),
        lax.all_gather(weight_shards[6], ("dp", "ctx"), axis=0, tiled=True),
        lax.all_gather(weight_shards[7], ("dp", "ctx"), axis=0, tiled=True),
        lax.all_gather(weight_shards[8], ("dp", "ctx"), axis=0, tiled=True),
        lax.all_gather(weight_shards[9], ("dp", "ctx"), axis=0, tiled=True),
        lax.all_gather(weight_shards[10], ("dp", "ctx"), axis=0, tiled=True),
        lax.all_gather(weight_shards[11], ("dp", "ctx"), axis=0, tiled=True),
        lax.all_gather(weight_shards[12], ("dp", "ctx"), axis=0, tiled=True),
    )
    (
        full_qkv,
        full_bquery,
        full_bvalue,
        full_out,
        full_bout,
        full_gain_one,
        full_bias_one,
        full_up,
        full_bup,
        full_down,
        full_bdown,
        full_gain_two,
        full_bias_two,
    ) = gathered
    rows_here = tokens.shape[1]
    seq_length = rows_here * lax.axis_size("ctx")
    own_index = lax.axis_index("ctx")
    inputs = tokens[0]
    inputs_wide = inputs.astype(jnp.float32)
    model_width = inputs.shape[1]
    token_tags = 2 * (segment_ids[0] + 1) + pad_mask[0]
    query_place = own_index * rows_here + jnp.arange(rows_here, dtype=jnp.int32)
    mixed = matmul(inputs, full_qkv)
    queries = (mixed[:, :model_width] + full_bquery.astype(jnp.float32)).astype(jnp.bfloat16)
    keys = mixed[:, model_width : 2 * model_width].astype(jnp.bfloat16)
    values = (mixed[:, 2 * model_width :] + full_bvalue.astype(jnp.float32)).astype(jnp.bfloat16)
    (key_window, value_window, tag_window), first_key = window_keys(
        (keys, values, token_tags), rows_here, seq_length, own_index
    )
    key_place = first_key + jnp.arange(key_window.shape[0], dtype=jnp.int32)
    attended, totals = attend_forward(
        split_heads(queries),
        split_heads(key_window),
        split_heads(value_window),
        token_tags,
        query_place,
        tag_window,
        key_place,
    )
    attended_low = attended.astype(jnp.bfloat16)
    first = inputs_wide + matmul(attended_low, full_out) + full_bout.astype(jnp.float32)
    normed, first_pull = jax.vjp(
        layer_norm, first, full_gain_one.astype(jnp.float32), full_bias_one.astype(jnp.float32)
    )
    normed_low = normed.astype(jnp.bfloat16)
    hidden = matmul(normed_low, full_up) + full_bup.astype(jnp.float32)
    active, gelu_pull = jax.vjp(partial(jax.nn.gelu, approximate=False), hidden)
    active_low = active.astype(jnp.bfloat16)
    second = normed + matmul(active_low, full_down) + full_bdown.astype(jnp.float32)
    result, second_pull = jax.vjp(
        layer_norm, second, full_gain_two.astype(jnp.float32), full_bias_two.astype(jnp.float32)
    )
    gathered = (
        lax.all_gather(weight_shards[0], ("dp", "ctx"), axis=0, tiled=True),
        lax.all_gather(weight_shards[1], ("dp", "ctx"), axis=0, tiled=True),
        lax.all_gather(weight_shards[2], ("dp", "ctx"), axis=0, tiled=True),
        lax.all_gather(weight_shards[3], ("dp", "ctx"), axis=0, tiled=True),
        lax.all_gather(weight_shards[4], ("dp", "ctx"), axis=0, tiled=True),
        lax.all_gather(weight_shards[5], ("dp", "ctx"), axis=0, tiled=True),
        lax.all_gather(weight_shards[6], ("dp", "ctx"), axis=0, tiled=True),
        lax.all_gather(weight_shards[7], ("dp", "ctx"), axis=0, tiled=True),
        lax.all_gather(weight_shards[8], ("dp", "ctx"), axis=0, tiled=True),
        lax.all_gather(weight_shards[9], ("dp", "ctx"), axis=0, tiled=True),
        lax.all_gather(weight_shards[10], ("dp", "ctx"), axis=0, tiled=True),
        lax.all_gather(weight_shards[11], ("dp", "ctx"), axis=0, tiled=True),
        lax.all_gather(weight_shards[12], ("dp", "ctx"), axis=0, tiled=True),
    )
    back_qkv = gathered[0]
    back_out = gathered[3]
    back_up = gathered[7]
    back_down = gathered[9]
    grad_second, grad_gain_two, grad_bias_two = second_pull(cotangent[0].astype(jnp.float32))
    grad_outcome = grad_second.astype(jnp.bfloat16)
    grad_wdown = rows_product(active_low, grad_outcome)
    grad_bdown = jnp.sum(grad_outcome.astype(jnp.float32), axis=0)
    (grad_active,) = gelu_pull(cols_product(grad_outcome, back_down))
    grad_hidden = grad_active.astype(jnp.bfloat16)
    grad_wup = rows_product(normed_low, grad_hidden)
    grad_bup = jnp.sum(grad_hidden.astype(jnp.float32), axis=0)
    grad_normed = grad_second + cols_product(grad_hidden, back_up)
    grad_first, grad_gain_one, grad_bias_one = first_pull(grad_normed)
    grad_branch = grad_first.astype(jnp.bfloat16)
    grad_wout = rows_product(attended_low, grad_branch)
    grad_bout = jnp.sum(grad_branch.astype(jnp.float32), axis=0)
    grad_attended = cols_product(grad_branch, back_out).astype(jnp.bfloat16)
    deltas = jnp.sum(
        (grad_attended.astype(jnp.float32) * attended).reshape(rows_here, HEADS, HEAD), axis=2
    ).T
    (key_again, value_again, tag_again), first_again = window_keys_again(
        (keys, values, token_tags), rows_here, seq_length, own_index
    )
    place_again = first_again + jnp.arange(key_again.shape[0], dtype=jnp.int32)
    grad_queries, key_grad, value_grad = attend_backward(
        split_heads(queries),
        split_heads(key_again),
        split_heads(value_again),
        split_heads(grad_attended),
        deltas,
        totals,
        token_tags,
        query_place,
        tag_again,
        place_again,
    )
    key_total, value_total = return_key_grads(key_grad, value_grad, rows_here, first_again)
    grad_query_low = grad_queries.astype(jnp.bfloat16)
    grad_value_low = value_total.astype(jnp.bfloat16)
    grad_mixed = jnp.concatenate(
        [grad_query_low, key_total.astype(jnp.bfloat16), grad_value_low], axis=1
    )
    grad_wqkv = rows_product(inputs, grad_mixed)
    grad_bquery = jnp.sum(grad_query_low.astype(jnp.float32), axis=0)
    grad_bvalue = jnp.sum(grad_value_low.astype(jnp.float32), axis=0)
    grad_inputs = grad_first + cols_product(grad_mixed, back_qkv)
    summed = (
        lax.psum_scatter(grad_wqkv, ("dp", "ctx"), scatter_dimension=0, tiled=True),
        lax.psum_scatter(grad_bquery, ("dp", "ctx"), scatter_dimension=0, tiled=True),
        lax.psum_scatter(grad_bvalue, ("dp", "ctx"), scatter_dimension=0, tiled=True),
        lax.psum_scatter(grad_wout, ("dp", "ctx"), scatter_dimension=0, tiled=True),
        lax.psum_scatter(grad_bout, ("dp", "ctx"), scatter_dimension=0, tiled=True),
        lax.psum_scatter(grad_gain_one, ("dp", "ctx"), scatter_dimension=0, tiled=True),
        lax.psum_scatter(grad_bias_one, ("dp", "ctx"), scatter_dimension=0, tiled=True),
        lax.psum_scatter(grad_wup, ("dp", "ctx"), scatter_dimension=0, tiled=True),
        lax.psum_scatter(grad_bup, ("dp", "ctx"), scatter_dimension=0, tiled=True),
        lax.psum_scatter(grad_wdown, ("dp", "ctx"), scatter_dimension=0, tiled=True),
        lax.psum_scatter(grad_bdown, ("dp", "ctx"), scatter_dimension=0, tiled=True),
        lax.psum_scatter(grad_gain_two, ("dp", "ctx"), scatter_dimension=0, tiled=True),
        lax.psum_scatter(grad_bias_two, ("dp", "ctx"), scatter_dimension=0, tiled=True),
    )
    return (
        result.astype(jnp.bfloat16)[None],
        grad_inputs.astype(jnp.bfloat16)[None],
        summed[0],
        summed[1],
        summed[2],
        summed[3],
        summed[4],
        summed[5],
        summed[6],
        summed[7],
        summed[8],
        summed[9],
        summed[10],
        summed[11],
        summed[12],
    )


GROUP = ("y", "core", "x")
CTX = ("z", "x")
DP = ("y", "core")
EVERY = ("y", "core", "z", "x")
bf16, f32 = jnp.bfloat16, jnp.float32


def swap(member, axes, code):
    count = 1
    for axis in axes:
        count *= lax.axis_size(axis)
    return lax.ppermute(member, axes, [(place, place ^ code) for place in range(count)])


def like(shape, kind):
    return jax.ShapeDtypeStruct(shape, kind)


def local(kernel, outs, place, *operands, scratch=(), flops=0):
    whole = pl.BlockSpec(memory_space=pltpu.VMEM)
    moved = sum(v.size * v.dtype.itemsize for v in operands)
    moved += sum(o.size * jnp.dtype(o.dtype).itemsize for o in outs)
    return pl.pallas_call(
        kernel,
        out_shape=list(outs),
        in_specs=[pl.BlockSpec(memory_space=pltpu.SMEM)] + [whole] * len(operands),
        out_specs=[whole] * len(outs),
        scratch_shapes=list(scratch),
        cost_estimate=pl.CostEstimate(flops=flops, bytes_accessed=moved, transcendentals=0),
        compiler_params=pltpu.CompilerParams(vmem_limit_bytes=48 << 20),
    )(place, *operands)


def pair_product(left, right):
    return lax.dot_general(
        left, right, (((0,), (0,)), ((), ())), preferred_element_type=jnp.float32
    )


def plane_gather(block):
    return [block] + [swap(block, ("y", "x"), code) for code in range(1, 4)]


def group_gather(block):
    plane = plane_gather(block)
    return plane + [swap(member, ("core",), 1) for member in plane]


def merge_kernel(place, near, far, own, *sent):
    rows = own.shape[0]
    for code in range(4):
        part = pl.ds(code * rows, rows)
        total = near[part, :].astype(f32) + far[part, :].astype(f32)
        if code == 0:
            own[...] = total
        else:
            sent[code - 1][...] = total.astype(bf16)


def group_scatter(near, far, place):
    rows, width = near.shape[0] // 4, near.shape[1]
    crossed = swap(far, ("core",), 1)
    outs = [like((rows, width), f32)] + [like((rows, width), bf16)] * 3
    own, *sent = local(merge_kernel, outs, place, near, crossed)
    return [own] + [swap(sent[code - 1], ("y", "x"), code) for code in range(1, 4)]


def sum_over_z(parts):
    total = parts[0].astype(f32)
    for code in range(1, 4):
        total = total + swap(parts[code], ("z",), code).astype(f32)
    return total


def ctx_gather(block):
    line = [block] + [swap(block, ("z",), code) for code in range(1, 4)]
    return [piece for member in line for piece in (member, swap(member, ("x",), 1))]


def out_gather(block):
    line = jnp.stack([block] + [swap(block, ("z",), code) for code in range(1, 4)])
    both = [line, swap(line, ("y",), 1)]
    both = jnp.stack(both)
    far = swap(both, ("x",), 1)
    return [both, far, swap(both, ("core",), 1), swap(far, ("core",), 1)]


def order_kernel(place, p00, p01, p10, p11, up_ref, out_ref, up_out):
    rows = p00.shape[2]
    own = place[0]
    for core in range(2):
        for x in range(2):
            piece = ((p00, p01), (p10, p11))[core][x]
            for y in range(2):
                for z in range(4):
                    at = own ^ (y * 16 + core * 8 + z * 2 + x)
                    out_ref[pl.ds(at * rows, rows), :] = piece[y, z]
    for y in range(2):
        for core in range(2):
            for z in range(4):
                for x in range(2):
                    at = y * 16 + core * 8 + z * 2 + x
                    block = up_ref[pl.ds((z * 8 + y * 4 + core * 2 + x) * rows, rows), :]
                    up_out[pl.ds(at * rows, rows), :] = block


def allowed_here(query_tags, query_place, key_tags, key_place):
    same_doc = (query_tags >> 1) == (key_tags >> 1)
    distance = jnp.abs(query_place - key_place)
    usable = ((key_tags & 1) == 1) | (distance == 0)
    return same_doc & (distance <= WINDOW // 2) & usable


def places(own_ctx, rows, shape, axis, start=0):
    index = lax.broadcasted_iota(jnp.int32, shape, axis) + start
    return ((index // rows) ^ own_ctx) * rows + index % rows


def attend_kernel(
    place, *refs, n_blocks, rows, cols
):
    blocks, refs = refs[:n_blocks], refs[n_blocks:]
    pieces, refs = refs[:4], refs[4:]
    bias, tags_col, tags_row, q_ref, k_ref, v_ref, att_ref, msg_ref, lse_ref, qkv_ref = refs[:10]
    own_dp, own_ctx = place[1], place[2]
    shard = 32
    for m, piece in enumerate(pieces):
        for c in range(n_blocks):
            at = ((own_dp ^ m) * n_blocks + c) * shard
            qkv_ref[pl.ds(at, shard), :] = piece[c, :shard, :]
    for j, block in enumerate(blocks):
        part = pl.ds(j * rows, rows)
        mixed = matmul(block[...], qkv_ref[...]) + bias[...]
        q_ref[part, :] = mixed[:, :cols].astype(bf16)
        k_ref[part, :] = mixed[:, cols : 2 * cols].astype(bf16)
        v_ref[part, :] = mixed[:, 2 * cols :].astype(bf16)
    length = n_blocks * rows
    chunk = 2 * rows

    def step(index, carry):
        part = pl.ds(index * chunk, chunk)
        allowed = allowed_here(
            tags_col[part, :],
            places(own_ctx, rows, (chunk, 1), 0, index * chunk),
            tags_row[...],
            places(own_ctx, rows, (1, length), 1),
        )
        found = []
        for head in range(cols // HEAD):
            lanes = slice(head * HEAD, (head + 1) * HEAD)
            scores = cols_product(q_ref[part, lanes], k_ref[:, lanes]) * 0.125
            scores = jnp.where(allowed, scores, MASKED)
            top = jnp.max(scores, axis=1, keepdims=True)
            weights = jnp.exp(scores - top)
            mass = jnp.sum(weights, axis=1, keepdims=True)
            found.append(matmul(weights.astype(bf16), v_ref[:, lanes]) / mass)
            total = top + jnp.log(mass)
            lse_ref[pl.ds(head, 1), part] = jnp.broadcast_to(total, (chunk, 128)).T[:1, :]
        attended = jnp.concatenate(found, axis=1)
        att_ref[part, :] = attended
        for half in range(2):
            at = ((index * 2 + half) ^ own_ctx) * rows
            msg_ref[pl.ds(at, rows), :] = attended[half * rows : (half + 1) * rows].astype(bf16)
        return carry

    lax.fori_loop(0, length // chunk, step, 0)


def branch_kernel(place, moved, w_out, inputs, vectors, normed_ref, low_ref, hat_ref, rate_ref):
    groups, rows, cols = moved.shape
    total = inputs[...].astype(f32) + vectors[2:3, :]
    for c in range(groups):
        total = total + matmul(moved[c], w_out[pl.ds(c * cols, cols), :])
    centred = total - jnp.mean(total, axis=1, keepdims=True)
    rate = lax.rsqrt(jnp.mean(centred * centred, axis=1, keepdims=True) + EPSILON)
    hat = centred * rate
    normed = hat * vectors[3:4, :] + vectors[4:5, :]
    normed_ref[...] = normed
    low_ref[...] = normed.astype(bf16)
    hat_ref[...] = hat
    rate_ref[...] = jnp.broadcast_to(rate, rate_ref.shape)


def forward_kernel(place, *refs):
    blocks = refs[:8]
    up, bias, down, hidden_ref, active_ref, near, far = refs[8:]
    rows = blocks[0].shape[0]
    for pair in range(4):
        lines = jnp.concatenate([blocks[2 * pair][...], blocks[2 * pair + 1][...]], axis=0)
        part = pl.ds(pair * 2 * rows, 2 * rows)
        hidden = matmul(lines, up[...]) + bias[...]
        hidden_ref[part, :] = hidden
        active = (0.5 * hidden * (1 + lax.erf(hidden * 0.7071067811865476))).astype(bf16)
        active_ref[part, :] = active
        target = near if pair < 2 else far
        target[pl.ds(pair % 2 * 2 * rows, 2 * rows), :] = matmul(active, down[...]).astype(bf16)


def second_kernel(
    place, normed, own, p1, p2, p3, vectors, cotangent, result_ref, grad_ref, low_ref, sums_ref
):
    second = normed[...] + own[...] + p1[...].astype(f32) + p2[...].astype(f32)
    second = second + p3[...].astype(f32) + vectors[5:6, :]
    centred = second - jnp.mean(second, axis=1, keepdims=True)
    rate = lax.rsqrt(jnp.mean(centred * centred, axis=1, keepdims=True) + EPSILON)
    hat = centred * rate
    gain = vectors[6:7, :]
    result_ref[...] = (hat * gain + vectors[7:8, :]).astype(bf16)
    grad = cotangent[...].astype(f32)
    scaled = grad * gain
    mean_scaled = jnp.mean(scaled, axis=1, keepdims=True)
    mean_hat = jnp.mean(scaled * hat, axis=1, keepdims=True)
    grad_second = rate * (scaled - mean_scaled - hat * mean_hat)
    grad_ref[...] = grad_second
    low = grad_second.astype(bf16)
    low_ref[...] = low
    sums_ref[0:1, :] = jnp.sum(low.astype(f32), axis=0, keepdims=True)
    sums_ref[1:2, :] = jnp.sum(grad * hat, axis=0, keepdims=True)
    sums_ref[2:3, :] = jnp.sum(grad, axis=0, keepdims=True)


def backward_kernel(place, *refs):
    blocks = refs[:8]
    up, down, slope, grad_ref, near, far = refs[8:]
    rows = blocks[0].shape[0]
    for pair in range(4):
        lines = jnp.concatenate([blocks[2 * pair][...], blocks[2 * pair + 1][...]], axis=0)
        part = pl.ds(pair * 2 * rows, 2 * rows)
        grad = (slope[part, :] * cols_product(lines, down[...])).astype(bf16)
        grad_ref[part, :] = grad
        target = near if pair < 2 else far
        target[pl.ds(pair % 2 * 2 * rows, 2 * rows), :] = cols_product(grad, up[...]).astype(bf16)


def ff_grads_kernel(place, *refs):
    grads, normed = refs[:8], refs[8:16]
    active, grad_hidden, down_ref, up_ref, lines, sums = refs[16:]
    own_z = place[3]
    rows, width = grads[0].shape
    units = active.shape[1]
    shard = units // 4
    for j in range(8):
        lines[pl.ds(j * rows, rows), :] = grads[j][...]
    total = jnp.sum(grad_hidden[...].astype(f32), axis=0, keepdims=True)
    for z in range(4):
        at = own_z ^ z
        part = slice(z * shard, (z + 1) * shard)
        down_ref[at, :shard, :] = pair_product(active[:, part], lines[...]).astype(bf16)
        down_ref[at, shard:, :shard] = jnp.broadcast_to(total[:, part], (16, shard)).astype(bf16)
        down_ref[at, shard:, shard:] = jnp.zeros((16, width - shard), bf16)
    for j in range(8):
        lines[pl.ds(j * rows, rows), :] = normed[j][...]
    for quarter in range(4):
        span = 8 * 32
        part = slice(quarter * span, (quarter + 1) * span)
        found = pair_product(lines[:, part], grad_hidden[...]).astype(bf16)
        for z in range(4):
            for x in range(2):
                piece = found[(z * 2 + x) * 32 : (z * 2 + x + 1) * 32]
                up_ref[own_z ^ z, pl.ds((quarter * 2 + x) * 32, 32), :] = piece


def first_kernel(
    place, grad_second, own, p1, p2, p3, vectors, hat_ref, rate_ref, w_out, grad_ref, low_ref, msg_ref,
    sums_ref,
):
    grad = grad_second[...] + own[...] + p1[...].astype(f32) + p2[...].astype(f32)
    grad = grad + p3[...].astype(f32)
    hat = hat_ref[...]
    scaled = grad * vectors[3:4, :]
    mean_scaled = jnp.mean(scaled, axis=1, keepdims=True)
    mean_hat = jnp.mean(scaled * hat, axis=1, keepdims=True)
    grad_first = rate_ref[:, :1] * (scaled - mean_scaled - hat * mean_hat)
    grad_ref[...] = grad_first
    low = grad_first.astype(bf16)
    low_ref[...] = low
    groups, rows, cols = msg_ref.shape
    for c in range(groups):
        msg_ref[c] = cols_product(low, w_out[pl.ds(c * cols, cols), :]).astype(bf16)
    sums_ref[0:1, :] = jnp.sum(low.astype(f32), axis=0, keepdims=True)
    sums_ref[1:2, :] = jnp.sum(grad * hat, axis=0, keepdims=True)
    sums_ref[2:3, :] = jnp.sum(grad, axis=0, keepdims=True)


def out_grad_kernel(place, moved, low, near, far, parts):
    groups, rows, cols = moved.shape
    own_y, own_core, own_x = place[4], place[5], place[6]
    for c in range(groups):
        found = pair_product(moved[c], low[...]).astype(bf16)
        for m in range(4):
            y, core, z, x = c // 4, c // 2 % 2, c % 2 * 2 + m // 2, m % 2
            code = (core ^ own_core) * 4 + (y ^ own_y) * 2 + (x ^ own_x)
            parts[code, pl.ds(z * 32, 32), :] = found[m * 32 : (m + 1) * 32]
    for code in range(4):
        near[pl.ds(code * rows, rows), :] = parts[code]
        far[pl.ds(code * rows, rows), :] = parts[code + 4]


def attend_grad_kernel(
    place, moved, q_ref, k_ref, v_ref, att_ref, lse_ref, tags_col, tags_row, qkv_ref,
    mixed_ref, sums_ref, m0, m1, m2, m3, m4, m5, m6, m7, key_grad, value_grad, back,
):
    messages = (m0, m1, m2, m3, m4, m5, m6, m7)
    groups, rows, cols = moved.shape
    length = groups * rows
    own_ctx = place[2]
    for j in range(groups):
        back[pl.ds(j * rows, rows), :] = moved[own_ctx ^ j]
    key_grad[...] = jnp.zeros(key_grad.shape, f32)
    value_grad[...] = jnp.zeros(value_grad.shape, f32)
    chunk = 2 * rows

    def step(index, carry):
        part = pl.ds(index * chunk, chunk)
        allowed = allowed_here(
            tags_row[:, part],
            places(own_ctx, rows, (1, chunk), 1, index * chunk),
            tags_col[...],
            places(own_ctx, rows, (length, 1), 0),
        )
        weighted = (back[part, :].astype(f32) * att_ref[part, :]).T
        found = []
        for head in range(cols // HEAD):
            lanes = slice(head * HEAD, (head + 1) * HEAD)
            delta = jnp.sum(weighted[lanes, :], axis=0, keepdims=True)
            scores = cols_product(k_ref[:, lanes], q_ref[part, lanes]) * 0.125
            probs = jnp.where(allowed, jnp.exp(scores - lse_ref[pl.ds(head, 1), part]), 0.0)
            grads = cols_product(v_ref[:, lanes], back[part, lanes])
            grads = (probs * (grads - delta)).astype(bf16)
            value_grad[:, lanes] += matmul(probs.astype(bf16), back[part, lanes])
            key_grad[:, lanes] += matmul(grads, q_ref[part, lanes])
            found.append(pair_product(grads, k_ref[:, lanes]) * 0.125)
        mixed_ref[part, :cols] = jnp.concatenate(found, axis=1).astype(bf16)
        return carry

    lax.fori_loop(0, length // chunk, step, 0)
    mixed_ref[:, cols : 2 * cols] = (key_grad[...] * 0.125).astype(bf16)
    mixed_ref[:, 2 * cols :] = value_grad[...].astype(bf16)
    sums_ref[...] = jnp.sum(mixed_ref[...].astype(f32), axis=0, keepdims=True)
    for j in range(groups):
        part = cols_product(mixed_ref[pl.ds(j * rows, rows), :], qkv_ref[...])
        messages[j][...] = part.astype(messages[j].dtype)


def qkv_grad_kernel(place, *refs):
    blocks = refs[:8]
    mixed, sums, near, far, lines = refs[8:]
    own_dp = place[1]
    rows = blocks[0].shape[0]
    for j in range(8):
        lines[pl.ds(j * rows, rows), :] = blocks[j][...]
    span = lines.shape[1] // 4
    for ky in range(2):
        for kc in range(2):
            start = pl.multiple_of((own_dp ^ (ky * 2 + kc)) * span, span)
            found = pair_product(lines[:, pl.ds(start, span)], mixed[...]).astype(bf16)
            target = far if kc else near
            target[ky, :span, :] = found
            target[ky, span:, :] = jnp.broadcast_to(sums[...], (16, mixed.shape[1])).astype(bf16)


def dp_sum(near, far):
    crossed = swap(far, ("core",), 1).astype(f32)
    total = near.astype(f32) + crossed
    return total[0] + swap(total[1].astype(bf16), ("y",), 1).astype(f32)


def ctx_sum(parts):
    line = [None] * 4
    for code in (3, 2, 1, 0):
        crossed = swap(parts[2 * code + 1], ("x",), 1)
        line[code] = parts[2 * code].astype(f32) + crossed.astype(f32)
        if code:
            line[code] = swap(line[code].astype(bf16), ("z",), code).astype(f32)
    return line[0] + line[1] + line[2] + line[3]


def up_final_kernel(place, moved, out):
    groups, shard, wide = moved.shape
    units = wide // 4
    for g in range(groups):
        for z in range(4):
            at = ((g // 2 * 4 + z) * 2 + g % 2) * units
            out[:, at : at + units] = moved[g, :, z * units : (z + 1) * units].astype(f32)


def qkv_final_kernel(place, moved, out):
    groups, _, wide = moved.shape
    shard, cols = out.shape[0], wide // 3
    for c in range(groups):
        for kind in range(3):
            at = (kind * groups + c) * cols
            out[:, at : at + cols] = moved[c, :shard, kind * cols : (kind + 1) * cols].astype(f32)


def heads_body(
    tokens, w_qkv, b_query, b_value, w_out, b_out, ln1_gain, ln1_bias, w_up, b_up, w_down, b_down,
    ln2_gain, ln2_bias, segment_ids, pad_mask, cotangent,
):
    inputs = tokens[0]
    rows, width = inputs.shape
    n_ctx = lax.axis_size(CTX)
    n_dp = lax.axis_size(DP)
    n_z = lax.axis_size("z")
    length = rows * n_ctx
    cols = width // n_ctx
    shard = w_qkv.shape[0]
    units = w_down.shape[0]
    wide = n_z * units
    own_ctx = lax.axis_index(CTX)
    own_dp = lax.axis_index(DP)
    own = lax.axis_index(EVERY)
    place = jnp.stack(
        [own, own_dp, own_ctx, lax.axis_index("z")] + [lax.axis_index(a) for a in GROUP]
    ).astype(jnp.int32)

    blocks = ctx_gather(inputs)
    tags_here = (2 * (segment_ids[0] + 1) + pad_mask[0]).astype(bf16)
    packed = jnp.concatenate(
        [b_query, b_value, b_out, ln1_gain, ln1_bias, b_down, ln2_gain, ln2_bias, b_up, tags_here]
    )
    packed = jnp.pad(packed, (0, 6 * cols - packed.size)).reshape(2, 3 * cols)
    qkv = w_qkv.reshape(shard, 3, n_ctx, cols).transpose(2, 0, 1, 3).reshape(n_ctx, shard, 3 * cols)
    packed = jnp.broadcast_to(jnp.pad(packed, ((0, 14), (0, 0))), (n_ctx, 16, 3 * cols))
    qkv = jnp.concatenate([qkv, packed], axis=1)
    qkv = lax.all_to_all(qkv, CTX, 0, 0, tiled=True)
    qkv_y = swap(qkv, ("y",), 1)
    pieces = [qkv, swap(qkv, ("core",), 1), qkv_y, swap(qkv_y, ("core",), 1)]
    small = jnp.stack([piece[:, shard : shard + 2] for piece in pieces])
    small = jnp.take(small, own_dp ^ jnp.arange(n_dp), axis=0).reshape(n_dp * n_ctx, 6 * cols)
    vectors = small[:, : 8 * shard].reshape(-1, 8, shard).transpose(1, 0, 2).reshape(8, width)
    vectors = vectors.astype(f32)
    at = 8 * shard
    bias_up = small[:, at : at + units].reshape(n_dp, n_z, 2, units)
    bias_up = lax.dynamic_slice(bias_up, (own_dp, 0, lax.axis_index("x"), 0), (1, n_z, 1, units))
    bias_up = bias_up.reshape(1, wide).astype(f32)
    at += units
    tags = small[:, at : at + rows].reshape(n_dp, n_ctx, rows)
    tags = lax.dynamic_slice(tags, (own_dp, 0, 0), (1, n_ctx, rows))[0].astype(jnp.int32)
    tags = jnp.take(tags, own_ctx ^ jnp.arange(n_ctx), axis=0)
    tags_row, tags_col = tags.reshape(1, length), tags.reshape(length, 1)
    bias = lax.dynamic_slice(vectors, (0, own_ctx * cols), (2, cols))
    bias = jnp.concatenate([bias[:1], jnp.zeros((1, cols), f32), bias[1:]], axis=1)

    up = w_up.reshape(shard, 2, 2, n_z, 2, units).transpose(1, 2, 4, 0, 3, 5)
    up = lax.all_to_all(up.reshape(8 * shard, wide), GROUP, 0, 0, tiled=True)
    up = lax.all_gather(up, "z", axis=0, tiled=True)
    down = lax.all_gather(w_down, "z", axis=0, tiled=True)
    full_out, full_up = local(
        order_kernel, [like((width, width), bf16), like((width, wide), bf16)], place,
        *out_gather(w_out), up,
    )

    queries, keys, values, attended, message, totals, full_qkv = local(
        partial(attend_kernel, n_blocks=n_ctx, rows=rows, cols=cols),
        [like((length, cols), bf16)] * 3
        + [
            like((length, cols), f32),
            like((length, cols), bf16),
            like((8, length), f32),
            like((width, 3 * cols), bf16),
        ],
        place, *blocks, *pieces, bias, tags_col, tags_row,
        flops=8 * length * length * cols,
    )
    moved = lax.all_to_all(message, CTX, 0, 0, tiled=True).reshape(n_ctx, rows, cols)
    normed, normed_low, hat, rate = local(
        branch_kernel,
        [like((rows, width), f32), like((rows, width), bf16), like((rows, width), f32)]
        + [like((rows, 128), f32)],
        place, moved, full_out, inputs, vectors, flops=2 * rows * width * width,
    )
    normed_all = group_gather(normed_low)
    hidden, active, near, far = local(
        forward_kernel,
        [like((8 * rows, wide), f32), like((8 * rows, wide), bf16)]
        + [like((4 * rows, width), bf16)] * 2,
        place, *normed_all, full_up, bias_up, down, flops=32 * rows * width * wide,
    )
    parts = group_scatter(near, far, place)
    result, grad_second, grad_z, sums_two = local(
        second_kernel,
        [like((rows, width), bf16), like((rows, width), f32), like((rows, width), bf16)]
        + [like((8, width), f32)],
        place, normed, *parts, vectors, cotangent[0],
    )

    slope = 0.5 * (1 + lax.erf(hidden * 0.7071067811865476)) + hidden * (
        jnp.exp(-0.5 * hidden * hidden) * 0.3989422804014327
    )
    grad_z_all = group_gather(grad_z)
    grad_hidden, near, far = local(
        backward_kernel,
        [like((8 * rows, wide), bf16)] + [like((4 * rows, width), bf16)] * 2,
        place, *grad_z_all, full_up, down, slope, flops=32 * rows * width * wide,
    )
    parts = group_scatter(near, far, place)
    grad_first, grad_branch, message, sums_one = local(
        first_kernel,
        [like((rows, width), f32), like((rows, width), bf16), like((n_ctx, rows, cols), bf16)]
        + [like((8, width), f32)],
        place, grad_second, *parts, vectors, hat, rate, full_out, flops=2 * rows * width * width,
    )
    grad_moved = lax.all_to_all(message, CTX, 0, 0, tiled=True)
    down_parts, up_parts = local(
        ff_grads_kernel,
        [like((n_z, units + 16, width), bf16), like((n_z, 8 * shard, wide), bf16)],
        place, *grad_z_all, *normed_all, active, grad_hidden,
        scratch=[pltpu.VMEM((8 * rows, width), bf16), pltpu.VMEM((8, 128), f32)],
        flops=32 * rows * width * wide,
    )
    down_sum = sum_over_z(list(down_parts))
    up_sum = sum_over_z(list(up_parts)).astype(bf16)
    up_sum = lax.all_to_all(up_sum, GROUP, 0, 0, tiled=True).reshape(8, shard, wide)
    (grad_wup,) = local(up_final_kernel, [like((shard, w_up.shape[1]), f32)], place, up_sum)

    near, far = local(
        out_grad_kernel, [like((4 * rows, width), bf16)] * 2, place, moved, grad_branch,
        scratch=[pltpu.VMEM((8, rows, width), bf16)], flops=2 * rows * width * width,
    )
    own_part, *others = group_scatter(near, far, place)
    line = own_part + others[0].astype(f32) + others[1].astype(f32) + others[2].astype(f32)
    line = jnp.take(line.reshape(n_z, shard, width), lax.axis_index("z") ^ jnp.arange(n_z), axis=0)
    line = [line[0]] + list(line[1:].astype(bf16))
    grad_wout = sum_over_z(line)

    extra = jnp.concatenate([sums_one[:3], sums_two[:3]], axis=0)
    extra = extra.reshape(6, 32, shard).transpose(1, 0, 2).reshape(32, 6 * shard)
    extra = jnp.pad(extra, ((0, 0), (0, 2 * shard)))
    thin = jnp.sum(lax.all_to_all(extra, EVERY, 0, 0, tiled=True), axis=0).reshape(8, shard)

    mixed, sums, *messages = local(
        attend_grad_kernel,
        [like((length, 3 * cols), bf16), like((1, 3 * cols), f32)]
        + [like((rows, width), bf16)] * n_ctx,
        place, grad_moved, queries, keys, values, attended, totals, tags_col, tags_row, full_qkv,
        scratch=[
            pltpu.VMEM((length, cols), f32),
            pltpu.VMEM((length, cols), f32),
            pltpu.VMEM((length, cols), bf16),
        ],
        flops=20 * length * length * cols,
    )
    grad_inputs = grad_first + ctx_sum(messages)
    near, far = local(
        qkv_grad_kernel, [like((2, width // 4 + 16, 3 * cols), bf16)] * 2, place, *blocks, mixed,
        sums, scratch=[pltpu.VMEM((length, width), bf16)], flops=6 * length * width * cols,
    )
    qkv_sum = dp_sum(near, far)
    qkv_rows = qkv_sum[: n_ctx * shard].reshape(n_ctx, shard, 3 * cols)
    qkv_bias = jnp.broadcast_to(qkv_sum[n_ctx * shard :], (n_ctx, 16, 3 * cols))
    qkv_sum = jnp.concatenate([qkv_rows, qkv_bias], axis=1).astype(bf16)
    qkv_sum = lax.all_to_all(qkv_sum, CTX, 0, 0, tiled=True)
    (grad_wqkv,) = local(qkv_final_kernel, [like((shard, 3 * width), f32)], place, qkv_sum)
    bias_sum = qkv_sum[:, shard].reshape(n_ctx, 3, cols).transpose(1, 0, 2).reshape(3, width)
    bias_own = lax.dynamic_slice(bias_sum, (0, own * shard), (3, shard)).astype(f32)

    return (
        result[None],
        grad_inputs.astype(bf16)[None],
        grad_wqkv,
        bias_own[0],
        bias_own[2],
        grad_wout,
        thin[0],
        thin[1],
        thin[2],
        grad_wup,
        down_sum[units, :units],
        down_sum[:units],
        thin[3],
        thin[4],
        thin[5],
    )


def call_heads(mesh, *arrays):
    grid = Mesh(mesh.devices.reshape(2, 2, 4, 2), EVERY)
    lines, lone, block = P(EVERY, None), P(EVERY), P(DP, CTX, None)
    in_specs = (
        block, lines, lone, lone, lines, lone, lone, lone, lines, lone, lines, lone, lone, lone,
        P(DP, CTX), P(DP, CTX), block,
    )
    out_specs = (
        block, block, lines, lone, lone, lines, lone, lone, lone, lines, lone, lines, lone, lone,
        lone,
    )
    return jax.shard_map(
        heads_body, mesh=grid, in_specs=in_specs, out_specs=out_specs, check_vma=False
    )(*arrays)


def call(mesh, *arrays):
    if mesh.shape["dp"] == 4 and mesh.shape["ctx"] == 8 and arrays[0].shape[1] == 1024:
        return call_heads(mesh, *arrays)
    return general_call(mesh)(*arrays)


def general_call(mesh):
    in_specs = (
        P("dp", "ctx", None),
        P(("dp", "ctx"), None),
        P(("dp", "ctx")),
        P(("dp", "ctx")),
        P(("dp", "ctx"), None),
        P(("dp", "ctx")),
        P(("dp", "ctx")),
        P(("dp", "ctx")),
        P(("dp", "ctx"), None),
        P(("dp", "ctx")),
        P(("dp", "ctx"), None),
        P(("dp", "ctx")),
        P(("dp", "ctx")),
        P(("dp", "ctx")),
        P("dp", "ctx"),
        P("dp", "ctx"),
        P("dp", "ctx", None),
    )
    out_specs = (
        P("dp", "ctx", None),
        P("dp", "ctx", None),
        P(("dp", "ctx"), None),
        P(("dp", "ctx")),
        P(("dp", "ctx")),
        P(("dp", "ctx"), None),
        P(("dp", "ctx")),
        P(("dp", "ctx")),
        P(("dp", "ctx")),
        P(("dp", "ctx"), None),
        P(("dp", "ctx")),
        P(("dp", "ctx"), None),
        P(("dp", "ctx")),
        P(("dp", "ctx")),
        P(("dp", "ctx")),
    )
    return jax.shard_map(general_body, mesh=mesh, in_specs=in_specs, out_specs=out_specs, check_vma=False)


def solution(mesh):
    return partial(call, mesh)
```

```python
import math
from functools import partial

import jax
import jax.numpy as jnp
from jax import lax
from jax.experimental import pallas as pl
from jax.experimental.pallas import tpu as pltpu
from jax.sharding import Mesh
from jax.sharding import PartitionSpec as P

HEADS = 16
HEAD = 64
WINDOW = 1024


MASKED = -1e30
EPSILON = 1e-05


def layer_norm(values, scales, offsets):
    average = jnp.mean(values, axis=-1, keepdims=True)
    centred = values - average
    variance = jnp.mean(centred * centred, axis=-1, keepdims=True)
    return centred * lax.rsqrt(variance + EPSILON) * scales + offsets


def matmul(left, right):
    return jnp.dot(left, right, preferred_element_type=jnp.float32)


def rows_product(left, right):
    return lax.dot_general(
        left, right, (((0,), (0,)), ((), ())), preferred_element_type=jnp.float32
    )


def cols_product(left, right):
    return lax.dot_general(
        left, right, (((1,), (1,)), ((), ())), preferred_element_type=jnp.float32
    )


def split_heads(matrix):
    return matrix.reshape(matrix.shape[0], HEADS, HEAD)


def allowed_keys(query_tags, query_place, key_tags, key_place):
    same_doc = query_tags[:, None] // 2 == key_tags[None, :] // 2
    distance = jnp.abs(query_place[:, None] - key_place[None, :])
    usable = (key_tags[None, :] % 2 == 1) | (distance == 0)
    return same_doc & (distance <= WINDOW // 2) & usable


def masked_scores(query_block, key_heads, query_tags, query_place, key_tags, key_place):
    raw = (
        jnp.einsum("qhd,khd->hqk", query_block, key_heads, preferred_element_type=jnp.float32)
        * 0.125
    )
    return jnp.where(allowed_keys(query_tags, query_place, key_tags, key_place)[None], raw, MASKED)


def attend_forward(
    query_heads, key_heads, value_heads, query_tags, query_place, key_tags, key_place
):
    row_count = query_heads.shape[0]
    block_rows = min(row_count, 512)

    def one_block(block_index):
        scores = masked_scores(query_heads, key_heads, query_tags, query_place, key_tags, key_place)
        totals = jax.nn.logsumexp(scores, axis=2)
        probs = jnp.exp(scores - totals[:, :, None]).astype(jnp.bfloat16)
        output = jnp.einsum("hqk,khd->qhd", probs, value_heads, preferred_element_type=jnp.float32)
        return (output, totals)

    outputs, totals = lax.map(one_block, jnp.arange(row_count // block_rows, dtype=jnp.int32))
    return (outputs.reshape(row_count, HEADS * HEAD), totals)


def attend_backward(
    query_heads,
    key_heads,
    value_heads,
    grad_heads,
    deltas,
    totals,
    query_tags,
    query_place,
    key_tags,
    key_place,
):
    row_count = query_heads.shape[0]
    block_rows = min(row_count, 512)

    def one_block(running, block_index):
        key_grad, value_grad = running
        scores = masked_scores(query_heads, key_heads, query_tags, query_place, key_tags, key_place)
        probs = jnp.exp(scores - totals[block_index][:, :, None])
        dprobs = jnp.einsum(
            "qhd,khd->hqk", grad_heads, value_heads, preferred_element_type=jnp.float32
        )
        dscores = (probs * (dprobs - deltas[:, :, None])).astype(jnp.bfloat16)
        query_grad = (
            jnp.einsum("hqk,khd->qhd", dscores, key_heads, preferred_element_type=jnp.float32)
            * 0.125
        )
        key_grad = (
            key_grad
            + jnp.einsum("hqk,qhd->khd", dscores, query_heads, preferred_element_type=jnp.float32)
            * 0.125
        )
        value_grad = value_grad + jnp.einsum(
            "hqk,qhd->khd",
            probs.astype(jnp.bfloat16),
            grad_heads,
            preferred_element_type=jnp.float32,
        )
        return ((key_grad, value_grad), query_grad)

    zeros = jnp.zeros(key_heads.shape, jnp.float32)
    (key_grad, value_grad), query_grads = lax.scan(
        one_block, (zeros, zeros), jnp.arange(row_count // block_rows, dtype=jnp.int32)
    )
    key_count = key_heads.shape[0]
    return (
        query_grads.reshape(row_count, HEADS * HEAD),
        key_grad.reshape(key_count, HEADS * HEAD),
        value_grad.reshape(key_count, HEADS * HEAD),
    )


def clip_window(whole, rows_here, seq_length, own_index):
    neighbours = (WINDOW // 2 + rows_here - 1) // rows_here
    key_span = min((2 * neighbours + 1) * rows_here, seq_length)
    first_key = jnp.clip((own_index - neighbours) * rows_here, 0, seq_length - key_span)
    window = tuple((lax.dynamic_slice_in_dim(member, first_key, key_span, 0) for member in whole))
    return (window, first_key)


def window_keys(items, rows_here, seq_length, own_index):
    whole = (
        lax.all_gather(items[0], "ctx", axis=0, tiled=True),
        lax.all_gather(items[1], "ctx", axis=0, tiled=True),
        lax.all_gather(items[2], "ctx", axis=0, tiled=True),
    )
    return clip_window(whole, rows_here, seq_length, own_index)


def window_keys_again(items, rows_here, seq_length, own_index):
    whole = (
        lax.all_gather(items[0], "ctx", axis=0, tiled=True),
        lax.all_gather(items[1], "ctx", axis=0, tiled=True),
        lax.all_gather(items[2], "ctx", axis=0, tiled=True),
    )
    return clip_window(whole, rows_here, seq_length, own_index)


def return_key_grads(key_grad, value_grad, rows_here, first_key):
    width = key_grad.shape[1]
    joined = jnp.concatenate([key_grad, value_grad], axis=1)
    key_span = joined.shape[0]
    count = rows_here * lax.axis_size("ctx")
    padding = jnp.zeros((count, 2 * width), jnp.float32)
    padded = jnp.concatenate([padding, joined, padding], axis=0)
    offset = jnp.clip(jnp.int32(0) - first_key + count, 0, key_span + count)
    summed = lax.psum_scatter(
        lax.dynamic_slice_in_dim(padded, offset, count, 0), "ctx", scatter_dimension=0, tiled=True
    )
    return (summed[:, :width], summed[:, width:])


def general_body(
    tokens,
    w_qkv,
    b_query,
    b_value,
    w_out,
    b_out,
    ln1_gain,
    ln1_bias,
    w_up,
    b_up,
    w_down,
    b_down,
    ln2_gain,
    ln2_bias,
    segment_ids,
    pad_mask,
    cotangent,
):
    weight_shards = (
        w_qkv,
        b_query,
        b_value,
        w_out,
        b_out,
        ln1_gain,
        ln1_bias,
        w_up,
        b_up,
        w_down,
        b_down,
        ln2_gain,
        ln2_bias,
    )
    gathered = (
        lax.all_gather(weight_shards[0], ("dp", "ctx"), axis=0, tiled=True),
        lax.all_gather(weight_shards[1], ("dp", "ctx"), axis=0, tiled=True),
        lax.all_gather(weight_shards[2], ("dp", "ctx"), axis=0, tiled=True),
        lax.all_gather(weight_shards[3], ("dp", "ctx"), axis=0, tiled=True),
        lax.all_gather(weight_shards[4], ("dp", "ctx"), axis=0, tiled=True),
        lax.all_gather(weight_shards[5], ("dp", "ctx"), axis=0, tiled=True),
        lax.all_gather(weight_shards[6], ("dp", "ctx"), axis=0, tiled=True),
        lax.all_gather(weight_shards[7], ("dp", "ctx"), axis=0, tiled=True),
        lax.all_gather(weight_shards[8], ("dp", "ctx"), axis=0, tiled=True),
        lax.all_gather(weight_shards[9], ("dp", "ctx"), axis=0, tiled=True),
        lax.all_gather(weight_shards[10], ("dp", "ctx"), axis=0, tiled=True),
        lax.all_gather(weight_shards[11], ("dp", "ctx"), axis=0, tiled=True),
        lax.all_gather(weight_shards[12], ("dp", "ctx"), axis=0, tiled=True),
    )
    (
        full_qkv,
        full_bquery,
        full_bvalue,
        full_out,
        full_bout,
        full_gain_one,
        full_bias_one,
        full_up,
        full_bup,
        full_down,
        full_bdown,
        full_gain_two,
        full_bias_two,
    ) = gathered
    rows_here = tokens.shape[1]
    seq_length = rows_here * lax.axis_size("ctx")
    own_index = lax.axis_index("ctx")
    inputs = tokens[0]
    inputs_wide = inputs.astype(jnp.float32)
    model_width = inputs.shape[1]
    token_tags = 2 * (segment_ids[0] + 1) + pad_mask[0]
    query_place = own_index * rows_here + jnp.arange(rows_here, dtype=jnp.int32)
    mixed = matmul(inputs, full_qkv)
    queries = (mixed[:, :model_width] + full_bquery.astype(jnp.float32)).astype(jnp.bfloat16)
    keys = mixed[:, model_width : 2 * model_width].astype(jnp.bfloat16)
    values = (mixed[:, 2 * model_width :] + full_bvalue.astype(jnp.float32)).astype(jnp.bfloat16)
    (key_window, value_window, tag_window), first_key = window_keys(
        (keys, values, token_tags), rows_here, seq_length, own_index
    )
    key_place = first_key + jnp.arange(key_window.shape[0], dtype=jnp.int32)
    attended, totals = attend_forward(
        split_heads(queries),
        split_heads(key_window),
        split_heads(value_window),
        token_tags,
        query_place,
        tag_window,
        key_place,
    )
    attended_low = attended.astype(jnp.bfloat16)
    first = inputs_wide + matmul(attended_low, full_out) + full_bout.astype(jnp.float32)
    normed, first_pull = jax.vjp(
        layer_norm, first, full_gain_one.astype(jnp.float32), full_bias_one.astype(jnp.float32)
    )
    normed_low = normed.astype(jnp.bfloat16)
    hidden = matmul(normed_low, full_up) + full_bup.astype(jnp.float32)
    active, gelu_pull = jax.vjp(partial(jax.nn.gelu, approximate=False), hidden)
    active_low = active.astype(jnp.bfloat16)
    second = normed + matmul(active_low, full_down) + full_bdown.astype(jnp.float32)
    result, second_pull = jax.vjp(
        layer_norm, second, full_gain_two.astype(jnp.float32), full_bias_two.astype(jnp.float32)
    )
    gathered = (
        lax.all_gather(weight_shards[0], ("dp", "ctx"), axis=0, tiled=True),
        lax.all_gather(weight_shards[1], ("dp", "ctx"), axis=0, tiled=True),
        lax.all_gather(weight_shards[2], ("dp", "ctx"), axis=0, tiled=True),
        lax.all_gather(weight_shards[3], ("dp", "ctx"), axis=0, tiled=True),
        lax.all_gather(weight_shards[4], ("dp", "ctx"), axis=0, tiled=True),
        lax.all_gather(weight_shards[5], ("dp", "ctx"), axis=0, tiled=True),
        lax.all_gather(weight_shards[6], ("dp", "ctx"), axis=0, tiled=True),
        lax.all_gather(weight_shards[7], ("dp", "ctx"), axis=0, tiled=True),
        lax.all_gather(weight_shards[8], ("dp", "ctx"), axis=0, tiled=True),
        lax.all_gather(weight_shards[9], ("dp", "ctx"), axis=0, tiled=True),
        lax.all_gather(weight_shards[10], ("dp", "ctx"), axis=0, tiled=True),
        lax.all_gather(weight_shards[11], ("dp", "ctx"), axis=0, tiled=True),
        lax.all_gather(weight_shards[12], ("dp", "ctx"), axis=0, tiled=True),
    )
    back_qkv = gathered[0]
    back_out = gathered[3]
    back_up = gathered[7]
    back_down = gathered[9]
    grad_second, grad_gain_two, grad_bias_two = second_pull(cotangent[0].astype(jnp.float32))
    grad_outcome = grad_second.astype(jnp.bfloat16)
    grad_wdown = rows_product(active_low, grad_outcome)
    grad_bdown = jnp.sum(grad_outcome.astype(jnp.float32), axis=0)
    (grad_active,) = gelu_pull(cols_product(grad_outcome, back_down))
    grad_hidden = grad_active.astype(jnp.bfloat16)
    grad_wup = rows_product(normed_low, grad_hidden)
    grad_bup = jnp.sum(grad_hidden.astype(jnp.float32), axis=0)
    grad_normed = grad_second + cols_product(grad_hidden, back_up)
    grad_first, grad_gain_one, grad_bias_one = first_pull(grad_normed)
    grad_branch = grad_first.astype(jnp.bfloat16)
    grad_wout = rows_product(attended_low, grad_branch)
    grad_bout = jnp.sum(grad_branch.astype(jnp.float32), axis=0)
    grad_attended = cols_product(grad_branch, back_out).astype(jnp.bfloat16)
    deltas = jnp.sum(
        (grad_attended.astype(jnp.float32) * attended).reshape(rows_here, HEADS, HEAD), axis=2
    ).T
    (key_again, value_again, tag_again), first_again = window_keys_again(
        (keys, values, token_tags), rows_here, seq_length, own_index
    )
    place_again = first_again + jnp.arange(key_again.shape[0], dtype=jnp.int32)
    grad_queries, key_grad, value_grad = attend_backward(
        split_heads(queries),
        split_heads(key_again),
        split_heads(value_again),
        split_heads(grad_attended),
        deltas,
        totals,
        token_tags,
        query_place,
        tag_again,
        place_again,
    )
    key_total, value_total = return_key_grads(key_grad, value_grad, rows_here, first_again)
    grad_query_low = grad_queries.astype(jnp.bfloat16)
    grad_value_low = value_total.astype(jnp.bfloat16)
    grad_mixed = jnp.concatenate(
        [grad_query_low, key_total.astype(jnp.bfloat16), grad_value_low], axis=1
    )
    grad_wqkv = rows_product(inputs, grad_mixed)
    grad_bquery = jnp.sum(grad_query_low.astype(jnp.float32), axis=0)
    grad_bvalue = jnp.sum(grad_value_low.astype(jnp.float32), axis=0)
    grad_inputs = grad_first + cols_product(grad_mixed, back_qkv)
    summed = (
        lax.psum_scatter(grad_wqkv, ("dp", "ctx"), scatter_dimension=0, tiled=True),
        lax.psum_scatter(grad_bquery, ("dp", "ctx"), scatter_dimension=0, tiled=True),
        lax.psum_scatter(grad_bvalue, ("dp", "ctx"), scatter_dimension=0, tiled=True),
        lax.psum_scatter(grad_wout, ("dp", "ctx"), scatter_dimension=0, tiled=True),
        lax.psum_scatter(grad_bout, ("dp", "ctx"), scatter_dimension=0, tiled=True),
        lax.psum_scatter(grad_gain_one, ("dp", "ctx"), scatter_dimension=0, tiled=True),
        lax.psum_scatter(grad_bias_one, ("dp", "ctx"), scatter_dimension=0, tiled=True),
        lax.psum_scatter(grad_wup, ("dp", "ctx"), scatter_dimension=0, tiled=True),
        lax.psum_scatter(grad_bup, ("dp", "ctx"), scatter_dimension=0, tiled=True),
        lax.psum_scatter(grad_wdown, ("dp", "ctx"), scatter_dimension=0, tiled=True),
        lax.psum_scatter(grad_bdown, ("dp", "ctx"), scatter_dimension=0, tiled=True),
        lax.psum_scatter(grad_gain_two, ("dp", "ctx"), scatter_dimension=0, tiled=True),
        lax.psum_scatter(grad_bias_two, ("dp", "ctx"), scatter_dimension=0, tiled=True),
    )
    return (
        result.astype(jnp.bfloat16)[None],
        grad_inputs.astype(jnp.bfloat16)[None],
        summed[0],
        summed[1],
        summed[2],
        summed[3],
        summed[4],
        summed[5],
        summed[6],
        summed[7],
        summed[8],
        summed[9],
        summed[10],
        summed[11],
        summed[12],
    )


GROUP = ("y", "core", "x")
CTX = ("z", "x")
DP = ("y", "core")
EVERY = ("y", "core", "z", "x")
bf16, f32 = jnp.bfloat16, jnp.float32


def swap(member, axes, code):
    count = 1
    for axis in axes:
        count *= lax.axis_size(axis)
    return lax.ppermute(member, axes, [(place, place ^ code) for place in range(count)])


def after(member, *events):
    return lax.optimization_barrier((member,) + events)[0]


def like(shape, kind):
    return jax.ShapeDtypeStruct(shape, kind)


def staged(kernel, n_in, n_out, keep, place, *refs):
    given, refs = refs[:n_in], refs[n_in:]
    results, refs = refs[:n_out], refs[n_out:]
    held, refs = refs[:n_in], refs[n_in:]
    if keep:
        out, arrived, refs = results, refs[0], refs[1:]
    else:
        out, (arrived, left), refs = refs[:n_out], refs[n_out : n_out + 2], refs[n_out + 2 :]
    copies = [
        pltpu.make_async_copy(ref, held[i], arrived.at[i]) for i, ref in enumerate(given)
    ]
    for copy in copies:
        copy.start()
    for copy in copies:
        copy.wait()
    kernel(place, *held, *out, *refs)
    if keep:
        return
    copies = [pltpu.make_async_copy(out[i], ref, left.at[i]) for i, ref in enumerate(results)]
    for copy in copies:
        copy.start()
    for copy in copies:
        copy.wait()


def local(kernel, outs, place, *operands, scratch=(), far=False, keep=False, cost=0):
    size = sum(math.prod(v.shape) * jnp.dtype(v.dtype).itemsize for v in operands)
    size += sum(math.prod(v.shape) * jnp.dtype(v.dtype).itemsize for v in outs)
    size += sum(math.prod(v.shape) * jnp.dtype(v.dtype).itemsize for v in scratch)
    near = pl.BlockSpec(memory_space=pltpu.VMEM)
    whole = pl.BlockSpec(memory_space=pltpu.HBM) if far else near
    if far:
        kernel = partial(staged, kernel, len(operands), len(outs), keep)
        held = [pltpu.VMEM(v.shape, v.dtype) for v in (operands if keep else (*operands, *outs))]
        signals = [pltpu.SemaphoreType.DMA((len(operands),))]
        if not keep:
            signals.append(pltpu.SemaphoreType.DMA((len(outs),)))
            outs = [pltpu.HBM(v.shape, v.dtype) for v in outs]
        scratch = held + signals + list(scratch)
        operands = [pltpu.with_memory_space_constraint(v, pltpu.HBM) for v in operands]
    return pl.pallas_call(
        kernel,
        out_shape=list(outs),
        in_specs=[pl.BlockSpec(memory_space=pltpu.SMEM)] + [whole] * len(operands),
        out_specs=[near if keep else whole] * len(outs),
        scratch_shapes=list(scratch),
        cost_estimate=pl.CostEstimate(flops=cost * 10**9, bytes_accessed=0, transcendentals=0),
        compiler_params=pltpu.CompilerParams(vmem_limit_bytes=size + (6 << 20)),
    )(place, *operands)


def pair_product(left, right):
    return lax.dot_general(
        left, right, (((0,), (0,)), ((), ())), preferred_element_type=jnp.float32
    )


def plane_gather(block):
    return [block] + [swap(block, ("y", "x"), code) for code in range(1, 4)]


def group_gather(block):
    plane = plane_gather(block)
    return plane + [swap(member, ("core",), 1) for member in plane]


def merge_kernel(place, near, far, own, *sent):
    rows = own.shape[0]
    for code in range(4):
        part = pl.ds(code * rows, rows)
        total = near[part, :].astype(f32) + far[part, :].astype(f32)
        if code == 0:
            own[...] = total
        else:
            sent[code - 1][...] = total.astype(bf16)


def group_scatter(near, far, place, event=None):
    rows, width = near.shape[0] // 4, near.shape[1]
    crossed = swap(far, ("core",), 1)
    if event is not None:
        crossed = after(crossed, event)
    outs = [like((rows, width), f32)] + [like((rows, width), bf16)] * 3
    own, *sent = local(merge_kernel, outs, place, near, crossed)
    parts = [own] + [swap(sent[code - 1], ("y", "x"), code) for code in range(1, 4)]
    return parts


def sum_over_z(near, far, event):
    total = near.astype(f32) + after(far, event).astype(f32)
    return total[0] + swap(total[1].astype(bf16), ("z",), 2).astype(f32)


def ctx_gather(block):
    two, one = swap(block, ("z",), 2), swap(block, ("z",), 1)
    line = [block, one, two, swap(two, ("z",), 1)]
    return [piece for member in line for piece in (member, swap(member, ("x",), 1))]


def pack_kernel(place, w_qkv, w_up, *refs):
    vectors, (b_up, segments, pads, qkv_ref, up_ref) = refs[:8], refs[8:]
    groups, _, wide = qkv_ref.shape
    shard, cols = w_qkv.shape[0], wide // 3
    tags = (2 * (segments[...] + 1) + pads[...]).astype(f32)
    lone = jnp.concatenate([v[...].astype(f32) for v in vectors], axis=0)
    lone = jnp.concatenate([lone, jnp.zeros((8, 128 - shard), f32)], axis=1)
    small = jnp.concatenate([lone, b_up[...].astype(f32), tags, jnp.zeros((6, 128), f32)], axis=0)
    small = jnp.concatenate([small, jnp.zeros((16, wide - 128), f32)], axis=1).astype(bf16)
    for c in range(groups):
        for kind in range(3):
            at = (kind * groups + c) * cols
            qkv_ref[c, :shard, kind * cols : (kind + 1) * cols] = w_qkv[:, at : at + cols]
        qkv_ref[c, shard:, :] = small
    units = b_up.shape[1]
    own = place[4] * 4 + place[5] * 2 + place[6]
    for g in range(8):
        for z in range(4):
            at = ((g // 2 * 4 + z) * 2 + g % 2) * units
            up_ref[own ^ g, :, z * units : (z + 1) * units] = w_up[:, at : at + units]


def order_up_kernel(place, *refs):
    up_refs, up_out = refs[:4], refs[4]
    rows = up_out.shape[0] // 32
    own, own_z = place[4] * 4 + place[5] * 2 + place[6], place[3]
    for j in range(8):
        group = own ^ j
        for z in range(4):
            at = ((group >> 1) * 4 + (own_z ^ z)) * 2 + (group & 1)
            up_out[pl.ds(at * rows, rows), :] = up_refs[z][pl.ds(j * rows, rows), :]


def allowed_here(query_tags, query_place, key_tags, key_place):
    same_doc = (query_tags >> 1) == (key_tags >> 1)
    distance = jnp.abs(query_place - key_place)
    usable = ((key_tags & 1) == 1) | (distance == 0)
    return same_doc & (distance <= WINDOW // 2) & usable


def places(own_ctx, rows, shape, axis, start=0):
    index = lax.broadcasted_iota(jnp.int32, shape, axis) + start
    return ((index // rows) ^ own_ctx) * rows + index % rows


def attend_kernel(
    place, *refs, n_blocks, rows, cols
):
    blocks, refs = refs[:n_blocks], refs[n_blocks:]
    pieces, refs = refs[:4], refs[4:]
    bias, tags_row, q_ref, k_ref, v_ref, att_ref, msg_ref, lse_ref, qkv_ref = refs
    own_dp, own_ctx = place[1], place[2]
    shard = 32
    for m, piece in enumerate(pieces):
        for c in range(n_blocks):
            at = ((own_dp ^ m) * n_blocks + c) * shard
            qkv_ref[pl.ds(at, shard), :] = piece[c, :shard, :]
    for j, block in enumerate(blocks):
        part = pl.ds(j * rows, rows)
        mixed = matmul(block[...], qkv_ref[...]) + bias[...]
        q_ref[part, :] = mixed[:, :cols].astype(bf16)
        k_ref[part, :] = mixed[:, cols : 2 * cols].astype(bf16)
        v_ref[part, :] = mixed[:, 2 * cols :].astype(bf16)
    length = n_blocks * rows
    chunk = 2 * rows

    def step(index, carry):
        part = pl.ds(index * chunk, chunk)
        allowed = allowed_here(
            jnp.broadcast_to(tags_row[:, part], (128, chunk)).T[:, :1],
            places(own_ctx, rows, (chunk, 1), 0, index * chunk),
            tags_row[...],
            places(own_ctx, rows, (1, length), 1),
        )
        found = []
        for head in range(cols // HEAD):
            lanes = slice(head * HEAD, (head + 1) * HEAD)
            scores = cols_product(q_ref[part, lanes], k_ref[:, lanes]) * 0.125
            scores = jnp.where(allowed, scores, MASKED)
            top = jnp.max(scores, axis=1, keepdims=True)
            weights = jnp.exp(scores - top)
            mass = jnp.sum(weights, axis=1, keepdims=True)
            found.append(matmul(weights.astype(bf16), v_ref[:, lanes]) / mass)
            total = top + jnp.log(mass)
            lse_ref[pl.ds(head, 1), part] = jnp.broadcast_to(total, (chunk, 128)).T[:1, :]
        attended = jnp.concatenate(found, axis=1)
        att_ref[part, :] = attended
        for half in range(2):
            at = ((index * 2 + half) ^ own_ctx) * rows
            msg_ref[pl.ds(at, rows), :] = attended[half * rows : (half + 1) * rows].astype(bf16)
        return carry

    lax.fori_loop(0, length // chunk, step, 0)


def branch_kernel(place, moved, w_out, inputs, vectors, normed_ref, low_ref, hat_ref, rate_ref):
    groups, rows, cols = moved.shape
    total = inputs[...].astype(f32) + vectors[2:3, :]
    for c in range(groups):
        total = total + matmul(moved[c], w_out[pl.ds(c * cols, cols), :])
    centred = total - jnp.mean(total, axis=1, keepdims=True)
    rate = lax.rsqrt(jnp.mean(centred * centred, axis=1, keepdims=True) + EPSILON)
    hat = centred * rate
    normed = hat * vectors[3:4, :] + vectors[4:5, :]
    normed_ref[...] = normed
    low_ref[...] = normed.astype(bf16)
    hat_ref[...] = hat
    rate_ref[...] = jnp.broadcast_to(rate, rate_ref.shape)


def forward_kernel(place, *refs):
    blocks = refs[:8]
    up, bias, down, hidden_ref, active_ref, near, far = refs[8:]
    rows = blocks[0].shape[0]
    for pair in range(4):
        lines = jnp.concatenate([blocks[2 * pair][...], blocks[2 * pair + 1][...]], axis=0)
        part = pl.ds(pair * 2 * rows, 2 * rows)
        hidden = matmul(lines, up[...]) + bias[...]
        hidden_ref[part, :] = hidden
        active = (0.5 * hidden * (1 + lax.erf(hidden * 0.7071067811865476))).astype(bf16)
        active_ref[part, :] = active
        target = near if pair < 2 else far
        target[pl.ds(pair % 2 * 2 * rows, 2 * rows), :] = matmul(active, down[...]).astype(bf16)


def second_kernel(
    place, normed, own, p1, p2, p3, vectors, cotangent, result_ref, grad_ref, low_ref, sums_ref
):
    second = normed[...] + own[...] + p1[...].astype(f32) + p2[...].astype(f32)
    second = second + p3[...].astype(f32) + vectors[5:6, :]
    centred = second - jnp.mean(second, axis=1, keepdims=True)
    rate = lax.rsqrt(jnp.mean(centred * centred, axis=1, keepdims=True) + EPSILON)
    hat = centred * rate
    gain = vectors[6:7, :]
    result_ref[...] = (hat * gain + vectors[7:8, :]).astype(bf16)
    grad = cotangent[...].astype(f32)
    scaled = grad * gain
    mean_scaled = jnp.mean(scaled, axis=1, keepdims=True)
    mean_hat = jnp.mean(scaled * hat, axis=1, keepdims=True)
    grad_second = rate * (scaled - mean_scaled - hat * mean_hat)
    grad_ref[...] = grad_second
    low = grad_second.astype(bf16)
    low_ref[...] = low
    sums_ref[0:1, :] = jnp.sum(low.astype(f32), axis=0, keepdims=True)
    sums_ref[1:2, :] = jnp.sum(grad * hat, axis=0, keepdims=True)
    sums_ref[2:3, :] = jnp.sum(grad, axis=0, keepdims=True)


def backward_kernel(place, *refs):
    blocks = refs[:8]
    up, down, slope, grad_ref, near, far = refs[8:]
    rows = blocks[0].shape[0]
    for pair in range(4):
        lines = jnp.concatenate([blocks[2 * pair][...], blocks[2 * pair + 1][...]], axis=0)
        part = pl.ds(pair * 2 * rows, 2 * rows)
        grad = (slope[part, :] * cols_product(lines, down[...])).astype(bf16)
        grad_ref[part, :] = grad
        target = near if pair < 2 else far
        target[pl.ds(pair % 2 * 2 * rows, 2 * rows), :] = cols_product(grad, up[...]).astype(bf16)


def down_grad_kernel(place, *refs):
    grads, (active, grad_hidden, parts, lines) = refs[:8], refs[8:]
    rows, width = grads[0].shape
    shard = active.shape[1] // 4
    for j in range(8):
        lines[pl.ds(j * rows, rows), :] = grads[j][...]
    total = jnp.sum(grad_hidden[...].astype(f32), axis=0, keepdims=True)
    for z in range(4):
        part = slice(z * shard, (z + 1) * shard)
        parts[z, :shard, :] = pair_product(active[:, part], lines[...]).astype(bf16)
        parts[z, shard:, :shard] = jnp.broadcast_to(total[:, part], (16, shard)).astype(bf16)
        parts[z, shard:, shard:] = jnp.zeros((16, width - shard), bf16)


def up_grad_kernel(place, *refs):
    normed, (grad_hidden, parts, lines) = refs[:8], refs[8:]
    rows = normed[0].shape[0]
    for j in range(8):
        lines[pl.ds(j * rows, rows), :] = normed[j][...]
    for quarter in range(4):
        span = 8 * 32
        part = slice(quarter * span, (quarter + 1) * span)
        found = pair_product(lines[:, part], grad_hidden[...]).astype(bf16)
        for z in range(4):
            for x in range(2):
                piece = found[(z * 2 + x) * 32 : (z * 2 + x + 1) * 32]
                parts[z, pl.ds((quarter * 2 + x) * 32, 32), :] = piece


def first_kernel(
    place, grad_second, own, p1, p2, p3, vectors, hat_ref, rate_ref, w_out, grad_ref, low_ref, msg_ref,
    sums_ref,
):
    grad = grad_second[...] + own[...] + p1[...].astype(f32) + p2[...].astype(f32)
    grad = grad + p3[...].astype(f32)
    hat = hat_ref[...]
    scaled = grad * vectors[3:4, :]
    mean_scaled = jnp.mean(scaled, axis=1, keepdims=True)
    mean_hat = jnp.mean(scaled * hat, axis=1, keepdims=True)
    grad_first = rate_ref[:, :1] * (scaled - mean_scaled - hat * mean_hat)
    grad_ref[...] = grad_first
    low = grad_first.astype(bf16)
    low_ref[...] = low
    groups, rows, cols = msg_ref.shape
    for c in range(groups):
        msg_ref[c] = cols_product(low, w_out[pl.ds(c * cols, cols), :]).astype(bf16)
    sums_ref[0:1, :] = jnp.sum(low.astype(f32), axis=0, keepdims=True)
    sums_ref[1:2, :] = jnp.sum(grad * hat, axis=0, keepdims=True)
    sums_ref[2:3, :] = jnp.sum(grad, axis=0, keepdims=True)


def out_grad_kernel(place, moved, low, sums_one, sums_two, near, far, parts):
    groups, rows, cols = moved.shape
    high, width = parts.shape[1:]
    own_y, own_core, own_x = place[4], place[5], place[6]
    sums = [sums_one[0:3, :], sums_two[0:3, :], jnp.zeros((high - rows - 6, width), f32)]
    sums = jnp.concatenate(sums, axis=0).astype(bf16)
    for c in range(groups):
        found = pair_product(moved[c], low[...]).astype(bf16)
        for m in range(4):
            y, core, z, x = c // 4, c // 2 % 2, c % 2 * 2 + m // 2, m % 2
            code = (core ^ own_core) * 4 + (y ^ own_y) * 2 + (x ^ own_x)
            parts[code, pl.ds(z * 32, 32), :] = found[m * 32 : (m + 1) * 32]
            lanes = slice((c * 4 + m) * 32, (c * 4 + m + 1) * 32)
            parts[code, rows:, z * 32 : (z + 1) * 32] = sums[:, lanes]
    for code in range(4):
        near[pl.ds(code * high, high), :] = parts[code]
        far[pl.ds(code * high, high), :] = parts[code + 4]


def out_line_kernel(place, own, p1, p2, p3, near, far, parts):
    total = own[...] + p1[...].astype(f32) + p2[...].astype(f32) + p3[...].astype(f32)
    own_z = place[3]
    parts[...] = jnp.zeros(parts.shape, f32)
    for z in range(4):
        at = own_z ^ z
        parts[at, :32, :] = total[z * 32 : (z + 1) * 32]
        parts[at, 32:, :32] = total[128:, z * 32 : (z + 1) * 32]
    for half in range(2):
        near[half], far[half] = parts[2 * half], parts[2 * half + 1].astype(bf16)


def attend_grad_kernel(
    place, *refs,
):
    moved, q_ref, k_ref, v_ref, att_ref, lse_ref, tags_row, *refs = refs
    mixed_ref, key_grad, value_grad, back = refs
    groups, rows, cols = moved.shape
    length = groups * rows
    own_ctx = place[2]
    for j in range(groups):
        back[pl.ds(j * rows, rows), :] = moved[own_ctx ^ j]
    key_grad[...] = jnp.zeros(key_grad.shape, f32)
    value_grad[...] = jnp.zeros(value_grad.shape, f32)
    chunk = 2 * rows
    tags_col = jnp.broadcast_to(tags_row[...], (128, length)).T[:, :1]

    def step(index, carry):
        part = pl.ds(index * chunk, chunk)
        allowed = allowed_here(
            tags_row[:, part],
            places(own_ctx, rows, (1, chunk), 1, index * chunk),
            tags_col,
            places(own_ctx, rows, (length, 1), 0),
        )
        weighted = (back[part, :].astype(f32) * att_ref[part, :]).T
        found = []
        for head in range(cols // HEAD):
            lanes = slice(head * HEAD, (head + 1) * HEAD)
            delta = jnp.sum(weighted[lanes, :], axis=0, keepdims=True)
            scores = cols_product(k_ref[:, lanes], q_ref[part, lanes]) * 0.125
            probs = jnp.where(allowed, jnp.exp(scores - lse_ref[pl.ds(head, 1), part]), 0.0)
            grads = cols_product(v_ref[:, lanes], back[part, lanes])
            grads = (probs * (grads - delta)).astype(bf16)
            value_grad[:, lanes] += matmul(probs.astype(bf16), back[part, lanes])
            key_grad[:, lanes] += matmul(grads, q_ref[part, lanes])
            found.append(pair_product(grads, k_ref[:, lanes]) * 0.125)
        mixed_ref[part, :cols] = jnp.concatenate(found, axis=1).astype(bf16)
        return carry

    lax.fori_loop(0, length // chunk, step, 0)
    mixed_ref[:, cols : 2 * cols] = (key_grad[...] * 0.125).astype(bf16)
    mixed_ref[:, 2 * cols :] = value_grad[...].astype(bf16)


def leave_kernel(place, *refs):
    mixed_ref, qkv_ref, even_near, even_far, odd_near, odd_far = refs
    messages = ((even_near, even_far), (odd_near, odd_far))
    groups, rows = 8, mixed_ref.shape[0] // 8
    for j in range(groups):
        part = cols_product(mixed_ref[pl.ds(j * rows, rows), :], qkv_ref[...])
        target = messages[j // 2 % 2][j % 2]
        target[pl.ds(j // 4 * rows, rows), :] = part.astype(bf16)


def qkv_grad_kernel(place, *refs):
    blocks, (mixed_ref, near, far, lines) = refs[:8], refs[8:]
    groups, rows = 8, blocks[0].shape[0]
    cols = mixed_ref.shape[1] // 3
    own_dp = place[1]
    for j in range(groups):
        lines[pl.ds(j * rows, rows), :] = blocks[j][...]
    sums = jnp.sum(mixed_ref[...].astype(f32), axis=0, keepdims=True)
    sums = jnp.broadcast_to(sums, (16, 3 * cols)).astype(bf16)
    span = lines.shape[1] // 4
    for ky in range(2):
        for kc in range(2):
            start = pl.multiple_of((own_dp ^ (ky * 2 + kc)) * span, span)
            found = pair_product(lines[:, pl.ds(start, span)], mixed_ref[...]).astype(bf16)
            target = far if kc else near
            target[ky, :span, :] = found
            target[ky, span:, :] = sums


def dp_sum(near, far):
    crossed = swap(far, ("core",), 1).astype(f32)
    total = near.astype(f32) + crossed
    return total[0] + swap(total[1].astype(bf16), ("y",), 1).astype(f32)


def up_final_kernel(place, moved, out):
    groups, shard, wide = moved.shape
    units = wide // 4
    for g in range(groups):
        for z in range(4):
            at = ((g // 2 * 4 + z) * 2 + g % 2) * units
            out[:, at : at + units] = moved[g, :, z * units : (z + 1) * units].astype(f32)


def qkv_final_kernel(place, moved, out):
    groups, _, wide = moved.shape
    shard, cols = out.shape[0], wide // 3
    for c in range(groups):
        for kind in range(3):
            at = (kind * groups + c) * cols
            out[:, at : at + cols] = moved[c, :shard, kind * cols : (kind + 1) * cols].astype(f32)


def heads_body(
    tokens, w_qkv, b_query, b_value, w_out, b_out, ln1_gain, ln1_bias, w_up, b_up, w_down, b_down,
    ln2_gain, ln2_bias, segment_ids, pad_mask, cotangent,
):
    inputs = tokens[0]
    rows, width = inputs.shape
    n_ctx = lax.axis_size(CTX)
    n_dp = lax.axis_size(DP)
    n_z = lax.axis_size("z")
    length = rows * n_ctx
    cols = width // n_ctx
    shard = w_qkv.shape[0]
    units = w_down.shape[0]
    wide = n_z * units
    own_ctx = lax.axis_index(CTX)
    own_dp = lax.axis_index(DP)
    own = lax.axis_index(EVERY)
    place = jnp.stack(
        [own, own_dp, own_ctx, lax.axis_index("z")] + [lax.axis_index(a) for a in GROUP]
    ).astype(jnp.int32)

    vectors = (b_query, b_value, b_out, ln1_gain, ln1_bias, b_down, ln2_gain, ln2_bias)
    qkv_parts, up_parts = local(
        pack_kernel,
        [like((n_ctx, shard + 16, 3 * cols), bf16), like((8, shard, wide), bf16)],
        place, w_qkv, w_up, *[v[None] for v in vectors], b_up[None], segment_ids, pad_mask,
        far=True,
    )
    blocks = ctx_gather(inputs)
    qkv = after(qkv_parts, blocks[1], blocks[2], blocks[4])
    qkv = lax.all_to_all(qkv, CTX, 0, 0, tiled=True)
    qkv_y = swap(after(qkv, blocks[3], blocks[5]), ("y",), 1)
    qkv_c, qkv_y = after(qkv, blocks[7]), after(qkv_y, blocks[7])
    pieces = [qkv, swap(qkv_c, ("core",), 1), qkv_y, swap(qkv_y, ("core",), 1)]
    up = after(up_parts, blocks[6])
    up = [up[:1]] + [swap(up[j : j + 1], GROUP, j) for j in range(1, 8)]
    small = jnp.stack([piece[:, shard : shard + 10, :128] for piece in pieces])
    small = jnp.take(small, own_dp ^ jnp.arange(n_dp), axis=0).reshape(n_dp * n_ctx, 10, 128)
    vectors = small[:, :8, :shard].transpose(1, 0, 2).reshape(8, width).astype(f32)
    bias_up = small[:, 8].reshape(n_dp, n_z, 2, units)
    bias_up = lax.dynamic_slice(bias_up, (own_dp, 0, lax.axis_index("x"), 0), (1, n_z, 1, units))
    bias_up = bias_up.reshape(1, wide).astype(f32)
    tags = lax.dynamic_slice(small[:, 9], (own_dp * n_ctx, 0), (n_ctx, rows)).astype(jnp.int32)
    tags_row = jnp.take(tags, own_ctx ^ jnp.arange(n_ctx), axis=0).reshape(1, length)
    bias = lax.dynamic_slice(vectors, (0, own_ctx * cols), (2, cols))
    bias = jnp.concatenate([bias[:1], jnp.zeros((1, cols), f32), bias[1:]], axis=1)

    full_out = lax.all_gather(w_out, EVERY, axis=0, tiled=True)
    down = lax.all_gather(after(w_down, full_out), "z", axis=0, tiled=True)
    queries, keys, values, attended, message, totals, full_qkv = local(
        partial(attend_kernel, n_blocks=n_ctx, rows=rows, cols=cols),
        [like((length, cols), bf16)] * 3
        + [
            like((length, cols), f32),
            like((length, cols), bf16),
            like((8, length), f32),
            like((width, 3 * cols), bf16),
        ],
        place, *blocks, *pieces, bias, tags_row, far=True, cost=10,
    )
    up = jnp.concatenate([after(up[0], message)] + up[1:]).reshape(8 * shard, wide)
    up_z = swap(up, ("z",), 2)
    up_lines = [up, swap(up, ("z",), 1), up_z, swap(up_z, ("z",), 1)]
    moved = lax.all_to_all(message, CTX, 0, 0, tiled=True).reshape(n_ctx, rows, cols)
    normed, normed_low, hat, rate = local(
        branch_kernel,
        [like((rows, width), f32), like((rows, width), bf16), like((rows, width), f32)]
        + [like((rows, 128), f32)],
        place, moved, full_out, inputs, vectors,
    )
    normed_all = group_gather(normed_low)
    (full_up,) = local(
        order_up_kernel, [like((width, wide), bf16)], place, after(up_lines[0], normed_all[1]),
        *up_lines[1:], far=True, keep=True,
    )
    hidden, active, near, far = local(
        forward_kernel,
        [like((8 * rows, wide), f32), like((8 * rows, wide), bf16)]
        + [like((4 * rows, width), bf16)] * 2,
        place, *normed_all, full_up, bias_up, down,
    )
    parts = group_scatter(near, far, place)
    hidden = after(hidden, parts[1])
    result, grad_second, grad_z, sums_two = local(
        second_kernel,
        [like((rows, width), bf16), like((rows, width), f32), like((rows, width), bf16)]
        + [like((8, width), f32)],
        place, normed, *parts, vectors, cotangent[0],
    )

    slope = 0.5 * (1 + lax.erf(hidden * 0.7071067811865476)) + hidden * (
        jnp.exp(-0.5 * hidden * hidden) * 0.3989422804014327
    )
    grad_z_all = group_gather(grad_z)
    grad_hidden, near, far = local(
        backward_kernel,
        [like((8 * rows, wide), bf16)] + [like((4 * rows, width), bf16)] * 2,
        place, *grad_z_all, full_up, down, slope,
    )
    (down_parts,) = local(
        down_grad_kernel, [like((n_z, units + 16, width), bf16)],
        place, *grad_z_all, active, grad_hidden, far=True,
        scratch=[pltpu.VMEM((8 * rows, width), bf16)],
    )
    parts = group_scatter(near, far, place, down_parts)
    down_sum = lax.psum_scatter(
        down_parts.reshape(-1, width), "z", scatter_dimension=0, tiled=True
    )
    (up_parts,) = local(
        up_grad_kernel, [like((n_z, 8 * shard, wide), bf16)],
        place, *normed_all, after(grad_hidden, parts[1]), far=True,
        scratch=[pltpu.VMEM((8 * rows, width), bf16)],
    )
    up_sum = lax.psum_scatter(up_parts.reshape(-1, wide), "z", scatter_dimension=0, tiled=True)
    grad_first, grad_branch, message, sums_one = local(
        first_kernel,
        [like((rows, width), f32), like((rows, width), bf16), like((n_ctx, rows, cols), bf16)]
        + [like((8, width), f32)],
        place, after(grad_second, up_parts), *parts, vectors, hat, rate, full_out,
    )
    grad_moved = lax.all_to_all(message, CTX, 0, 0, tiled=True)
    high = rows + 16
    near, far = local(
        out_grad_kernel, [like((4 * high, width), bf16)] * 2, place, moved, grad_branch, sums_one,
        sums_two, far=True, scratch=[pltpu.VMEM((8, high, width), bf16)],
    )
    out_sent, *out_parts = group_scatter(near, far, place)
    out_parts = [out_sent] + out_parts

    (mixed,) = local(
        attend_grad_kernel, [like((length, 3 * cols), bf16)],
        place, after(grad_moved, out_sent), queries, keys, values, attended, totals, tags_row,
        far=True, cost=14,
        scratch=[
            pltpu.VMEM((length, cols), f32),
            pltpu.VMEM((length, cols), f32),
            pltpu.VMEM((length, cols), bf16),
        ],
    )
    mixed = after(mixed, *out_parts)
    even_near, even_far, odd_near, odd_far = local(
        leave_kernel, [like((2 * rows, width), bf16)] * 4, place, mixed, full_qkv, far=True,
        cost=3,
    )
    near, far = local(
        qkv_grad_kernel, [like((2, width // 4 + 16, 3 * cols), bf16)] * 2,
        place, *blocks, after(mixed, odd_near), far=True, cost=4,
        scratch=[pltpu.VMEM((length, width), bf16)],
    )
    odd_far = swap(odd_far, ("x",), 1)
    even_far = swap(after(even_far, odd_far), ("x",), 1)
    near = after(near, odd_far)
    odd = odd_near.astype(f32) + odd_far.astype(f32)
    even = even_near.astype(f32) + even_far.astype(f32)
    even = even + swap(odd.astype(bf16), ("z",), 1).astype(f32)
    final = swap(even[rows:].astype(bf16), ("z",), 2)
    grad_inputs = grad_first + even[:rows] + final.astype(f32)

    qkv_sum = dp_sum(near, far)
    qkv_rows = qkv_sum[: n_ctx * shard].reshape(n_ctx, shard, 3 * cols)
    qkv_bias = jnp.broadcast_to(qkv_sum[n_ctx * shard :], (n_ctx, 16, 3 * cols))
    qkv_sum = jnp.concatenate([qkv_rows, qkv_bias], axis=1).astype(bf16)
    qkv_sum = lax.all_to_all(qkv_sum, CTX, 0, 0, tiled=True)
    (grad_wqkv,) = local(
        qkv_final_kernel, [like((shard, 3 * width), f32)], place, qkv_sum, far=True
    )
    bias_sum = qkv_sum[:, shard].reshape(n_ctx, 3, cols).transpose(1, 0, 2).reshape(3, width)
    bias_own = lax.dynamic_slice(bias_sum, (0, own * shard), (3, shard)).astype(f32)

    out_near, out_far = local(
        out_line_kernel, [like((2, shard + 16, width), f32), like((2, shard + 16, width), bf16)],
        place, after(out_parts[0], odd_far), *out_parts[1:],
        scratch=[pltpu.VMEM((4, shard + 16, width), f32)],
    )
    up_sum = after(up_sum, odd_far)
    up_sum = lax.all_to_all(up_sum, GROUP, 0, 0, tiled=True).reshape(8, shard, wide)
    (grad_wup,) = local(
        up_final_kernel, [like((shard, w_up.shape[1]), f32)], place, up_sum, far=True
    )
    out_sum = sum_over_z(out_near, swap(out_far, ("z",), 1), odd_far)
    thin = out_sum[shard:, :shard]

    return (
        result[None],
        grad_inputs.astype(bf16)[None],
        grad_wqkv,
        bias_own[0],
        bias_own[2],
        out_sum[:shard],
        thin[0],
        thin[1],
        thin[2],
        grad_wup,
        down_sum[units, :units].astype(f32),
        down_sum[:units].astype(f32),
        thin[3],
        thin[4],
        thin[5],
    )


def call_heads(mesh, *arrays):
    grid = Mesh(mesh.devices.reshape(2, 2, 4, 2), EVERY)
    lines, lone, block = P(EVERY, None), P(EVERY), P(DP, CTX, None)
    in_specs = (
        block, lines, lone, lone, lines, lone, lone, lone, lines, lone, lines, lone, lone, lone,
        P(DP, CTX), P(DP, CTX), block,
    )
    out_specs = (
        block, block, lines, lone, lone, lines, lone, lone, lone, lines, lone, lines, lone, lone,
        lone,
    )
    return jax.shard_map(
        heads_body, mesh=grid, in_specs=in_specs, out_specs=out_specs, check_vma=False
    )(*arrays)


def call(mesh, *arrays):
    if mesh.shape["dp"] == 4 and mesh.shape["ctx"] == 8 and arrays[0].shape[1] == 1024:
        return call_heads(mesh, *arrays)
    return general_call(mesh)(*arrays)


def general_call(mesh):
    in_specs = (
        P("dp", "ctx", None),
        P(("dp", "ctx"), None),
        P(("dp", "ctx")),
        P(("dp", "ctx")),
        P(("dp", "ctx"), None),
        P(("dp", "ctx")),
        P(("dp", "ctx")),
        P(("dp", "ctx")),
        P(("dp", "ctx"), None),
        P(("dp", "ctx")),
        P(("dp", "ctx"), None),
        P(("dp", "ctx")),
        P(("dp", "ctx")),
        P(("dp", "ctx")),
        P("dp", "ctx"),
        P("dp", "ctx"),
        P("dp", "ctx", None),
    )
    out_specs = (
        P("dp", "ctx", None),
        P("dp", "ctx", None),
        P(("dp", "ctx"), None),
        P(("dp", "ctx")),
        P(("dp", "ctx")),
        P(("dp", "ctx"), None),
        P(("dp", "ctx")),
        P(("dp", "ctx")),
        P(("dp", "ctx")),
        P(("dp", "ctx"), None),
        P(("dp", "ctx")),
        P(("dp", "ctx"), None),
        P(("dp", "ctx")),
        P(("dp", "ctx")),
        P(("dp", "ctx")),
    )
    return jax.shard_map(general_body, mesh=mesh, in_specs=in_specs, out_specs=out_specs, check_vma=False)


def solution(mesh):
    return partial(call, mesh)
```

```python
import math
from functools import partial

import jax
import jax.numpy as jnp
from jax import lax
from jax.experimental import pallas as pl
from jax.experimental.pallas import tpu as pltpu
from jax.sharding import Mesh
from jax.sharding import PartitionSpec as P

HEADS = 16
HEAD = 64
WINDOW = 1024


MASKED = -1e30
EPSILON = 1e-05


def layer_norm(values, scales, offsets):
    average = jnp.mean(values, axis=-1, keepdims=True)
    centred = values - average
    variance = jnp.mean(centred * centred, axis=-1, keepdims=True)
    return centred * lax.rsqrt(variance + EPSILON) * scales + offsets


def matmul(left, right):
    return jnp.dot(left, right, preferred_element_type=jnp.float32)


def rows_product(left, right):
    return lax.dot_general(
        left, right, (((0,), (0,)), ((), ())), preferred_element_type=jnp.float32
    )


def cols_product(left, right):
    return lax.dot_general(
        left, right, (((1,), (1,)), ((), ())), preferred_element_type=jnp.float32
    )


def split_heads(matrix):
    return matrix.reshape(matrix.shape[0], HEADS, HEAD)


def allowed_keys(query_tags, query_place, key_tags, key_place):
    same_doc = query_tags[:, None] // 2 == key_tags[None, :] // 2
    distance = jnp.abs(query_place[:, None] - key_place[None, :])
    usable = (key_tags[None, :] % 2 == 1) | (distance == 0)
    return same_doc & (distance <= WINDOW // 2) & usable


def masked_scores(query_block, key_heads, query_tags, query_place, key_tags, key_place):
    raw = (
        jnp.einsum("qhd,khd->hqk", query_block, key_heads, preferred_element_type=jnp.float32)
        * 0.125
    )
    return jnp.where(allowed_keys(query_tags, query_place, key_tags, key_place)[None], raw, MASKED)


def attend_forward(
    query_heads, key_heads, value_heads, query_tags, query_place, key_tags, key_place
):
    row_count = query_heads.shape[0]
    block_rows = min(row_count, 512)

    def one_block(block_index):
        scores = masked_scores(query_heads, key_heads, query_tags, query_place, key_tags, key_place)
        totals = jax.nn.logsumexp(scores, axis=2)
        probs = jnp.exp(scores - totals[:, :, None]).astype(jnp.bfloat16)
        output = jnp.einsum("hqk,khd->qhd", probs, value_heads, preferred_element_type=jnp.float32)
        return (output, totals)

    outputs, totals = lax.map(one_block, jnp.arange(row_count // block_rows, dtype=jnp.int32))
    return (outputs.reshape(row_count, HEADS * HEAD), totals)


def attend_backward(
    query_heads,
    key_heads,
    value_heads,
    grad_heads,
    deltas,
    totals,
    query_tags,
    query_place,
    key_tags,
    key_place,
):
    row_count = query_heads.shape[0]
    block_rows = min(row_count, 512)

    def one_block(running, block_index):
        key_grad, value_grad = running
        scores = masked_scores(query_heads, key_heads, query_tags, query_place, key_tags, key_place)
        probs = jnp.exp(scores - totals[block_index][:, :, None])
        dprobs = jnp.einsum(
            "qhd,khd->hqk", grad_heads, value_heads, preferred_element_type=jnp.float32
        )
        dscores = (probs * (dprobs - deltas[:, :, None])).astype(jnp.bfloat16)
        query_grad = (
            jnp.einsum("hqk,khd->qhd", dscores, key_heads, preferred_element_type=jnp.float32)
            * 0.125
        )
        key_grad = (
            key_grad
            + jnp.einsum("hqk,qhd->khd", dscores, query_heads, preferred_element_type=jnp.float32)
            * 0.125
        )
        value_grad = value_grad + jnp.einsum(
            "hqk,qhd->khd",
            probs.astype(jnp.bfloat16),
            grad_heads,
            preferred_element_type=jnp.float32,
        )
        return ((key_grad, value_grad), query_grad)

    zeros = jnp.zeros(key_heads.shape, jnp.float32)
    (key_grad, value_grad), query_grads = lax.scan(
        one_block, (zeros, zeros), jnp.arange(row_count // block_rows, dtype=jnp.int32)
    )
    key_count = key_heads.shape[0]
    return (
        query_grads.reshape(row_count, HEADS * HEAD),
        key_grad.reshape(key_count, HEADS * HEAD),
        value_grad.reshape(key_count, HEADS * HEAD),
    )


def clip_window(whole, rows_here, seq_length, own_index):
    neighbours = (WINDOW // 2 + rows_here - 1) // rows_here
    key_span = min((2 * neighbours + 1) * rows_here, seq_length)
    first_key = jnp.clip((own_index - neighbours) * rows_here, 0, seq_length - key_span)
    window = tuple((lax.dynamic_slice_in_dim(member, first_key, key_span, 0) for member in whole))
    return (window, first_key)


def window_keys(items, rows_here, seq_length, own_index):
    whole = (
        lax.all_gather(items[0], "ctx", axis=0, tiled=True),
        lax.all_gather(items[1], "ctx", axis=0, tiled=True),
        lax.all_gather(items[2], "ctx", axis=0, tiled=True),
    )
    return clip_window(whole, rows_here, seq_length, own_index)


def window_keys_again(items, rows_here, seq_length, own_index):
    whole = (
        lax.all_gather(items[0], "ctx", axis=0, tiled=True),
        lax.all_gather(items[1], "ctx", axis=0, tiled=True),
        lax.all_gather(items[2], "ctx", axis=0, tiled=True),
    )
    return clip_window(whole, rows_here, seq_length, own_index)


def return_key_grads(key_grad, value_grad, rows_here, first_key):
    width = key_grad.shape[1]
    joined = jnp.concatenate([key_grad, value_grad], axis=1)
    key_span = joined.shape[0]
    count = rows_here * lax.axis_size("ctx")
    padding = jnp.zeros((count, 2 * width), jnp.float32)
    padded = jnp.concatenate([padding, joined, padding], axis=0)
    offset = jnp.clip(jnp.int32(0) - first_key + count, 0, key_span + count)
    summed = lax.psum_scatter(
        lax.dynamic_slice_in_dim(padded, offset, count, 0), "ctx", scatter_dimension=0, tiled=True
    )
    return (summed[:, :width], summed[:, width:])


def general_body(
    tokens,
    w_qkv,
    b_query,
    b_value,
    w_out,
    b_out,
    ln1_gain,
    ln1_bias,
    w_up,
    b_up,
    w_down,
    b_down,
    ln2_gain,
    ln2_bias,
    segment_ids,
    pad_mask,
    cotangent,
):
    weight_shards = (
        w_qkv,
        b_query,
        b_value,
        w_out,
        b_out,
        ln1_gain,
        ln1_bias,
        w_up,
        b_up,
        w_down,
        b_down,
        ln2_gain,
        ln2_bias,
    )
    gathered = (
        lax.all_gather(weight_shards[0], ("dp", "ctx"), axis=0, tiled=True),
        lax.all_gather(weight_shards[1], ("dp", "ctx"), axis=0, tiled=True),
        lax.all_gather(weight_shards[2], ("dp", "ctx"), axis=0, tiled=True),
        lax.all_gather(weight_shards[3], ("dp", "ctx"), axis=0, tiled=True),
        lax.all_gather(weight_shards[4], ("dp", "ctx"), axis=0, tiled=True),
        lax.all_gather(weight_shards[5], ("dp", "ctx"), axis=0, tiled=True),
        lax.all_gather(weight_shards[6], ("dp", "ctx"), axis=0, tiled=True),
        lax.all_gather(weight_shards[7], ("dp", "ctx"), axis=0, tiled=True),
        lax.all_gather(weight_shards[8], ("dp", "ctx"), axis=0, tiled=True),
        lax.all_gather(weight_shards[9], ("dp", "ctx"), axis=0, tiled=True),
        lax.all_gather(weight_shards[10], ("dp", "ctx"), axis=0, tiled=True),
        lax.all_gather(weight_shards[11], ("dp", "ctx"), axis=0, tiled=True),
        lax.all_gather(weight_shards[12], ("dp", "ctx"), axis=0, tiled=True),
    )
    (
        full_qkv,
        full_bquery,
        full_bvalue,
        full_out,
        full_bout,
        full_gain_one,
        full_bias_one,
        full_up,
        full_bup,
        full_down,
        full_bdown,
        full_gain_two,
        full_bias_two,
    ) = gathered
    rows_here = tokens.shape[1]
    seq_length = rows_here * lax.axis_size("ctx")
    own_index = lax.axis_index("ctx")
    inputs = tokens[0]
    inputs_wide = inputs.astype(jnp.float32)
    model_width = inputs.shape[1]
    token_tags = 2 * (segment_ids[0] + 1) + pad_mask[0]
    query_place = own_index * rows_here + jnp.arange(rows_here, dtype=jnp.int32)
    mixed = matmul(inputs, full_qkv)
    queries = (mixed[:, :model_width] + full_bquery.astype(jnp.float32)).astype(jnp.bfloat16)
    keys = mixed[:, model_width : 2 * model_width].astype(jnp.bfloat16)
    values = (mixed[:, 2 * model_width :] + full_bvalue.astype(jnp.float32)).astype(jnp.bfloat16)
    (key_window, value_window, tag_window), first_key = window_keys(
        (keys, values, token_tags), rows_here, seq_length, own_index
    )
    key_place = first_key + jnp.arange(key_window.shape[0], dtype=jnp.int32)
    attended, totals = attend_forward(
        split_heads(queries),
        split_heads(key_window),
        split_heads(value_window),
        token_tags,
        query_place,
        tag_window,
        key_place,
    )
    attended_low = attended.astype(jnp.bfloat16)
    first = inputs_wide + matmul(attended_low, full_out) + full_bout.astype(jnp.float32)
    normed, first_pull = jax.vjp(
        layer_norm, first, full_gain_one.astype(jnp.float32), full_bias_one.astype(jnp.float32)
    )
    normed_low = normed.astype(jnp.bfloat16)
    hidden = matmul(normed_low, full_up) + full_bup.astype(jnp.float32)
    active, gelu_pull = jax.vjp(partial(jax.nn.gelu, approximate=False), hidden)
    active_low = active.astype(jnp.bfloat16)
    second = normed + matmul(active_low, full_down) + full_bdown.astype(jnp.float32)
    result, second_pull = jax.vjp(
        layer_norm, second, full_gain_two.astype(jnp.float32), full_bias_two.astype(jnp.float32)
    )
    gathered = (
        lax.all_gather(weight_shards[0], ("dp", "ctx"), axis=0, tiled=True),
        lax.all_gather(weight_shards[1], ("dp", "ctx"), axis=0, tiled=True),
        lax.all_gather(weight_shards[2], ("dp", "ctx"), axis=0, tiled=True),
        lax.all_gather(weight_shards[3], ("dp", "ctx"), axis=0, tiled=True),
        lax.all_gather(weight_shards[4], ("dp", "ctx"), axis=0, tiled=True),
        lax.all_gather(weight_shards[5], ("dp", "ctx"), axis=0, tiled=True),
        lax.all_gather(weight_shards[6], ("dp", "ctx"), axis=0, tiled=True),
        lax.all_gather(weight_shards[7], ("dp", "ctx"), axis=0, tiled=True),
        lax.all_gather(weight_shards[8], ("dp", "ctx"), axis=0, tiled=True),
        lax.all_gather(weight_shards[9], ("dp", "ctx"), axis=0, tiled=True),
        lax.all_gather(weight_shards[10], ("dp", "ctx"), axis=0, tiled=True),
        lax.all_gather(weight_shards[11], ("dp", "ctx"), axis=0, tiled=True),
        lax.all_gather(weight_shards[12], ("dp", "ctx"), axis=0, tiled=True),
    )
    back_qkv = gathered[0]
    back_out = gathered[3]
    back_up = gathered[7]
    back_down = gathered[9]
    grad_second, grad_gain_two, grad_bias_two = second_pull(cotangent[0].astype(jnp.float32))
    grad_outcome = grad_second.astype(jnp.bfloat16)
    grad_wdown = rows_product(active_low, grad_outcome)
    grad_bdown = jnp.sum(grad_outcome.astype(jnp.float32), axis=0)
    (grad_active,) = gelu_pull(cols_product(grad_outcome, back_down))
    grad_hidden = grad_active.astype(jnp.bfloat16)
    grad_wup = rows_product(normed_low, grad_hidden)
    grad_bup = jnp.sum(grad_hidden.astype(jnp.float32), axis=0)
    grad_normed = grad_second + cols_product(grad_hidden, back_up)
    grad_first, grad_gain_one, grad_bias_one = first_pull(grad_normed)
    grad_branch = grad_first.astype(jnp.bfloat16)
    grad_wout = rows_product(attended_low, grad_branch)
    grad_bout = jnp.sum(grad_branch.astype(jnp.float32), axis=0)
    grad_attended = cols_product(grad_branch, back_out).astype(jnp.bfloat16)
    deltas = jnp.sum(
        (grad_attended.astype(jnp.float32) * attended).reshape(rows_here, HEADS, HEAD), axis=2
    ).T
    (key_again, value_again, tag_again), first_again = window_keys_again(
        (keys, values, token_tags), rows_here, seq_length, own_index
    )
    place_again = first_again + jnp.arange(key_again.shape[0], dtype=jnp.int32)
    grad_queries, key_grad, value_grad = attend_backward(
        split_heads(queries),
        split_heads(key_again),
        split_heads(value_again),
        split_heads(grad_attended),
        deltas,
        totals,
        token_tags,
        query_place,
        tag_again,
        place_again,
    )
    key_total, value_total = return_key_grads(key_grad, value_grad, rows_here, first_again)
    grad_query_low = grad_queries.astype(jnp.bfloat16)
    grad_value_low = value_total.astype(jnp.bfloat16)
    grad_mixed = jnp.concatenate(
        [grad_query_low, key_total.astype(jnp.bfloat16), grad_value_low], axis=1
    )
    grad_wqkv = rows_product(inputs, grad_mixed)
    grad_bquery = jnp.sum(grad_query_low.astype(jnp.float32), axis=0)
    grad_bvalue = jnp.sum(grad_value_low.astype(jnp.float32), axis=0)
    grad_inputs = grad_first + cols_product(grad_mixed, back_qkv)
    summed = (
        lax.psum_scatter(grad_wqkv, ("dp", "ctx"), scatter_dimension=0, tiled=True),
        lax.psum_scatter(grad_bquery, ("dp", "ctx"), scatter_dimension=0, tiled=True),
        lax.psum_scatter(grad_bvalue, ("dp", "ctx"), scatter_dimension=0, tiled=True),
        lax.psum_scatter(grad_wout, ("dp", "ctx"), scatter_dimension=0, tiled=True),
        lax.psum_scatter(grad_bout, ("dp", "ctx"), scatter_dimension=0, tiled=True),
        lax.psum_scatter(grad_gain_one, ("dp", "ctx"), scatter_dimension=0, tiled=True),
        lax.psum_scatter(grad_bias_one, ("dp", "ctx"), scatter_dimension=0, tiled=True),
        lax.psum_scatter(grad_wup, ("dp", "ctx"), scatter_dimension=0, tiled=True),
        lax.psum_scatter(grad_bup, ("dp", "ctx"), scatter_dimension=0, tiled=True),
        lax.psum_scatter(grad_wdown, ("dp", "ctx"), scatter_dimension=0, tiled=True),
        lax.psum_scatter(grad_bdown, ("dp", "ctx"), scatter_dimension=0, tiled=True),
        lax.psum_scatter(grad_gain_two, ("dp", "ctx"), scatter_dimension=0, tiled=True),
        lax.psum_scatter(grad_bias_two, ("dp", "ctx"), scatter_dimension=0, tiled=True),
    )
    return (
        result.astype(jnp.bfloat16)[None],
        grad_inputs.astype(jnp.bfloat16)[None],
        summed[0],
        summed[1],
        summed[2],
        summed[3],
        summed[4],
        summed[5],
        summed[6],
        summed[7],
        summed[8],
        summed[9],
        summed[10],
        summed[11],
        summed[12],
    )


GROUP = ("y", "core", "x")
CTX = ("z", "x")
DP = ("y", "core")
EVERY = ("y", "core", "z", "x")
bf16, f32 = jnp.bfloat16, jnp.float32


def swap(member, axes, code):
    count = 1
    for axis in axes:
        count *= lax.axis_size(axis)
    return lax.ppermute(member, axes, [(place, place ^ code) for place in range(count)])


def after(member, *events):
    return lax.optimization_barrier((member,) + events)[0]


class Turns:
    def __init__(self, last):
        self.last = last

    def take(self, *members):
        return lax.optimization_barrier((*members, self.last))[:-1]


def like(shape, kind):
    return jax.ShapeDtypeStruct(shape, kind)


def staged(kernel, groups, results, lazy, place, *refs):
    count = sum(groups)
    given, refs = refs[:count], refs[count:]
    out, refs = list(refs[: len(results)]), refs[len(results) :]
    held, refs = refs[: len(groups)], refs[len(groups) :]
    staging, refs = refs[: sum(results)], refs[sum(results) :]
    (arrived, left), refs = refs[:2], refs[2:]
    copies, index, first = [], 0, []
    for size, target in zip(groups, held):
        first.append(index)
        rows = target.shape[0] // size
        for member in range(size):
            part = target if size == 1 else target.at[pl.ds(member * rows, rows)]
            copies.append(pltpu.make_async_copy(given[index], part, arrived.at[index]))
            index += 1
    for copy in copies:
        copy.start()
    if lazy:
        arrivals = copies
        kernel = partial(kernel, lambda group, member=0: arrivals[first[group] + member].wait())
    else:
        for copy in copies:
            copy.wait()
    copies, index = [], 0
    for i, far in enumerate(results):
        if far:
            copies.append(pltpu.make_async_copy(staging[index], out[i], left.at[index]))
            out[i] = staging[index]
            index += 1
    kernel(place, *held, *out, *refs)
    for copy in copies:
        copy.start()
    for copy in copies:
        copy.wait()


def bytes_of(v):
    return math.prod(v.shape) * jnp.dtype(v.dtype).itemsize


def local(kernel, outs, place, *operands, scratch=(), far=False, keep=(), lazy=False, cost=0):
    near = pl.BlockSpec(memory_space=pltpu.VMEM)
    groups = [v if isinstance(v, (tuple, list)) else (v,) for v in operands]
    operands = [v for group in groups for v in group]
    size = sum(bytes_of(v) for v in (*operands, *outs, *scratch))
    results = [far and i not in keep for i in range(len(outs))]
    if far:
        kernel = partial(staged, kernel, [len(group) for group in groups], results, lazy)
        held = [
            pltpu.VMEM((len(g) * g[0].shape[0],) + g[0].shape[1:], g[0].dtype) for g in groups
        ]
        held += [pltpu.VMEM(v.shape, v.dtype) for v, out in zip(outs, results) if out]
        held += [pltpu.SemaphoreType.DMA((len(operands),))]
        held += [pltpu.SemaphoreType.DMA((max(sum(results), 1),))]
        scratch = held + list(scratch)
        operands = [pltpu.with_memory_space_constraint(v, pltpu.HBM) for v in operands]
        outs = [pltpu.HBM(v.shape, v.dtype) if out else v for v, out in zip(outs, results)]
    hbm = pl.BlockSpec(memory_space=pltpu.HBM)
    return pl.pallas_call(
        kernel,
        out_shape=list(outs),
        in_specs=[pl.BlockSpec(memory_space=pltpu.SMEM)] + [hbm if far else near] * len(operands),
        out_specs=[hbm if out else near for out in results],
        scratch_shapes=list(scratch),
        cost_estimate=pl.CostEstimate(flops=cost * 10**9, bytes_accessed=0, transcendentals=0),
        compiler_params=pltpu.CompilerParams(vmem_limit_bytes=size + ((24 if cost > 8 else 6) << 20)),
    )(place, *operands)


def pair_product(left, right):
    return lax.dot_general(
        left, right, (((0,), (0,)), ((), ())), preferred_element_type=jnp.float32
    )


def plane_gather(block):
    return [block] + [swap(block, ("y", "x"), code) for code in range(1, 4)]


def group_gather(block):
    plane = plane_gather(block)
    return plane + [swap(member, ("core",), 1) for member in plane]


def merge_kernel(place, near, far, own, *sent):
    rows = own.shape[0]
    for code in range(4):
        part = pl.ds(code * rows, rows)
        total = near[part, :].astype(f32) + far[part, :].astype(f32)
        if code == 0:
            own[...] = total
        else:
            sent[code - 1][...] = total.astype(bf16)


def group_scatter(near, far, place, event=None):
    crossed = swap(far, ("core",), 1)
    if event is not None:
        crossed = after(crossed, event)
    return plane_scatter(near, crossed, place)


def plane_scatter(near, crossed, place):
    rows, width = near.shape[0] // 4, near.shape[1]
    outs = [like((rows, width), f32)] + [like((rows, width), bf16)] * 3
    own, *sent = local(merge_kernel, outs, place, near, crossed)
    parts = [own] + [swap(sent[code - 1], ("y", "x"), code) for code in range(1, 4)]
    return parts


def ctx_gather(block):
    two, one = swap(block, ("z",), 2), swap(block, ("z",), 1)
    line = [block, one, two, swap(two, ("z",), 1)]
    blocks = [piece for member in line[:3] for piece in (member, swap(member, ("x",), 1))]
    return blocks + [line[3]]


def pack_kernel(place, w_qkv, w_up, *refs):
    vectors, (b_up, segments, pads, qkv_ref, up_ref) = refs[:8], refs[8:]
    groups, _, wide = qkv_ref.shape
    shard, cols = w_qkv.shape[0], wide // 3
    tags = (2 * (segments[...] + 1) + pads[...]).astype(f32)
    lone = jnp.concatenate([v[...].astype(f32) for v in vectors], axis=0)
    lone = jnp.concatenate([lone, jnp.zeros((8, 128 - shard), f32)], axis=1)
    small = jnp.concatenate([lone, b_up[...].astype(f32), tags, jnp.zeros((6, 128), f32)], axis=0)
    small = jnp.concatenate([small, jnp.zeros((16, wide - 128), f32)], axis=1).astype(bf16)
    for c in range(groups):
        for kind in range(3):
            at = (kind * groups + c) * cols
            qkv_ref[c, :shard, kind * cols : (kind + 1) * cols] = w_qkv[:, at : at + cols]
        qkv_ref[c, shard:, :] = small
    units = b_up.shape[1]
    for g in range(8):
        for z in range(4):
            at = ((g // 2 * 4 + z) * 2 + g % 2) * units
            up_ref[g, :, z * units : (z + 1) * units] = w_up[:, at : at + units]


def out_gather(block, *events):
    pair = after(jnp.stack([block, swap(block, ("z",), 1)]), events[0])
    line = after(jnp.concatenate([pair, swap(pair, ("z",), 2)]), events[1])
    both = after(jnp.stack([line, swap(line, ("y",), 1)]), events[2])
    far = swap(both, ("x",), 1)
    both, far = after(both, events[3]), after(far, events[3])
    return [both, far, swap(both, ("core",), 1), swap(far, ("core",), 1)]


def order_out_kernel(place, p00, p01, p10, p11, out_ref):
    rows = p00.shape[2]
    own = place[0]
    for core in range(2):
        for x in range(2):
            piece = ((p00, p01), (p10, p11))[core][x]
            for y in range(2):
                for z in range(4):
                    at = own ^ (y * 16 + core * 8 + z * 2 + x)
                    out_ref[pl.ds(at * rows, rows), :] = piece[y, z]


def order_kernel(place, *refs):
    up_refs, down_refs, (up_out, down_out) = refs[:4], refs[4:8], refs[8:]
    rows, units = up_out.shape[0] // 32, down_refs[0].shape[0]
    own_z = place[3]
    for z in range(4):
        down_out[pl.ds((own_z ^ z) * units, units), :] = down_refs[z][...]
        for j in range(8):
            at = (j // 2 * 4 + (own_z ^ z)) * 2 + j % 2
            up_out[pl.ds(at * rows, rows), :] = up_refs[z][pl.ds(j * rows, rows), :]


def allowed_here(query_tags, query_place, key_tags, key_place):
    same_doc = (query_tags >> 1) == (key_tags >> 1)
    distance = jnp.abs(query_place - key_place)
    usable = ((key_tags & 1) == 1) | (distance == 0)
    return same_doc & (distance <= WINDOW // 2) & usable


def places(own_ctx, rows, shape, axis, start=0):
    index = lax.broadcasted_iota(jnp.int32, shape, axis) + start
    return ((index // rows) ^ own_ctx) * rows + index % rows


def attend_kernel(ready, place, *refs, n_blocks, rows, cols):
    pieces, refs = refs[:4], refs[4:]
    bias, tags_row, lines, q_ref, k_ref, v_ref, att_ref, msg_ref, lse_ref, qkv_ref = refs
    own_dp, own_ctx = place[1], place[2]
    shard = 32
    for m, piece in enumerate(pieces):
        ready(m)
        for c in range(n_blocks):
            at = ((own_dp ^ m) * n_blocks + c) * shard
            qkv_ref[pl.ds(at, shard), :] = piece[c, :shard, :]
    ready(4)
    ready(5)
    for j in range(n_blocks // 2):
        part = pl.ds(j * 2 * rows, 2 * rows)
        ready(6, 2 * j)
        ready(6, 2 * j + 1)
        mixed = matmul(lines[part, :], qkv_ref[...]) + bias[...]
        q_ref[part, :] = mixed[:, :cols].astype(bf16)
        k_ref[part, :] = mixed[:, cols : 2 * cols].astype(bf16)
        v_ref[part, :] = mixed[:, 2 * cols :].astype(bf16)
    length = n_blocks * rows
    chunk = 2 * rows

    def step(index, carry):
        part = pl.ds(index * chunk, chunk)
        allowed = allowed_here(
            jnp.broadcast_to(tags_row[:, part], (128, chunk)).T[:, :1],
            places(own_ctx, rows, (chunk, 1), 0, index * chunk),
            tags_row[...],
            places(own_ctx, rows, (1, length), 1),
        )
        found = []
        for head in range(cols // HEAD):
            lanes = slice(head * HEAD, (head + 1) * HEAD)
            scores = cols_product(q_ref[part, lanes], k_ref[:, lanes]) * 0.125
            scores = jnp.where(allowed, scores, MASKED)
            top = jnp.max(scores, axis=1, keepdims=True)
            weights = jnp.exp(scores - top)
            mass = jnp.sum(weights, axis=1, keepdims=True)
            found.append(matmul(weights.astype(bf16), v_ref[:, lanes]) / mass)
            total = top + jnp.log(mass)
            lse_ref[pl.ds(head, 1), part] = jnp.broadcast_to(total, (chunk, 128)).T[:1, :]
        attended = jnp.concatenate(found, axis=1)
        att_ref[part, :] = attended
        for half in range(2):
            at = ((index * 2 + half) ^ own_ctx) * rows
            msg_ref[pl.ds(at, rows), :] = attended[half * rows : (half + 1) * rows].astype(bf16)
        return carry

    lax.fori_loop(0, length // chunk, step, 0, unroll=True)


def branch_kernel(
    place, moved, w_out, inputs, vectors, normed_ref, low_ref, hat_ref, rate_ref
):
    groups, rows, cols = moved.shape
    total = inputs[...].astype(f32) + vectors[2:3, :]
    for c in range(groups):
        total = total + matmul(moved[c], w_out[pl.ds(c * cols, cols), :])
    centred = total - jnp.mean(total, axis=1, keepdims=True)
    rate = lax.rsqrt(jnp.mean(centred * centred, axis=1, keepdims=True) + EPSILON)
    hat = centred * rate
    normed = hat * vectors[3:4, :] + vectors[4:5, :]
    normed_ref[...] = normed
    low_ref[...] = normed.astype(bf16)
    hat_ref[...] = hat
    rate_ref[...] = jnp.broadcast_to(rate, rate_ref.shape)


def forward_kernel(ready, place, up, bias, lines, down, hidden_ref, active_ref, near, far):
    rows = lines.shape[0] // 4
    ready(0)
    ready(1)
    for quarter in range(4):
        part = pl.ds(quarter * rows, rows)
        ready(2, 2 * quarter)
        ready(2, 2 * quarter + 1)
        hidden = matmul(lines[part, :], up[...]) + bias[...]
        hidden_ref[part, :] = hidden
        active = (0.5 * hidden * (1 + lax.erf(hidden * 0.7071067811865476))).astype(bf16)
        active_ref[part, :] = active
        if quarter == 0:
            ready(3)
        target = near if quarter < 2 else far
        target[pl.ds(quarter % 2 * rows, rows), :] = matmul(active, down[...]).astype(bf16)


def second_kernel(
    place, normed, own, p1, p2, p3, vectors, cotangent, result_ref, grad_ref, low_ref, sums_ref
):
    second = normed[...] + own[...] + p1[...].astype(f32) + p2[...].astype(f32)
    second = second + p3[...].astype(f32) + vectors[5:6, :]
    centred = second - jnp.mean(second, axis=1, keepdims=True)
    rate = lax.rsqrt(jnp.mean(centred * centred, axis=1, keepdims=True) + EPSILON)
    hat = centred * rate
    gain = vectors[6:7, :]
    result_ref[...] = (hat * gain + vectors[7:8, :]).astype(bf16)
    grad = cotangent[...].astype(f32)
    scaled = grad * gain
    mean_scaled = jnp.mean(scaled, axis=1, keepdims=True)
    mean_hat = jnp.mean(scaled * hat, axis=1, keepdims=True)
    grad_second = rate * (scaled - mean_scaled - hat * mean_hat)
    grad_ref[...] = grad_second
    low = grad_second.astype(bf16)
    low_ref[...] = low
    sums_ref[0:1, :] = jnp.sum(low.astype(f32), axis=0, keepdims=True)
    sums_ref[1:2, :] = jnp.sum(grad * hat, axis=0, keepdims=True)
    sums_ref[2:3, :] = jnp.sum(grad, axis=0, keepdims=True)


def backward_kernel(place, *refs):
    blocks = refs[:8]
    up, down, slope, grad_ref, near, far = refs[8:]
    rows = blocks[0].shape[0]
    for pair in range(4):
        lines = jnp.concatenate([blocks[2 * pair][...], blocks[2 * pair + 1][...]], axis=0)
        part = pl.ds(pair * 2 * rows, 2 * rows)
        grad = (slope[part, :] * cols_product(lines, down[...])).astype(bf16)
        grad_ref[part, :] = grad
        target = near if pair < 2 else far
        target[pl.ds(pair % 2 * 2 * rows, 2 * rows), :] = cols_product(grad, up[...]).astype(bf16)


def down_grad_kernel(place, lines, active, grad_hidden, near, far, parts):
    width = lines.shape[1]
    shard = active.shape[1] // 4
    total = jnp.sum(grad_hidden[...].astype(f32), axis=0, keepdims=True)
    for z in range(4):
        part = slice(z * shard, (z + 1) * shard)
        at = place[3] ^ z
        parts[at, :shard, :] = pair_product(active[:, part], lines[...]).astype(bf16)
        parts[at, shard:, :shard] = jnp.broadcast_to(total[:, part], (16, shard)).astype(bf16)
        parts[at, shard:, shard:] = jnp.zeros((16, width - shard), bf16)
    for half in range(2):
        near[half], far[half] = parts[2 * half], parts[2 * half + 1]


def up_grad_kernel(place, lines, grad_hidden, near, far, parts):
    own_z = place[3]
    for quarter in range(4):
        span = 8 * 32
        part = slice(quarter * span, (quarter + 1) * span)
        found = pair_product(lines[:, part], grad_hidden[...]).astype(bf16)
        for z in range(4):
            for x in range(2):
                piece = found[(z * 2 + x) * 32 : (z * 2 + x + 1) * 32]
                parts[own_z ^ z, pl.ds((quarter * 2 + x) * 32, 32), :] = piece
    for half in range(2):
        near[half], far[half] = parts[2 * half], parts[2 * half + 1]


def first_kernel(
    place, grad_second, own, p1, p2, p3, vectors, hat_ref, rate_ref, w_out, grad_ref, low_ref,
    msg_ref, sums_ref,
):
    grad = grad_second[...] + own[...] + p1[...].astype(f32) + p2[...].astype(f32)
    grad = grad + p3[...].astype(f32)
    hat = hat_ref[...]
    scaled = grad * vectors[3:4, :]
    mean_scaled = jnp.mean(scaled, axis=1, keepdims=True)
    mean_hat = jnp.mean(scaled * hat, axis=1, keepdims=True)
    grad_first = rate_ref[:, :1] * (scaled - mean_scaled - hat * mean_hat)
    grad_ref[...] = grad_first
    low = grad_first.astype(bf16)
    low_ref[...] = low
    groups, rows, cols = msg_ref.shape
    for c in range(groups):
        msg_ref[c] = cols_product(low, w_out[pl.ds(c * cols, cols), :]).astype(bf16)
    sums_ref[0:1, :] = jnp.sum(low.astype(f32), axis=0, keepdims=True)
    sums_ref[1:2, :] = jnp.sum(grad * hat, axis=0, keepdims=True)
    sums_ref[2:3, :] = jnp.sum(grad, axis=0, keepdims=True)


def out_grad_kernel(place, moved, low, sums_one, sums_two, near, far, parts):
    groups, rows, cols = moved.shape
    high, width = parts.shape[1:]
    own_y, own_core, own_x = place[4], place[5], place[6]
    sums = [sums_one[0:3, :], sums_two[0:3, :], jnp.zeros((high - rows - 6, width), f32)]
    sums = jnp.concatenate(sums, axis=0).astype(bf16)
    for c in range(groups):
        found = pair_product(moved[c], low[...]).astype(bf16)
        for m in range(4):
            y, core, z, x = c // 4, c // 2 % 2, c % 2 * 2 + m // 2, m % 2
            code = (core ^ own_core) * 4 + (y ^ own_y) * 2 + (x ^ own_x)
            parts[code, pl.ds(z * 32, 32), :] = found[m * 32 : (m + 1) * 32]
            lanes = slice((c * 4 + m) * 32, (c * 4 + m + 1) * 32)
            parts[code, rows:, z * 32 : (z + 1) * 32] = sums[:, lanes]
    for code in range(4):
        near[pl.ds(code * high, high), :] = parts[code]
        far[pl.ds(code * high, high), :] = parts[code + 4]


def out_line_kernel(place, own, p1, p2, p3, near, far, parts):
    total = own[...] + p1[...].astype(f32) + p2[...].astype(f32) + p3[...].astype(f32)
    own_z = place[3]
    parts[...] = jnp.zeros(parts.shape, f32)
    for z in range(4):
        at = own_z ^ z
        parts[at, :32, :] = total[z * 32 : (z + 1) * 32]
        parts[at, 32:, :32] = total[128:, z * 32 : (z + 1) * 32]
    for half in range(2):
        near[half], far[half] = parts[2 * half], parts[2 * half + 1].astype(bf16)


def attend_grad_kernel(
    place, *refs,
):
    moved, q_ref, k_ref, v_ref, att_ref, lse_ref, tags_row, *refs = refs
    mixed_ref, key_grad, value_grad, back = refs
    groups, rows, cols = moved.shape
    length = groups * rows
    own_ctx = place[2]
    for j in range(groups):
        back[pl.ds(j * rows, rows), :] = moved[own_ctx ^ j]
    key_grad[...] = jnp.zeros(key_grad.shape, f32)
    value_grad[...] = jnp.zeros(value_grad.shape, f32)
    chunk = 2 * rows
    tags_col = jnp.broadcast_to(tags_row[...], (128, length)).T[:, :1]

    def step(index, carry):
        part = pl.ds(index * chunk, chunk)
        allowed = allowed_here(
            tags_row[:, part],
            places(own_ctx, rows, (1, chunk), 1, index * chunk),
            tags_col,
            places(own_ctx, rows, (length, 1), 0),
        )
        weighted = (back[part, :].astype(f32) * att_ref[part, :]).T
        found = []
        for head in range(cols // HEAD):
            lanes = slice(head * HEAD, (head + 1) * HEAD)
            delta = jnp.sum(weighted[lanes, :], axis=0, keepdims=True)
            scores = cols_product(k_ref[:, lanes], q_ref[part, lanes]) * 0.125
            probs = jnp.where(allowed, jnp.exp(scores - lse_ref[pl.ds(head, 1), part]), 0.0)
            grads = cols_product(v_ref[:, lanes], back[part, lanes])
            grads = (probs * (grads - delta)).astype(bf16)
            value_grad[:, lanes] += matmul(probs.astype(bf16), back[part, lanes])
            key_grad[:, lanes] += matmul(grads, q_ref[part, lanes])
            found.append(pair_product(grads, k_ref[:, lanes]) * 0.125)
        mixed_ref[part, :cols] = jnp.concatenate(found, axis=1).astype(bf16)
        return carry

    lax.fori_loop(0, length // chunk, step, 0, unroll=True)
    mixed_ref[:, cols : 2 * cols] = (key_grad[...] * 0.125).astype(bf16)
    mixed_ref[:, 2 * cols :] = value_grad[...].astype(bf16)


def leave_kernel(place, *refs):
    mixed_ref, qkv_ref, even_near, even_far, odd_near, odd_far = refs
    messages = ((even_near, even_far), (odd_near, odd_far))
    groups, rows = 8, mixed_ref.shape[0] // 8
    for j in range(groups):
        part = cols_product(mixed_ref[pl.ds(j * rows, rows), :], qkv_ref[...])
        target = messages[j // 2 % 2][j % 2]
        target[pl.ds(j // 4 * rows, rows), :] = part.astype(bf16)


def qkv_grad_kernel(place, lines, mixed_ref, near, far):
    own_dp = place[1]
    cols = mixed_ref.shape[1] // 3
    sums = jnp.sum(mixed_ref[...].astype(f32), axis=0, keepdims=True)
    sums = jnp.broadcast_to(sums, (16, 3 * cols)).astype(bf16)
    span = lines.shape[1] // 4
    for ky in range(2):
        for kc in range(2):
            start = pl.multiple_of((own_dp ^ (ky * 2 + kc)) * span, span)
            found = pair_product(lines[:, pl.ds(start, span)], mixed_ref[...]).astype(bf16)
            target = far if kc else near
            target[ky, :span, :] = found
            target[ky, span:, :] = sums


def up_final_kernel(place, moved, out):
    groups, shard, wide = moved.shape
    units = wide // 4
    for g in range(groups):
        for z in range(4):
            at = ((g // 2 * 4 + z) * 2 + g % 2) * units
            out[:, at : at + units] = moved[g, :, z * units : (z + 1) * units].astype(f32)


def qkv_final_kernel(place, moved, out):
    groups, _, wide = moved.shape
    shard, cols = out.shape[0], wide // 3
    for c in range(groups):
        for kind in range(3):
            at = (kind * groups + c) * cols
            out[:, at : at + cols] = moved[c, :shard, kind * cols : (kind + 1) * cols].astype(f32)


def heads_body(
    tokens, w_qkv, b_query, b_value, w_out, b_out, ln1_gain, ln1_bias, w_up, b_up, w_down, b_down,
    ln2_gain, ln2_bias, segment_ids, pad_mask, cotangent,
):
    inputs = tokens[0]
    rows, width = inputs.shape
    n_ctx = lax.axis_size(CTX)
    n_dp = lax.axis_size(DP)
    n_z = lax.axis_size("z")
    length = rows * n_ctx
    cols = width // n_ctx
    shard = w_qkv.shape[0]
    units = w_down.shape[0]
    wide = n_z * units
    own_ctx = lax.axis_index(CTX)
    own_dp = lax.axis_index(DP)
    own = lax.axis_index(EVERY)
    place = jnp.stack(
        [own, own_dp, own_ctx, lax.axis_index("z")] + [lax.axis_index(a) for a in GROUP]
    ).astype(jnp.int32)

    vectors = (b_query, b_value, b_out, ln1_gain, ln1_bias, b_down, ln2_gain, ln2_bias)
    qkv_parts, up_parts = local(
        pack_kernel,
        [like((n_ctx, shard + 16, 3 * cols), bf16), like((8, shard, wide), bf16)],
        place, w_qkv, w_up, *[v[None] for v in vectors], b_up[None], segment_ids, pad_mask,
        far=True,
    )
    blocks = ctx_gather(inputs)
    qkv = after(qkv_parts, blocks[1], blocks[2])
    qkv = lax.all_to_all(qkv, CTX, 0, 0, tiled=True)
    blocks.append(swap(blocks[6], ("x",), 1))
    qkv_y = swap(after(qkv, blocks[3], blocks[6]), ("y",), 1)
    qkv_c, qkv_y = after(qkv, blocks[5]), after(qkv_y, blocks[5])
    pieces = [qkv, swap(qkv_c, ("core",), 1), qkv_y, swap(qkv_y, ("core",), 1)]
    up = after(up_parts.reshape(8 * shard, wide), qkv)
    up = lax.all_to_all(up, GROUP, 0, 0, tiled=True)
    small = jnp.stack([piece[:, shard : shard + 10, :128] for piece in pieces])
    small = jnp.take(small, own_dp ^ jnp.arange(n_dp), axis=0).reshape(n_dp * n_ctx, 10, 128)
    vectors = small[:, :8, :shard].transpose(1, 0, 2).reshape(8, width).astype(f32)
    bias_up = small[:, 8].reshape(n_dp, n_z, 2, units)
    bias_up = lax.dynamic_slice(bias_up, (own_dp, 0, lax.axis_index("x"), 0), (1, n_z, 1, units))
    bias_up = bias_up.reshape(1, wide).astype(f32)
    tags = lax.dynamic_slice(small[:, 9], (own_dp * n_ctx, 0), (n_ctx, rows)).astype(jnp.int32)
    tags_row = jnp.take(tags, own_ctx ^ jnp.arange(n_ctx), axis=0).reshape(1, length)
    bias = lax.dynamic_slice(vectors, (0, own_ctx * cols), (2, cols))
    bias = jnp.concatenate([bias[:1], jnp.zeros((1, cols), f32), bias[1:]], axis=1)

    down = after(w_down, blocks[6])
    down_z = swap(down, ("z",), 2)
    down_lines = [down, swap(down, ("z",), 1), down_z, swap(down_z, ("z",), 1)]
    queries, keys, values, attended, message, totals, full_qkv = local(
        partial(attend_kernel, n_blocks=n_ctx, rows=rows, cols=cols),
        [like((length, cols), bf16)] * 3
        + [
            like((length, cols), f32),
            like((length, cols), bf16),
            like((8, length), f32),
            like((width, 3 * cols), bf16),
        ],
        place, *pieces, bias, tags_row, blocks, far=True, lazy=True, cost=10,
    )
    up_z = swap(up, ("z",), 2)
    up_lines = [up, swap(up, ("z",), 1), up_z, swap(up_z, ("z",), 1)]
    (full_out,) = local(
        order_out_kernel, [like((width, width), bf16)], place,
        *out_gather(after(w_out, blocks[2]), blocks[4], qkv, blocks[7], message), far=True,
        keep=(0,),
    )
    moved = lax.all_to_all(message, CTX, 0, 0, tiled=True).reshape(n_ctx, rows, cols)
    normed, normed_low, hat, rate = local(
        branch_kernel,
        [like((rows, width), f32), like((rows, width), bf16), like((rows, width), f32)]
        + [like((rows, 128), f32)],
        place, moved, full_out, inputs, vectors,
    )
    normed_all = group_gather(normed_low)
    full_up, down = local(
        order_kernel, [like((width, wide), bf16), like((wide, width), bf16)], place,
        after(up_lines[0], normed_all[1]), *up_lines[1:], *down_lines, far=True,
    )
    hidden, active, near, far = local(
        forward_kernel,
        [like((8 * rows, wide), f32), like((8 * rows, wide), bf16)]
        + [like((4 * rows, width), bf16)] * 2,
        place, full_up, bias_up, normed_all, down, far=True, keep=(0, 2, 3), lazy=True,
    )
    parts = group_scatter(near, far, place)
    hidden = after(hidden, parts[1])
    result, grad_second, grad_z, sums_two = local(
        second_kernel,
        [like((rows, width), bf16), like((rows, width), f32), like((rows, width), bf16)]
        + [like((8, width), f32)],
        place, normed, *parts, vectors, cotangent[0],
    )

    slope = 0.5 * (1 + lax.erf(hidden * 0.7071067811865476)) + hidden * (
        jnp.exp(-0.5 * hidden * hidden) * 0.3989422804014327
    )
    grad_z_all = group_gather(grad_z)
    grad_hidden, near, far = local(
        backward_kernel,
        [like((8 * rows, wide), bf16)] + [like((4 * rows, width), bf16)] * 2,
        place, *grad_z_all, full_up, down, slope,
    )
    down_near, down_far = local(
        down_grad_kernel, [like((2, units + 16, width), bf16)] * 2,
        place, grad_z_all, active, grad_hidden, far=True,
        scratch=[pltpu.VMEM((4, units + 16, width), bf16)],
    )
    parts = group_scatter(near, far, place, down_near)
    down_far = swap(down_far, ("z",), 1)
    up_near, up_far = local(
        up_grad_kernel, [like((2, 8 * shard, wide), bf16)] * 2,
        place, normed_all, after(grad_hidden, parts[1]), far=True,
        scratch=[pltpu.VMEM((4, 8 * shard, wide), bf16)],
    )
    grad_first, grad_branch, message, sums_one = local(
        first_kernel,
        [like((rows, width), f32), like((rows, width), bf16), like((n_ctx, rows, cols), bf16)]
        + [like((8, width), f32)],
        place, after(grad_second, up_near), *parts, vectors, hat, rate, full_out,
    )
    grad_moved = lax.all_to_all(message, CTX, 0, 0, tiled=True)
    high = rows + 16
    near, far = local(
        out_grad_kernel, [like((4 * high, width), bf16)] * 2, place, moved, grad_branch, sums_one,
        sums_two, far=True, scratch=[pltpu.VMEM((8, high, width), bf16)],
    )
    out_near, out_far = near, swap(far, ("core",), 1)
    turns = Turns(near)
    (down_far,) = turns.take(down_far)
    turns.last = down_sent = (down_near[1].astype(f32) + down_far[1].astype(f32)).astype(bf16)
    (grad_moved,) = turns.take(grad_moved)
    (mixed,) = local(
        attend_grad_kernel, [like((length, 3 * cols), bf16)],
        place, grad_moved, queries, keys, values, attended, totals, tags_row,
        far=True, cost=14,
        scratch=[
            pltpu.VMEM((length, cols), f32),
            pltpu.VMEM((length, cols), f32),
            pltpu.VMEM((length, cols), bf16),
        ],
    )
    up_far = swap(after(up_far, grad_moved), ("z",), 1)
    even_near, even_far, odd_near, odd_far = local(
        leave_kernel, [like((2 * rows, width), bf16)] * 4, place, mixed, full_qkv, far=True,
        cost=3,
    )
    near, far = local(
        qkv_grad_kernel, [like((2, width // 4 + 16, 3 * cols), bf16)] * 2,
        place, blocks, after(mixed, odd_near), far=True, cost=4,
    )

    odd_far, far, down_last = swap(odd_far, ("x",), 1), swap(far, ("core",), 1), swap(down_sent, ("z",), 2)
    turns = Turns(near)
    down_last, up_far = turns.take(down_last, up_far)
    up_sent = (up_near[1].astype(f32) + up_far[1].astype(f32)).astype(bf16)
    up_last = swap(up_sent, ("z",), 2)
    down_sum = down_near[0].astype(f32) + down_far[0].astype(f32) + down_last.astype(f32)
    turns.last = up_sent
    (far,) = turns.take(far)
    qkv_sent = (near[1].astype(f32) + far[1].astype(f32)).astype(bf16)
    qkv_last = swap(qkv_sent, ("y",), 1)
    turns.last = qkv_sent
    (odd_far,) = turns.take(odd_far)
    even_far = swap(after(even_far, odd_far), ("x",), 1)
    odd = (odd_near.astype(f32) + odd_far.astype(f32)).astype(bf16)
    odd_last = swap(odd, ("z",), 1)
    turns.last = odd
    (up_last,) = turns.take(up_last)
    up_sum = up_near[0].astype(f32) + up_far[0].astype(f32) + up_last.astype(f32)
    turns.last = up_sum = up_sum.astype(bf16)
    up_sum = lax.all_to_all(up_sum, GROUP, 0, 0, tiled=True).reshape(8, shard, wide)
    (qkv_last,) = turns.take(qkv_last)
    qkv_sum = near[0].astype(f32) + far[0].astype(f32) + qkv_last.astype(f32)
    qkv_sum = qkv_sum.astype(bf16)
    qkv_rows = qkv_sum[: n_ctx * shard].reshape(n_ctx, shard, 3 * cols)
    qkv_bias = jnp.broadcast_to(qkv_sum[n_ctx * shard :], (n_ctx, 16, 3 * cols))
    turns.last = qkv_sum = jnp.concatenate([qkv_rows, qkv_bias], axis=1)
    (out_far,) = turns.take(out_far)
    out_parts = plane_scatter(out_near, out_far, place)
    turns.last = out_parts[0]
    even_far, odd_last = turns.take(even_far, odd_last)
    even = even_near.astype(f32) + even_far.astype(f32) + odd_last.astype(f32)
    final = swap(even[rows:].astype(bf16), ("z",), 2)
    turns.last = even
    up_sum, qkv_sum = turns.take(up_sum, qkv_sum)
    qkv_sum = lax.all_to_all(qkv_sum, CTX, 0, 0, tiled=True)
    (grad_wup,) = local(
        up_final_kernel, [like((shard, w_up.shape[1]), f32)], place, up_sum
    )
    turns.last = grad_wup
    out_parts = turns.take(*out_parts)
    line_near, line_far = local(
        out_line_kernel, [like((2, shard + 16, width), f32), like((2, shard + 16, width), bf16)],
        place, *out_parts,
        scratch=[pltpu.VMEM((4, shard + 16, width), f32)],
    )
    line_far = swap(line_far, ("z",), 1)
    turns.last = line_near
    (final,) = turns.take(final)
    turns.last = grad_inputs = (grad_first + even[:rows] + final.astype(f32)).astype(bf16)
    (line_far,) = turns.take(line_far)
    turns.last = line_sent = (line_near[1] + line_far[1].astype(f32)).astype(bf16)
    line_last = swap(line_sent, ("z",), 2)
    (qkv_sum,) = turns.take(qkv_sum)
    (grad_wqkv,) = local(
        qkv_final_kernel, [like((shard, 3 * width), f32)], place, qkv_sum
    )
    bias_sum = qkv_sum[:, shard].reshape(n_ctx, 3, cols).transpose(1, 0, 2).reshape(3, width)
    bias_own = lax.dynamic_slice(bias_sum, (0, own * shard), (3, shard)).astype(f32)
    turns.last = grad_wqkv
    (line_last,) = turns.take(line_last)
    out_sum = line_near[0] + line_far[0].astype(f32) + line_last.astype(f32)
    thin = out_sum[shard:, :shard]

    return (
        result[None],
        grad_inputs[None],
        grad_wqkv,
        bias_own[0],
        bias_own[2],
        out_sum[:shard],
        thin[0],
        thin[1],
        thin[2],
        grad_wup,
        down_sum[units, :units],
        down_sum[:units],
        thin[3],
        thin[4],
        thin[5],
    )


def call_heads(mesh, *arrays):
    grid = Mesh(mesh.devices.reshape(2, 2, 4, 2), EVERY)
    lines, lone, block = P(EVERY, None), P(EVERY), P(DP, CTX, None)
    in_specs = (
        block, lines, lone, lone, lines, lone, lone, lone, lines, lone, lines, lone, lone, lone,
        P(DP, CTX), P(DP, CTX), block,
    )
    out_specs = (
        block, block, lines, lone, lone, lines, lone, lone, lone, lines, lone, lines, lone, lone,
        lone,
    )
    return jax.shard_map(
        heads_body, mesh=grid, in_specs=in_specs, out_specs=out_specs, check_vma=False
    )(*arrays)


def call(mesh, *arrays):
    if mesh.shape["dp"] == 4 and mesh.shape["ctx"] == 8 and arrays[0].shape[1] == 1024:
        return call_heads(mesh, *arrays)
    return general_call(mesh)(*arrays)


def general_call(mesh):
    in_specs = (
        P("dp", "ctx", None),
        P(("dp", "ctx"), None),
        P(("dp", "ctx")),
        P(("dp", "ctx")),
        P(("dp", "ctx"), None),
        P(("dp", "ctx")),
        P(("dp", "ctx")),
        P(("dp", "ctx")),
        P(("dp", "ctx"), None),
        P(("dp", "ctx")),
        P(("dp", "ctx"), None),
        P(("dp", "ctx")),
        P(("dp", "ctx")),
        P(("dp", "ctx")),
        P("dp", "ctx"),
        P("dp", "ctx"),
        P("dp", "ctx", None),
    )
    out_specs = (
        P("dp", "ctx", None),
        P("dp", "ctx", None),
        P(("dp", "ctx"), None),
        P(("dp", "ctx")),
        P(("dp", "ctx")),
        P(("dp", "ctx"), None),
        P(("dp", "ctx")),
        P(("dp", "ctx")),
        P(("dp", "ctx")),
        P(("dp", "ctx"), None),
        P(("dp", "ctx")),
        P(("dp", "ctx"), None),
        P(("dp", "ctx")),
        P(("dp", "ctx")),
        P(("dp", "ctx")),
    )
    return jax.shard_map(general_body, mesh=mesh, in_specs=in_specs, out_specs=out_specs, check_vma=False)


def solution(mesh):
    return partial(call, mesh)
```

```python
import math
from functools import partial

import jax
import jax.numpy as jnp
from jax import lax
from jax.experimental import pallas as pl
from jax.experimental.pallas import tpu as pltpu
from jax.sharding import Mesh
from jax.sharding import PartitionSpec as P

HEADS = 16
HEAD = 64
WINDOW = 1024


MASKED = -1e30
EPSILON = 1e-05


def layer_norm(values, scales, offsets):
    average = jnp.mean(values, axis=-1, keepdims=True)
    centred = values - average
    variance = jnp.mean(centred * centred, axis=-1, keepdims=True)
    return centred * lax.rsqrt(variance + EPSILON) * scales + offsets


def matmul(left, right):
    return jnp.dot(left, right, preferred_element_type=jnp.float32)


def rows_product(left, right):
    return lax.dot_general(
        left, right, (((0,), (0,)), ((), ())), preferred_element_type=jnp.float32
    )


def cols_product(left, right):
    return lax.dot_general(
        left, right, (((1,), (1,)), ((), ())), preferred_element_type=jnp.float32
    )


def split_heads(matrix):
    return matrix.reshape(matrix.shape[0], HEADS, HEAD)


def allowed_keys(query_tags, query_place, key_tags, key_place):
    same_doc = query_tags[:, None] // 2 == key_tags[None, :] // 2
    distance = jnp.abs(query_place[:, None] - key_place[None, :])
    usable = (key_tags[None, :] % 2 == 1) | (distance == 0)
    return same_doc & (distance <= WINDOW // 2) & usable


def masked_scores(query_block, key_heads, query_tags, query_place, key_tags, key_place):
    raw = (
        jnp.einsum("qhd,khd->hqk", query_block, key_heads, preferred_element_type=jnp.float32)
        * 0.125
    )
    return jnp.where(allowed_keys(query_tags, query_place, key_tags, key_place)[None], raw, MASKED)


def attend_forward(
    query_heads, key_heads, value_heads, query_tags, query_place, key_tags, key_place
):
    row_count = query_heads.shape[0]
    block_rows = min(row_count, 512)

    def one_block(block_index):
        scores = masked_scores(query_heads, key_heads, query_tags, query_place, key_tags, key_place)
        totals = jax.nn.logsumexp(scores, axis=2)
        probs = jnp.exp(scores - totals[:, :, None]).astype(jnp.bfloat16)
        output = jnp.einsum("hqk,khd->qhd", probs, value_heads, preferred_element_type=jnp.float32)
        return (output, totals)

    outputs, totals = lax.map(one_block, jnp.arange(row_count // block_rows, dtype=jnp.int32))
    return (outputs.reshape(row_count, HEADS * HEAD), totals)


def attend_backward(
    query_heads,
    key_heads,
    value_heads,
    grad_heads,
    deltas,
    totals,
    query_tags,
    query_place,
    key_tags,
    key_place,
):
    row_count = query_heads.shape[0]
    block_rows = min(row_count, 512)

    def one_block(running, block_index):
        key_grad, value_grad = running
        scores = masked_scores(query_heads, key_heads, query_tags, query_place, key_tags, key_place)
        probs = jnp.exp(scores - totals[block_index][:, :, None])
        dprobs = jnp.einsum(
            "qhd,khd->hqk", grad_heads, value_heads, preferred_element_type=jnp.float32
        )
        dscores = (probs * (dprobs - deltas[:, :, None])).astype(jnp.bfloat16)
        query_grad = (
            jnp.einsum("hqk,khd->qhd", dscores, key_heads, preferred_element_type=jnp.float32)
            * 0.125
        )
        key_grad = (
            key_grad
            + jnp.einsum("hqk,qhd->khd", dscores, query_heads, preferred_element_type=jnp.float32)
            * 0.125
        )
        value_grad = value_grad + jnp.einsum(
            "hqk,qhd->khd",
            probs.astype(jnp.bfloat16),
            grad_heads,
            preferred_element_type=jnp.float32,
        )
        return ((key_grad, value_grad), query_grad)

    zeros = jnp.zeros(key_heads.shape, jnp.float32)
    (key_grad, value_grad), query_grads = lax.scan(
        one_block, (zeros, zeros), jnp.arange(row_count // block_rows, dtype=jnp.int32)
    )
    key_count = key_heads.shape[0]
    return (
        query_grads.reshape(row_count, HEADS * HEAD),
        key_grad.reshape(key_count, HEADS * HEAD),
        value_grad.reshape(key_count, HEADS * HEAD),
    )


def clip_window(whole, rows_here, seq_length, own_index):
    neighbours = (WINDOW // 2 + rows_here - 1) // rows_here
    key_span = min((2 * neighbours + 1) * rows_here, seq_length)
    first_key = jnp.clip((own_index - neighbours) * rows_here, 0, seq_length - key_span)
    window = tuple((lax.dynamic_slice_in_dim(member, first_key, key_span, 0) for member in whole))
    return (window, first_key)


def window_keys(items, rows_here, seq_length, own_index):
    whole = (
        lax.all_gather(items[0], "ctx", axis=0, tiled=True),
        lax.all_gather(items[1], "ctx", axis=0, tiled=True),
        lax.all_gather(items[2], "ctx", axis=0, tiled=True),
    )
    return clip_window(whole, rows_here, seq_length, own_index)


def window_keys_again(items, rows_here, seq_length, own_index):
    whole = (
        lax.all_gather(items[0], "ctx", axis=0, tiled=True),
        lax.all_gather(items[1], "ctx", axis=0, tiled=True),
        lax.all_gather(items[2], "ctx", axis=0, tiled=True),
    )
    return clip_window(whole, rows_here, seq_length, own_index)


def return_key_grads(key_grad, value_grad, rows_here, first_key):
    width = key_grad.shape[1]
    joined = jnp.concatenate([key_grad, value_grad], axis=1)
    key_span = joined.shape[0]
    count = rows_here * lax.axis_size("ctx")
    padding = jnp.zeros((count, 2 * width), jnp.float32)
    padded = jnp.concatenate([padding, joined, padding], axis=0)
    offset = jnp.clip(jnp.int32(0) - first_key + count, 0, key_span + count)
    summed = lax.psum_scatter(
        lax.dynamic_slice_in_dim(padded, offset, count, 0), "ctx", scatter_dimension=0, tiled=True
    )
    return (summed[:, :width], summed[:, width:])


def general_body(
    tokens,
    w_qkv,
    b_query,
    b_value,
    w_out,
    b_out,
    ln1_gain,
    ln1_bias,
    w_up,
    b_up,
    w_down,
    b_down,
    ln2_gain,
    ln2_bias,
    segment_ids,
    pad_mask,
    cotangent,
):
    weight_shards = (
        w_qkv,
        b_query,
        b_value,
        w_out,
        b_out,
        ln1_gain,
        ln1_bias,
        w_up,
        b_up,
        w_down,
        b_down,
        ln2_gain,
        ln2_bias,
    )
    gathered = (
        lax.all_gather(weight_shards[0], ("dp", "ctx"), axis=0, tiled=True),
        lax.all_gather(weight_shards[1], ("dp", "ctx"), axis=0, tiled=True),
        lax.all_gather(weight_shards[2], ("dp", "ctx"), axis=0, tiled=True),
        lax.all_gather(weight_shards[3], ("dp", "ctx"), axis=0, tiled=True),
        lax.all_gather(weight_shards[4], ("dp", "ctx"), axis=0, tiled=True),
        lax.all_gather(weight_shards[5], ("dp", "ctx"), axis=0, tiled=True),
        lax.all_gather(weight_shards[6], ("dp", "ctx"), axis=0, tiled=True),
        lax.all_gather(weight_shards[7], ("dp", "ctx"), axis=0, tiled=True),
        lax.all_gather(weight_shards[8], ("dp", "ctx"), axis=0, tiled=True),
        lax.all_gather(weight_shards[9], ("dp", "ctx"), axis=0, tiled=True),
        lax.all_gather(weight_shards[10], ("dp", "ctx"), axis=0, tiled=True),
        lax.all_gather(weight_shards[11], ("dp", "ctx"), axis=0, tiled=True),
        lax.all_gather(weight_shards[12], ("dp", "ctx"), axis=0, tiled=True),
    )
    (
        full_qkv,
        full_bquery,
        full_bvalue,
        full_out,
        full_bout,
        full_gain_one,
        full_bias_one,
        full_up,
        full_bup,
        full_down,
        full_bdown,
        full_gain_two,
        full_bias_two,
    ) = gathered
    rows_here = tokens.shape[1]
    seq_length = rows_here * lax.axis_size("ctx")
    own_index = lax.axis_index("ctx")
    inputs = tokens[0]
    inputs_wide = inputs.astype(jnp.float32)
    model_width = inputs.shape[1]
    token_tags = 2 * (segment_ids[0] + 1) + pad_mask[0]
    query_place = own_index * rows_here + jnp.arange(rows_here, dtype=jnp.int32)
    mixed = matmul(inputs, full_qkv)
    queries = (mixed[:, :model_width] + full_bquery.astype(jnp.float32)).astype(jnp.bfloat16)
    keys = mixed[:, model_width : 2 * model_width].astype(jnp.bfloat16)
    values = (mixed[:, 2 * model_width :] + full_bvalue.astype(jnp.float32)).astype(jnp.bfloat16)
    (key_window, value_window, tag_window), first_key = window_keys(
        (keys, values, token_tags), rows_here, seq_length, own_index
    )
    key_place = first_key + jnp.arange(key_window.shape[0], dtype=jnp.int32)
    attended, totals = attend_forward(
        split_heads(queries),
        split_heads(key_window),
        split_heads(value_window),
        token_tags,
        query_place,
        tag_window,
        key_place,
    )
    attended_low = attended.astype(jnp.bfloat16)
    first = inputs_wide + matmul(attended_low, full_out) + full_bout.astype(jnp.float32)
    normed, first_pull = jax.vjp(
        layer_norm, first, full_gain_one.astype(jnp.float32), full_bias_one.astype(jnp.float32)
    )
    normed_low = normed.astype(jnp.bfloat16)
    hidden = matmul(normed_low, full_up) + full_bup.astype(jnp.float32)
    active, gelu_pull = jax.vjp(partial(jax.nn.gelu, approximate=False), hidden)
    active_low = active.astype(jnp.bfloat16)
    second = normed + matmul(active_low, full_down) + full_bdown.astype(jnp.float32)
    result, second_pull = jax.vjp(
        layer_norm, second, full_gain_two.astype(jnp.float32), full_bias_two.astype(jnp.float32)
    )
    gathered = (
        lax.all_gather(weight_shards[0], ("dp", "ctx"), axis=0, tiled=True),
        lax.all_gather(weight_shards[1], ("dp", "ctx"), axis=0, tiled=True),
        lax.all_gather(weight_shards[2], ("dp", "ctx"), axis=0, tiled=True),
        lax.all_gather(weight_shards[3], ("dp", "ctx"), axis=0, tiled=True),
        lax.all_gather(weight_shards[4], ("dp", "ctx"), axis=0, tiled=True),
        lax.all_gather(weight_shards[5], ("dp", "ctx"), axis=0, tiled=True),
        lax.all_gather(weight_shards[6], ("dp", "ctx"), axis=0, tiled=True),
        lax.all_gather(weight_shards[7], ("dp", "ctx"), axis=0, tiled=True),
        lax.all_gather(weight_shards[8], ("dp", "ctx"), axis=0, tiled=True),
        lax.all_gather(weight_shards[9], ("dp", "ctx"), axis=0, tiled=True),
        lax.all_gather(weight_shards[10], ("dp", "ctx"), axis=0, tiled=True),
        lax.all_gather(weight_shards[11], ("dp", "ctx"), axis=0, tiled=True),
        lax.all_gather(weight_shards[12], ("dp", "ctx"), axis=0, tiled=True),
    )
    back_qkv = gathered[0]
    back_out = gathered[3]
    back_up = gathered[7]
    back_down = gathered[9]
    grad_second, grad_gain_two, grad_bias_two = second_pull(cotangent[0].astype(jnp.float32))
    grad_outcome = grad_second.astype(jnp.bfloat16)
    grad_wdown = rows_product(active_low, grad_outcome)
    grad_bdown = jnp.sum(grad_outcome.astype(jnp.float32), axis=0)
    (grad_active,) = gelu_pull(cols_product(grad_outcome, back_down))
    grad_hidden = grad_active.astype(jnp.bfloat16)
    grad_wup = rows_product(normed_low, grad_hidden)
    grad_bup = jnp.sum(grad_hidden.astype(jnp.float32), axis=0)
    grad_normed = grad_second + cols_product(grad_hidden, back_up)
    grad_first, grad_gain_one, grad_bias_one = first_pull(grad_normed)
    grad_branch = grad_first.astype(jnp.bfloat16)
    grad_wout = rows_product(attended_low, grad_branch)
    grad_bout = jnp.sum(grad_branch.astype(jnp.float32), axis=0)
    grad_attended = cols_product(grad_branch, back_out).astype(jnp.bfloat16)
    deltas = jnp.sum(
        (grad_attended.astype(jnp.float32) * attended).reshape(rows_here, HEADS, HEAD), axis=2
    ).T
    (key_again, value_again, tag_again), first_again = window_keys_again(
        (keys, values, token_tags), rows_here, seq_length, own_index
    )
    place_again = first_again + jnp.arange(key_again.shape[0], dtype=jnp.int32)
    grad_queries, key_grad, value_grad = attend_backward(
        split_heads(queries),
        split_heads(key_again),
        split_heads(value_again),
        split_heads(grad_attended),
        deltas,
        totals,
        token_tags,
        query_place,
        tag_again,
        place_again,
    )
    key_total, value_total = return_key_grads(key_grad, value_grad, rows_here, first_again)
    grad_query_low = grad_queries.astype(jnp.bfloat16)
    grad_value_low = value_total.astype(jnp.bfloat16)
    grad_mixed = jnp.concatenate(
        [grad_query_low, key_total.astype(jnp.bfloat16), grad_value_low], axis=1
    )
    grad_wqkv = rows_product(inputs, grad_mixed)
    grad_bquery = jnp.sum(grad_query_low.astype(jnp.float32), axis=0)
    grad_bvalue = jnp.sum(grad_value_low.astype(jnp.float32), axis=0)
    grad_inputs = grad_first + cols_product(grad_mixed, back_qkv)
    summed = (
        lax.psum_scatter(grad_wqkv, ("dp", "ctx"), scatter_dimension=0, tiled=True),
        lax.psum_scatter(grad_bquery, ("dp", "ctx"), scatter_dimension=0, tiled=True),
        lax.psum_scatter(grad_bvalue, ("dp", "ctx"), scatter_dimension=0, tiled=True),
        lax.psum_scatter(grad_wout, ("dp", "ctx"), scatter_dimension=0, tiled=True),
        lax.psum_scatter(grad_bout, ("dp", "ctx"), scatter_dimension=0, tiled=True),
        lax.psum_scatter(grad_gain_one, ("dp", "ctx"), scatter_dimension=0, tiled=True),
        lax.psum_scatter(grad_bias_one, ("dp", "ctx"), scatter_dimension=0, tiled=True),
        lax.psum_scatter(grad_wup, ("dp", "ctx"), scatter_dimension=0, tiled=True),
        lax.psum_scatter(grad_bup, ("dp", "ctx"), scatter_dimension=0, tiled=True),
        lax.psum_scatter(grad_wdown, ("dp", "ctx"), scatter_dimension=0, tiled=True),
        lax.psum_scatter(grad_bdown, ("dp", "ctx"), scatter_dimension=0, tiled=True),
        lax.psum_scatter(grad_gain_two, ("dp", "ctx"), scatter_dimension=0, tiled=True),
        lax.psum_scatter(grad_bias_two, ("dp", "ctx"), scatter_dimension=0, tiled=True),
    )
    return (
        result.astype(jnp.bfloat16)[None],
        grad_inputs.astype(jnp.bfloat16)[None],
        summed[0],
        summed[1],
        summed[2],
        summed[3],
        summed[4],
        summed[5],
        summed[6],
        summed[7],
        summed[8],
        summed[9],
        summed[10],
        summed[11],
        summed[12],
    )


GROUP = ("y", "core", "x")
CTX = ("z", "x")
DP = ("y", "core")
EVERY = ("y", "core", "z", "x")
bf16, f32 = jnp.bfloat16, jnp.float32


def swap(member, axes, code):
    count = 1
    for axis in axes:
        count *= lax.axis_size(axis)
    return lax.ppermute(member, axes, [(place, place ^ code) for place in range(count)])


def after(member, *events):
    return lax.optimization_barrier((member,) + events)[0]


class Turns:
    def __init__(self, last):
        self.last = last

    def take(self, *members):
        return lax.optimization_barrier((*members, self.last))[:-1]


def like(shape, kind):
    return jax.ShapeDtypeStruct(shape, kind)


def staged(kernel, groups, results, lazy, place, *refs):
    count = sum(groups)
    given, refs = refs[:count], refs[count:]
    out, refs = list(refs[: len(results)]), refs[len(results) :]
    held, refs = refs[: len(groups)], refs[len(groups) :]
    staging, refs = refs[: sum(results)], refs[sum(results) :]
    (arrived, left), refs = refs[:2], refs[2:]
    copies, index, first = [], 0, []
    for size, target in zip(groups, held):
        first.append(index)
        rows = target.shape[0] // size
        for member in range(size):
            part = target if size == 1 else target.at[pl.ds(member * rows, rows)]
            copies.append(pltpu.make_async_copy(given[index], part, arrived.at[index]))
            index += 1
    for copy in copies:
        copy.start()
    if lazy:
        arrivals = copies
        kernel = partial(kernel, lambda group, member=0: arrivals[first[group] + member].wait())
    else:
        for copy in copies:
            copy.wait()
    copies, index = [], 0
    for i, far in enumerate(results):
        if far:
            copies.append(pltpu.make_async_copy(staging[index], out[i], left.at[index]))
            out[i] = staging[index]
            index += 1
    kernel(place, *held, *out, *refs)
    for copy in copies:
        copy.start()
    for copy in copies:
        copy.wait()


def bytes_of(v):
    return math.prod(v.shape) * jnp.dtype(v.dtype).itemsize


def local(kernel, outs, place, *operands, scratch=(), far=False, keep=(), lazy=False, cost=0):
    near = pl.BlockSpec(memory_space=pltpu.VMEM)
    groups = [v if isinstance(v, (tuple, list)) else (v,) for v in operands]
    operands = [v for group in groups for v in group]
    size = sum(bytes_of(v) for v in (*operands, *outs, *scratch))
    results = [far and i not in keep for i in range(len(outs))]
    if far:
        kernel = partial(staged, kernel, [len(group) for group in groups], results, lazy)
        held = [
            pltpu.VMEM((len(g) * g[0].shape[0],) + g[0].shape[1:], g[0].dtype) for g in groups
        ]
        held += [pltpu.VMEM(v.shape, v.dtype) for v, out in zip(outs, results) if out]
        held += [pltpu.SemaphoreType.DMA((len(operands),))]
        held += [pltpu.SemaphoreType.DMA((max(sum(results), 1),))]
        scratch = held + list(scratch)
        operands = [pltpu.with_memory_space_constraint(v, pltpu.HBM) for v in operands]
        outs = [pltpu.HBM(v.shape, v.dtype) if out else v for v, out in zip(outs, results)]
    hbm = pl.BlockSpec(memory_space=pltpu.HBM)
    return pl.pallas_call(
        kernel,
        out_shape=list(outs),
        in_specs=[pl.BlockSpec(memory_space=pltpu.SMEM)] + [hbm if far else near] * len(operands),
        out_specs=[hbm if out else near for out in results],
        scratch_shapes=list(scratch),
        cost_estimate=pl.CostEstimate(flops=cost * 10**9, bytes_accessed=0, transcendentals=0),
        compiler_params=pltpu.CompilerParams(vmem_limit_bytes=size + ((24 if cost > 8 else 6) << 20)),
    )(place, *operands)


def pair_product(left, right):
    return lax.dot_general(
        left, right, (((0,), (0,)), ((), ())), preferred_element_type=jnp.float32
    )


def plane_gather(block):
    return [block] + [swap(block, ("y", "x"), code) for code in range(1, 4)]


def group_gather(block):
    plane = plane_gather(block)
    return plane + [swap(member, ("core",), 1) for member in plane]


def merge_kernel(place, near, far, own, *sent):
    rows = own.shape[0]
    for code in range(4):
        part = pl.ds(code * rows, rows)
        total = near[part, :].astype(f32) + far[part, :].astype(f32)
        if code == 0:
            own[...] = total
        else:
            sent[code - 1][...] = total.astype(bf16)


def group_scatter(near, far, place, event=None):
    crossed = swap(far, ("core",), 1)
    if event is not None:
        crossed = after(crossed, event)
    return plane_scatter(near, crossed, place)


def plane_scatter(near, crossed, place):
    rows, width = near.shape[0] // 4, near.shape[1]
    outs = [like((rows, width), f32)] + [like((rows, width), bf16)] * 3
    own, *sent = local(merge_kernel, outs, place, near, crossed)
    parts = [own] + [swap(sent[code - 1], ("y", "x"), code) for code in range(1, 4)]
    return parts


def ctx_gather(block):
    two, one = swap(block, ("z",), 2), swap(block, ("z",), 1)
    line = [block, one, two, swap(two, ("z",), 1)]
    blocks = [piece for member in line[:3] for piece in (member, swap(member, ("x",), 1))]
    return blocks + [line[3]]


def pack_kernel(place, w_qkv, w_up, *refs):
    vectors, (b_up, segments, pads, qkv_ref, up_ref) = refs[:8], refs[8:]
    groups, _, wide = qkv_ref.shape
    shard, cols = w_qkv.shape[0], wide // 3
    tags = (2 * (segments[...] + 1) + pads[...]).astype(f32)
    lone = jnp.concatenate([v[...].astype(f32) for v in vectors], axis=0)
    lone = jnp.concatenate([lone, jnp.zeros((8, 128 - shard), f32)], axis=1)
    small = jnp.concatenate([lone, b_up[...].astype(f32), tags, jnp.zeros((6, 128), f32)], axis=0)
    small = jnp.concatenate([small, jnp.zeros((16, wide - 128), f32)], axis=1).astype(bf16)
    for c in range(groups):
        for kind in range(3):
            at = (kind * groups + c) * cols
            qkv_ref[c, :shard, kind * cols : (kind + 1) * cols] = w_qkv[:, at : at + cols]
        qkv_ref[c, shard:, :] = small
    units = b_up.shape[1]
    for g in range(8):
        for z in range(4):
            at = ((g // 2 * 4 + z) * 2 + g % 2) * units
            up_ref[g, :, z * units : (z + 1) * units] = w_up[:, at : at + units]


def out_gather(block, *events):
    pair = after(jnp.stack([block, swap(block, ("z",), 1)]), events[0])
    line = after(jnp.concatenate([pair, swap(pair, ("z",), 2)]), events[1])
    both = after(jnp.stack([line, swap(line, ("y",), 1)]), events[2])
    far = swap(both, ("x",), 1)
    both, far = after(both, events[3]), after(far, events[3])
    return [both, far, swap(both, ("core",), 1), swap(far, ("core",), 1)]


def order_out_kernel(place, p00, p01, p10, p11, out_ref):
    rows = p00.shape[2]
    own = place[0]
    for core in range(2):
        for x in range(2):
            piece = ((p00, p01), (p10, p11))[core][x]
            for y in range(2):
                for z in range(4):
                    at = own ^ (y * 16 + core * 8 + z * 2 + x)
                    out_ref[pl.ds(at * rows, rows), :] = piece[y, z]


def order_kernel(place, *refs):
    up_refs, down_refs, (up_out, down_out) = refs[:4], refs[4:8], refs[8:]
    rows, units = up_out.shape[0] // 32, down_refs[0].shape[0]
    own_z = place[3]
    for z in range(4):
        down_out[pl.ds((own_z ^ z) * units, units), :] = down_refs[z][...]
        for j in range(8):
            at = (j // 2 * 4 + (own_z ^ z)) * 2 + j % 2
            up_out[pl.ds(at * rows, rows), :] = up_refs[z][pl.ds(j * rows, rows), :]


def allowed_here(query_tags, query_place, key_tags, key_place):
    same_doc = (query_tags >> 1) == (key_tags >> 1)
    distance = jnp.abs(query_place - key_place)
    usable = ((key_tags & 1) == 1) | (distance == 0)
    return same_doc & (distance <= WINDOW // 2) & usable


def places(own_ctx, rows, shape, axis, start=0):
    index = lax.broadcasted_iota(jnp.int32, shape, axis) + start
    return ((index // rows) ^ own_ctx) * rows + index % rows


def attend_kernel(ready, place, *refs, n_blocks, rows, cols):
    pieces, refs = refs[:4], refs[4:]
    bias, tags_row, lines, q_ref, k_ref, v_ref, att_ref, msg_ref, lse_ref, qkv_ref = refs
    own_dp, own_ctx = place[1], place[2]
    shard = 32
    for m, piece in enumerate(pieces):
        ready(m)
        for c in range(n_blocks):
            at = ((own_dp ^ m) * n_blocks + c) * shard
            qkv_ref[pl.ds(at, shard), :] = piece[c, :shard, :]
    ready(4)
    ready(5)
    for j in range(n_blocks // 2):
        part = pl.ds(j * 2 * rows, 2 * rows)
        ready(6, 2 * j)
        ready(6, 2 * j + 1)
        mixed = matmul(lines[part, :], qkv_ref[...]) + bias[...]
        q_ref[part, :] = mixed[:, :cols].astype(bf16)
        k_ref[part, :] = mixed[:, cols : 2 * cols].astype(bf16)
        v_ref[part, :] = mixed[:, 2 * cols :].astype(bf16)
    length = n_blocks * rows
    chunk = 2 * rows

    def step(index, carry):
        part = pl.ds(index * chunk, chunk)
        allowed = allowed_here(
            jnp.broadcast_to(tags_row[:, part], (128, chunk)).T[:, :1],
            places(own_ctx, rows, (chunk, 1), 0, index * chunk),
            tags_row[...],
            places(own_ctx, rows, (1, length), 1),
        )
        found = []
        for head in range(cols // HEAD):
            lanes = slice(head * HEAD, (head + 1) * HEAD)
            scores = cols_product(q_ref[part, lanes], k_ref[:, lanes]) * 0.125
            scores = jnp.where(allowed, scores, MASKED)
            top = jnp.max(scores, axis=1, keepdims=True)
            weights = jnp.exp(scores - top)
            mass = jnp.sum(weights, axis=1, keepdims=True)
            found.append(matmul(weights.astype(bf16), v_ref[:, lanes]) / mass)
            total = top + jnp.log(mass)
            lse_ref[pl.ds(head, 1), part] = jnp.broadcast_to(total, (chunk, 128)).T[:1, :]
        attended = jnp.concatenate(found, axis=1)
        att_ref[part, :] = attended
        for half in range(2):
            at = ((index * 2 + half) ^ own_ctx) * rows
            msg_ref[pl.ds(at, rows), :] = attended[half * rows : (half + 1) * rows].astype(bf16)
        return carry

    lax.fori_loop(0, length // chunk, step, 0, unroll=True)


def branch_kernel(
    place, moved, w_out, inputs, vectors, normed_ref, low_ref, hat_ref, rate_ref
):
    groups, rows, cols = moved.shape
    total = inputs[...].astype(f32) + vectors[2:3, :]
    for c in range(groups):
        total = total + matmul(moved[c], w_out[pl.ds(c * cols, cols), :])
    centred = total - jnp.mean(total, axis=1, keepdims=True)
    rate = lax.rsqrt(jnp.mean(centred * centred, axis=1, keepdims=True) + EPSILON)
    hat = centred * rate
    normed = hat * vectors[3:4, :] + vectors[4:5, :]
    normed_ref[...] = normed
    low_ref[...] = normed.astype(bf16)
    hat_ref[...] = hat
    rate_ref[...] = jnp.broadcast_to(rate, rate_ref.shape)


def forward_kernel(ready, place, up, bias, lines, down, hidden_ref, active_ref, near, far):
    rows = lines.shape[0] // 4
    ready(0)
    ready(1)
    for quarter in range(4):
        part = pl.ds(quarter * rows, rows)
        ready(2, 2 * quarter)
        ready(2, 2 * quarter + 1)
        hidden = matmul(lines[part, :], up[...]) + bias[...]
        hidden_ref[part, :] = hidden
        active = (0.5 * hidden * (1 + lax.erf(hidden * 0.7071067811865476))).astype(bf16)
        active_ref[part, :] = active
        if quarter == 0:
            ready(3)
        target = near if quarter < 2 else far
        target[pl.ds(quarter % 2 * rows, rows), :] = matmul(active, down[...]).astype(bf16)


def second_kernel(
    place, normed, own, p1, p2, p3, vectors, cotangent, result_ref, grad_ref, low_ref, sums_ref
):
    second = normed[...] + own[...] + p1[...].astype(f32) + p2[...].astype(f32)
    second = second + p3[...].astype(f32) + vectors[5:6, :]
    centred = second - jnp.mean(second, axis=1, keepdims=True)
    rate = lax.rsqrt(jnp.mean(centred * centred, axis=1, keepdims=True) + EPSILON)
    hat = centred * rate
    gain = vectors[6:7, :]
    result_ref[...] = (hat * gain + vectors[7:8, :]).astype(bf16)
    grad = cotangent[...].astype(f32)
    scaled = grad * gain
    mean_scaled = jnp.mean(scaled, axis=1, keepdims=True)
    mean_hat = jnp.mean(scaled * hat, axis=1, keepdims=True)
    grad_second = rate * (scaled - mean_scaled - hat * mean_hat)
    grad_ref[...] = grad_second
    low = grad_second.astype(bf16)
    low_ref[...] = low
    sums_ref[0:1, :] = jnp.sum(low.astype(f32), axis=0, keepdims=True)
    sums_ref[1:2, :] = jnp.sum(grad * hat, axis=0, keepdims=True)
    sums_ref[2:3, :] = jnp.sum(grad, axis=0, keepdims=True)


def backward_kernel(place, *refs):
    blocks = refs[:8]
    up, down, slope, grad_ref, near, far = refs[8:]
    rows = blocks[0].shape[0]
    for pair in range(4):
        lines = jnp.concatenate([blocks[2 * pair][...], blocks[2 * pair + 1][...]], axis=0)
        part = pl.ds(pair * 2 * rows, 2 * rows)
        grad = (slope[part, :] * cols_product(lines, down[...])).astype(bf16)
        grad_ref[part, :] = grad
        target = near if pair < 2 else far
        target[pl.ds(pair % 2 * 2 * rows, 2 * rows), :] = cols_product(grad, up[...]).astype(bf16)


def down_grad_kernel(place, lines, active, grad_hidden, near, far, parts):
    width = lines.shape[1]
    shard = active.shape[1] // 4
    total = jnp.sum(grad_hidden[...].astype(f32), axis=0, keepdims=True)
    for z in range(4):
        part = slice(z * shard, (z + 1) * shard)
        at = place[3] ^ z
        parts[at, :shard, :] = pair_product(active[:, part], lines[...]).astype(bf16)
        parts[at, shard:, :shard] = jnp.broadcast_to(total[:, part], (16, shard)).astype(bf16)
        parts[at, shard:, shard:] = jnp.zeros((16, width - shard), bf16)
    for half in range(2):
        near[half], far[half] = parts[2 * half], parts[2 * half + 1]


def up_grad_kernel(place, lines, grad_hidden, near, far, parts):
    own_z = place[3]
    for quarter in range(4):
        span = 8 * 32
        part = slice(quarter * span, (quarter + 1) * span)
        found = pair_product(lines[:, part], grad_hidden[...]).astype(bf16)
        for z in range(4):
            for x in range(2):
                piece = found[(z * 2 + x) * 32 : (z * 2 + x + 1) * 32]
                parts[own_z ^ z, pl.ds((quarter * 2 + x) * 32, 32), :] = piece
    for half in range(2):
        near[half], far[half] = parts[2 * half], parts[2 * half + 1]


def first_kernel(
    place, grad_second, own, p1, p2, p3, vectors, hat_ref, rate_ref, w_out, grad_ref, low_ref,
    msg_ref, sums_ref,
):
    grad = grad_second[...] + own[...] + p1[...].astype(f32) + p2[...].astype(f32)
    grad = grad + p3[...].astype(f32)
    hat = hat_ref[...]
    scaled = grad * vectors[3:4, :]
    mean_scaled = jnp.mean(scaled, axis=1, keepdims=True)
    mean_hat = jnp.mean(scaled * hat, axis=1, keepdims=True)
    grad_first = rate_ref[:, :1] * (scaled - mean_scaled - hat * mean_hat)
    grad_ref[...] = grad_first
    low = grad_first.astype(bf16)
    low_ref[...] = low
    groups, rows, cols = msg_ref.shape
    for c in range(groups):
        msg_ref[c] = cols_product(low, w_out[pl.ds(c * cols, cols), :]).astype(bf16)
    sums_ref[0:1, :] = jnp.sum(low.astype(f32), axis=0, keepdims=True)
    sums_ref[1:2, :] = jnp.sum(grad * hat, axis=0, keepdims=True)
    sums_ref[2:3, :] = jnp.sum(grad, axis=0, keepdims=True)


def out_grad_kernel(place, moved, low, sums_one, sums_two, near, far, parts):
    groups, rows, cols = moved.shape
    high, width = parts.shape[1:]
    own_y, own_core, own_x = place[4], place[5], place[6]
    sums = [sums_one[0:3, :], sums_two[0:3, :], jnp.zeros((high - rows - 6, width), f32)]
    sums = jnp.concatenate(sums, axis=0).astype(bf16)
    for c in range(groups):
        found = pair_product(moved[c], low[...]).astype(bf16)
        for m in range(4):
            y, core, z, x = c // 4, c // 2 % 2, c % 2 * 2 + m // 2, m % 2
            code = (core ^ own_core) * 4 + (y ^ own_y) * 2 + (x ^ own_x)
            parts[code, pl.ds(z * 32, 32), :] = found[m * 32 : (m + 1) * 32]
            lanes = slice((c * 4 + m) * 32, (c * 4 + m + 1) * 32)
            parts[code, rows:, z * 32 : (z + 1) * 32] = sums[:, lanes]
    for code in range(4):
        near[pl.ds(code * high, high), :] = parts[code]
        far[pl.ds(code * high, high), :] = parts[code + 4]


def out_line_kernel(place, own, p1, p2, p3, near, far, parts):
    total = own[...] + p1[...].astype(f32) + p2[...].astype(f32) + p3[...].astype(f32)
    own_z = place[3]
    parts[...] = jnp.zeros(parts.shape, f32)
    for z in range(4):
        at = own_z ^ z
        parts[at, :32, :] = total[z * 32 : (z + 1) * 32]
        parts[at, 32:, :32] = total[128:, z * 32 : (z + 1) * 32]
    for half in range(2):
        near[half], far[half] = parts[2 * half], parts[2 * half + 1].astype(bf16)


def attend_grad_kernel(
    place, *refs,
):
    moved, q_ref, k_ref, v_ref, att_ref, lse_ref, tags_row, *refs = refs
    mixed_ref, key_grad, value_grad, back = refs
    groups, rows, cols = moved.shape
    length = groups * rows
    own_ctx = place[2]
    for j in range(groups):
        back[pl.ds(j * rows, rows), :] = moved[own_ctx ^ j]
    key_grad[...] = jnp.zeros(key_grad.shape, f32)
    value_grad[...] = jnp.zeros(value_grad.shape, f32)
    chunk = 2 * rows
    tags_col = jnp.broadcast_to(tags_row[...], (128, length)).T[:, :1]

    def step(index, carry):
        part = pl.ds(index * chunk, chunk)
        allowed = allowed_here(
            tags_row[:, part],
            places(own_ctx, rows, (1, chunk), 1, index * chunk),
            tags_col,
            places(own_ctx, rows, (length, 1), 0),
        )
        weighted = (back[part, :].astype(f32) * att_ref[part, :]).T
        found = []
        for head in range(cols // HEAD):
            lanes = slice(head * HEAD, (head + 1) * HEAD)
            delta = jnp.sum(weighted[lanes, :], axis=0, keepdims=True)
            scores = cols_product(k_ref[:, lanes], q_ref[part, lanes]) * 0.125
            probs = jnp.where(allowed, jnp.exp(scores - lse_ref[pl.ds(head, 1), part]), 0.0)
            grads = cols_product(v_ref[:, lanes], back[part, lanes])
            grads = (probs * (grads - delta)).astype(bf16)
            value_grad[:, lanes] += matmul(probs.astype(bf16), back[part, lanes])
            key_grad[:, lanes] += matmul(grads, q_ref[part, lanes])
            found.append(pair_product(grads, k_ref[:, lanes]) * 0.125)
        mixed_ref[part, :cols] = jnp.concatenate(found, axis=1).astype(bf16)
        return carry

    lax.fori_loop(0, length // chunk, step, 0, unroll=True)
    mixed_ref[:, cols : 2 * cols] = (key_grad[...] * 0.125).astype(bf16)
    mixed_ref[:, 2 * cols :] = value_grad[...].astype(bf16)


def leave_kernel(place, *refs):
    mixed_ref, qkv_ref, even_near, even_far, odd_near, odd_far = refs
    messages = ((even_near, even_far), (odd_near, odd_far))
    groups, rows = 8, mixed_ref.shape[0] // 8
    for j in range(groups):
        part = cols_product(mixed_ref[pl.ds(j * rows, rows), :], qkv_ref[...])
        target = messages[j // 2 % 2][j % 2]
        target[pl.ds(j // 4 * rows, rows), :] = part.astype(bf16)


def qkv_grad_kernel(place, lines, mixed_ref, near, far):
    own_dp = place[1]
    cols = mixed_ref.shape[1] // 3
    sums = jnp.sum(mixed_ref[...].astype(f32), axis=0, keepdims=True)
    sums = jnp.broadcast_to(sums, (16, 3 * cols)).astype(bf16)
    span = lines.shape[1] // 4
    for ky in range(2):
        for kc in range(2):
            start = pl.multiple_of((own_dp ^ (ky * 2 + kc)) * span, span)
            found = pair_product(lines[:, pl.ds(start, span)], mixed_ref[...]).astype(bf16)
            target = far if kc else near
            target[ky, :span, :] = found
            target[ky, span:, :] = sums


def up_final_kernel(place, moved, out):
    groups, shard, wide = moved.shape
    units = wide // 4
    for g in range(groups):
        for z in range(4):
            at = ((g // 2 * 4 + z) * 2 + g % 2) * units
            out[:, at : at + units] = moved[g, :, z * units : (z + 1) * units].astype(f32)


def qkv_final_kernel(place, moved, out):
    groups, _, wide = moved.shape
    shard, cols = out.shape[0], wide // 3
    for c in range(groups):
        for kind in range(3):
            at = (kind * groups + c) * cols
            out[:, at : at + cols] = moved[c, :shard, kind * cols : (kind + 1) * cols].astype(f32)


def heads_body(
    tokens, w_qkv, b_query, b_value, w_out, b_out, ln1_gain, ln1_bias, w_up, b_up, w_down, b_down,
    ln2_gain, ln2_bias, segment_ids, pad_mask, cotangent,
):
    inputs = tokens[0]
    rows, width = inputs.shape
    n_ctx = lax.axis_size(CTX)
    n_dp = lax.axis_size(DP)
    n_z = lax.axis_size("z")
    length = rows * n_ctx
    cols = width // n_ctx
    shard = w_qkv.shape[0]
    units = w_down.shape[0]
    wide = n_z * units
    own_ctx = lax.axis_index(CTX)
    own_dp = lax.axis_index(DP)
    own = lax.axis_index(EVERY)
    place = jnp.stack(
        [own, own_dp, own_ctx, lax.axis_index("z")] + [lax.axis_index(a) for a in GROUP]
    ).astype(jnp.int32)

    vectors = (b_query, b_value, b_out, ln1_gain, ln1_bias, b_down, ln2_gain, ln2_bias)
    qkv_parts, up_parts = local(
        pack_kernel,
        [like((n_ctx, shard + 16, 3 * cols), bf16), like((8, shard, wide), bf16)],
        place, w_qkv, w_up, *[v[None] for v in vectors], b_up[None], segment_ids, pad_mask,
        far=True,
    )
    blocks = ctx_gather(inputs)
    qkv = after(qkv_parts, blocks[1], blocks[2])
    qkv = lax.all_to_all(qkv, CTX, 0, 0, tiled=True)
    blocks.append(swap(blocks[6], ("x",), 1))
    qkv_y = swap(after(qkv, blocks[6]), ("y",), 1)
    qkv_c, qkv_y = after(qkv, blocks[5]), after(qkv_y, blocks[5])
    pieces = [qkv, swap(qkv_c, ("core",), 1), qkv_y, swap(qkv_y, ("core",), 1)]
    up = after(up_parts.reshape(8 * shard, wide), qkv)
    up = lax.all_to_all(up, GROUP, 0, 0, tiled=True)
    small = jnp.stack([piece[:, shard : shard + 10, :128] for piece in pieces])
    small = jnp.take(small, own_dp ^ jnp.arange(n_dp), axis=0).reshape(n_dp * n_ctx, 10, 128)
    vectors = small[:, :8, :shard].transpose(1, 0, 2).reshape(8, width).astype(f32)
    bias_up = small[:, 8].reshape(n_dp, n_z, 2, units)
    bias_up = lax.dynamic_slice(bias_up, (own_dp, 0, lax.axis_index("x"), 0), (1, n_z, 1, units))
    bias_up = bias_up.reshape(1, wide).astype(f32)
    tags = lax.dynamic_slice(small[:, 9], (own_dp * n_ctx, 0), (n_ctx, rows)).astype(jnp.int32)
    tags_row = jnp.take(tags, own_ctx ^ jnp.arange(n_ctx), axis=0).reshape(1, length)
    bias = lax.dynamic_slice(vectors, (0, own_ctx * cols), (2, cols))
    bias = jnp.concatenate([bias[:1], jnp.zeros((1, cols), f32), bias[1:]], axis=1)

    down = after(w_down, blocks[6])
    down_z = swap(down, ("z",), 2)
    down_lines = [down, swap(down, ("z",), 1), down_z, swap(down_z, ("z",), 1)]
    queries, keys, values, attended, message, totals, full_qkv = local(
        partial(attend_kernel, n_blocks=n_ctx, rows=rows, cols=cols),
        [like((length, cols), bf16)] * 3
        + [
            like((length, cols), f32),
            like((length, cols), bf16),
            like((8, length), f32),
            like((width, 3 * cols), bf16),
        ],
        place, *pieces, after(bias, down_z, down_lines[1]), tags_row, blocks, far=True, lazy=True,
        cost=10,
    )
    up_z = swap(up, ("z",), 2)
    up_lines = [up, swap(up, ("z",), 1), up_z, swap(up_z, ("z",), 1)]
    (full_out,) = local(
        order_out_kernel, [like((width, width), bf16)], place,
        *out_gather(after(w_out, blocks[2]), blocks[4], qkv, blocks[7], message), far=True,
        keep=(0,),
    )
    moved = lax.all_to_all(message, CTX, 0, 0, tiled=True).reshape(n_ctx, rows, cols)
    normed, normed_low, hat, rate = local(
        branch_kernel,
        [like((rows, width), f32), like((rows, width), bf16), like((rows, width), f32)]
        + [like((rows, 128), f32)],
        place, moved, full_out, inputs, vectors,
    )
    normed_all = group_gather(normed_low)
    full_up, down = local(
        order_kernel, [like((width, wide), bf16), like((wide, width), bf16)], place,
        after(up_lines[0], normed_all[1]), *up_lines[1:], *down_lines, far=True,
    )
    hidden, active, near, far = local(
        forward_kernel,
        [like((8 * rows, wide), f32), like((8 * rows, wide), bf16)]
        + [like((4 * rows, width), bf16)] * 2,
        place, full_up, bias_up, normed_all, down, far=True, keep=(0, 2, 3), lazy=True,
    )
    parts = group_scatter(near, far, place)
    hidden = after(hidden, parts[1])
    result, grad_second, grad_z, sums_two = local(
        second_kernel,
        [like((rows, width), bf16), like((rows, width), f32), like((rows, width), bf16)]
        + [like((8, width), f32)],
        place, normed, *parts, vectors, cotangent[0],
    )

    slope = 0.5 * (1 + lax.erf(hidden * 0.7071067811865476)) + hidden * (
        jnp.exp(-0.5 * hidden * hidden) * 0.3989422804014327
    )
    grad_z_all = group_gather(grad_z)
    grad_hidden, near, far = local(
        backward_kernel,
        [like((8 * rows, wide), bf16)] + [like((4 * rows, width), bf16)] * 2,
        place, *grad_z_all, full_up, down, slope,
    )
    down_near, down_far = local(
        down_grad_kernel, [like((2, units + 16, width), bf16)] * 2,
        place, grad_z_all, active, grad_hidden, far=True,
        scratch=[pltpu.VMEM((4, units + 16, width), bf16)],
    )
    parts = group_scatter(near, far, place, down_near)
    down_far = swap(down_far, ("z",), 1)
    up_near, up_far = local(
        up_grad_kernel, [like((2, 8 * shard, wide), bf16)] * 2,
        place, normed_all, after(grad_hidden, parts[1]), far=True,
        scratch=[pltpu.VMEM((4, 8 * shard, wide), bf16)],
    )
    grad_first, grad_branch, message, sums_one = local(
        first_kernel,
        [like((rows, width), f32), like((rows, width), bf16), like((n_ctx, rows, cols), bf16)]
        + [like((8, width), f32)],
        place, after(grad_second, up_near), *parts, vectors, hat, rate, full_out,
    )
    grad_moved = lax.all_to_all(message, CTX, 0, 0, tiled=True)
    high = rows + 16
    near, far = local(
        out_grad_kernel, [like((4 * high, width), bf16)] * 2, place, moved, grad_branch, sums_one,
        sums_two, far=True, scratch=[pltpu.VMEM((8, high, width), bf16)],
    )
    out_near, out_far = near, swap(far, ("core",), 1)
    turns = Turns(near)
    (down_far,) = turns.take(down_far)
    turns.last = down_sent = (down_near[1].astype(f32) + down_far[1].astype(f32)).astype(bf16)
    (grad_moved,) = turns.take(grad_moved)
    (mixed,) = local(
        attend_grad_kernel, [like((length, 3 * cols), bf16)],
        place, grad_moved, queries, keys, values, attended, totals, tags_row,
        far=True, cost=14,
        scratch=[
            pltpu.VMEM((length, cols), f32),
            pltpu.VMEM((length, cols), f32),
            pltpu.VMEM((length, cols), bf16),
        ],
    )
    up_far = swap(after(up_far, grad_moved), ("z",), 1)
    mixed = after(mixed, out_far)
    even_near, even_far, odd_near, odd_far = local(
        leave_kernel, [like((2 * rows, width), bf16)] * 4, place, mixed, full_qkv, far=True,
        cost=3,
    )
    near, far = local(
        qkv_grad_kernel, [like((2, width // 4 + 16, 3 * cols), bf16)] * 2,
        place, blocks, after(mixed, odd_near), far=True, cost=4,
    )

    odd_far, far, down_last = swap(odd_far, ("x",), 1), swap(far, ("core",), 1), swap(down_sent, ("z",), 2)
    turns = Turns(near)
    down_last, up_far = turns.take(down_last, up_far)
    up_sent = (up_near[1].astype(f32) + up_far[1].astype(f32)).astype(bf16)
    up_last = swap(up_sent, ("z",), 2)
    down_sum = down_near[0].astype(f32) + down_far[0].astype(f32) + down_last.astype(f32)
    turns.last = up_sent
    (far,) = turns.take(far)
    qkv_sent = (near[1].astype(f32) + far[1].astype(f32)).astype(bf16)
    qkv_last = swap(qkv_sent, ("y",), 1)
    turns.last = qkv_sent
    (odd_far,) = turns.take(odd_far)
    even_far = swap(after(even_far, odd_far), ("x",), 1)
    odd = (odd_near.astype(f32) + odd_far.astype(f32)).astype(bf16)
    odd_last = swap(odd, ("z",), 1)
    turns.last = odd
    (up_last,) = turns.take(up_last)
    up_sum = up_near[0].astype(f32) + up_far[0].astype(f32) + up_last.astype(f32)
    turns.last = up_sum = up_sum.astype(bf16)
    up_sum = lax.all_to_all(up_sum, GROUP, 0, 0, tiled=True).reshape(8, shard, wide)
    (qkv_last,) = turns.take(qkv_last)
    qkv_sum = near[0].astype(f32) + far[0].astype(f32) + qkv_last.astype(f32)
    qkv_sum = qkv_sum.astype(bf16)
    qkv_rows = qkv_sum[: n_ctx * shard].reshape(n_ctx, shard, 3 * cols)
    qkv_bias = jnp.broadcast_to(qkv_sum[n_ctx * shard :], (n_ctx, 16, 3 * cols))
    turns.last = qkv_sum = jnp.concatenate([qkv_rows, qkv_bias], axis=1)
    (out_far,) = turns.take(out_far)
    out_parts = plane_scatter(out_near, out_far, place)
    turns.last = out_parts[0]
    even_far, odd_last = turns.take(even_far, odd_last)
    even = even_near.astype(f32) + even_far.astype(f32) + odd_last.astype(f32)
    final = swap(even[rows:].astype(bf16), ("z",), 2)
    turns.last = even
    up_sum, qkv_sum = turns.take(up_sum, qkv_sum)
    qkv_sum = lax.all_to_all(qkv_sum, CTX, 0, 0, tiled=True)
    (grad_wup,) = local(
        up_final_kernel, [like((shard, w_up.shape[1]), f32)], place, up_sum
    )
    turns.last = grad_wup
    out_parts = turns.take(*out_parts)
    line_near, line_far = local(
        out_line_kernel, [like((2, shard + 16, width), f32), like((2, shard + 16, width), bf16)],
        place, *out_parts,
        scratch=[pltpu.VMEM((4, shard + 16, width), f32)],
    )
    line_far = swap(line_far, ("z",), 1)
    turns.last = line_near
    (final,) = turns.take(final)
    turns.last = grad_inputs = (grad_first + even[:rows] + final.astype(f32)).astype(bf16)
    (line_far,) = turns.take(line_far)
    turns.last = line_sent = (line_near[1] + line_far[1].astype(f32)).astype(bf16)
    line_last = swap(line_sent, ("z",), 2)
    (qkv_sum,) = turns.take(qkv_sum)
    (grad_wqkv,) = local(
        qkv_final_kernel, [like((shard, 3 * width), f32)], place, qkv_sum
    )
    bias_sum = qkv_sum[:, shard].reshape(n_ctx, 3, cols).transpose(1, 0, 2).reshape(3, width)
    bias_own = lax.dynamic_slice(bias_sum, (0, own * shard), (3, shard)).astype(f32)
    turns.last = grad_wqkv
    (line_last,) = turns.take(line_last)
    out_sum = line_near[0] + line_far[0].astype(f32) + line_last.astype(f32)
    thin = out_sum[shard:, :shard]

    return (
        result[None],
        grad_inputs[None],
        grad_wqkv,
        bias_own[0],
        bias_own[2],
        out_sum[:shard],
        thin[0],
        thin[1],
        thin[2],
        grad_wup,
        down_sum[units, :units],
        down_sum[:units],
        thin[3],
        thin[4],
        thin[5],
    )


def call_heads(mesh, *arrays):
    grid = Mesh(mesh.devices.reshape(2, 2, 4, 2), EVERY)
    lines, lone, block = P(EVERY, None), P(EVERY), P(DP, CTX, None)
    in_specs = (
        block, lines, lone, lone, lines, lone, lone, lone, lines, lone, lines, lone, lone, lone,
        P(DP, CTX), P(DP, CTX), block,
    )
    out_specs = (
        block, block, lines, lone, lone, lines, lone, lone, lone, lines, lone, lines, lone, lone,
        lone,
    )
    return jax.shard_map(
        heads_body, mesh=grid, in_specs=in_specs, out_specs=out_specs, check_vma=False
    )(*arrays)


def call(mesh, *arrays):
    if mesh.shape["dp"] == 4 and mesh.shape["ctx"] == 8 and arrays[0].shape[1] == 1024:
        return call_heads(mesh, *arrays)
    return general_call(mesh)(*arrays)


def general_call(mesh):
    in_specs = (
        P("dp", "ctx", None),
        P(("dp", "ctx"), None),
        P(("dp", "ctx")),
        P(("dp", "ctx")),
        P(("dp", "ctx"), None),
        P(("dp", "ctx")),
        P(("dp", "ctx")),
        P(("dp", "ctx")),
        P(("dp", "ctx"), None),
        P(("dp", "ctx")),
        P(("dp", "ctx"), None),
        P(("dp", "ctx")),
        P(("dp", "ctx")),
        P(("dp", "ctx")),
        P("dp", "ctx"),
        P("dp", "ctx"),
        P("dp", "ctx", None),
    )
    out_specs = (
        P("dp", "ctx", None),
        P("dp", "ctx", None),
        P(("dp", "ctx"), None),
        P(("dp", "ctx")),
        P(("dp", "ctx")),
        P(("dp", "ctx"), None),
        P(("dp", "ctx")),
        P(("dp", "ctx")),
        P(("dp", "ctx")),
        P(("dp", "ctx"), None),
        P(("dp", "ctx")),
        P(("dp", "ctx"), None),
        P(("dp", "ctx")),
        P(("dp", "ctx")),
        P(("dp", "ctx")),
    )
    return jax.shard_map(general_body, mesh=mesh, in_specs=in_specs, out_specs=out_specs, check_vma=False)


def solution(mesh):
    return partial(call, mesh)
```

```python
import math
from functools import partial

import jax
import jax.numpy as jnp
from jax import lax
from jax.experimental import pallas as pl
from jax.experimental.pallas import tpu as pltpu
from jax.sharding import Mesh
from jax.sharding import PartitionSpec as P

HEADS = 16
HEAD = 64
WINDOW = 1024


MASKED = -1e30
EPSILON = 1e-05


def layer_norm(values, scales, offsets):
    average = jnp.mean(values, axis=-1, keepdims=True)
    centred = values - average
    variance = jnp.mean(centred * centred, axis=-1, keepdims=True)
    return centred * lax.rsqrt(variance + EPSILON) * scales + offsets


def matmul(left, right):
    return jnp.dot(left, right, preferred_element_type=jnp.float32)


def rows_product(left, right):
    return lax.dot_general(
        left, right, (((0,), (0,)), ((), ())), preferred_element_type=jnp.float32
    )


def cols_product(left, right):
    return lax.dot_general(
        left, right, (((1,), (1,)), ((), ())), preferred_element_type=jnp.float32
    )


def split_heads(matrix):
    return matrix.reshape(matrix.shape[0], HEADS, HEAD)


def allowed_keys(query_tags, query_place, key_tags, key_place):
    same_doc = query_tags[:, None] // 2 == key_tags[None, :] // 2
    distance = jnp.abs(query_place[:, None] - key_place[None, :])
    usable = (key_tags[None, :] % 2 == 1) | (distance == 0)
    return same_doc & (distance <= WINDOW // 2) & usable


def masked_scores(query_block, key_heads, query_tags, query_place, key_tags, key_place):
    raw = (
        jnp.einsum("qhd,khd->hqk", query_block, key_heads, preferred_element_type=jnp.float32)
        * 0.125
    )
    return jnp.where(allowed_keys(query_tags, query_place, key_tags, key_place)[None], raw, MASKED)


def attend_forward(
    query_heads, key_heads, value_heads, query_tags, query_place, key_tags, key_place
):
    row_count = query_heads.shape[0]
    block_rows = min(row_count, 512)

    def one_block(block_index):
        scores = masked_scores(query_heads, key_heads, query_tags, query_place, key_tags, key_place)
        totals = jax.nn.logsumexp(scores, axis=2)
        probs = jnp.exp(scores - totals[:, :, None]).astype(jnp.bfloat16)
        output = jnp.einsum("hqk,khd->qhd", probs, value_heads, preferred_element_type=jnp.float32)
        return (output, totals)

    outputs, totals = lax.map(one_block, jnp.arange(row_count // block_rows, dtype=jnp.int32))
    return (outputs.reshape(row_count, HEADS * HEAD), totals)


def attend_backward(
    query_heads,
    key_heads,
    value_heads,
    grad_heads,
    deltas,
    totals,
    query_tags,
    query_place,
    key_tags,
    key_place,
):
    row_count = query_heads.shape[0]
    block_rows = min(row_count, 512)

    def one_block(running, block_index):
        key_grad, value_grad = running
        scores = masked_scores(query_heads, key_heads, query_tags, query_place, key_tags, key_place)
        probs = jnp.exp(scores - totals[block_index][:, :, None])
        dprobs = jnp.einsum(
            "qhd,khd->hqk", grad_heads, value_heads, preferred_element_type=jnp.float32
        )
        dscores = (probs * (dprobs - deltas[:, :, None])).astype(jnp.bfloat16)
        query_grad = (
            jnp.einsum("hqk,khd->qhd", dscores, key_heads, preferred_element_type=jnp.float32)
            * 0.125
        )
        key_grad = (
            key_grad
            + jnp.einsum("hqk,qhd->khd", dscores, query_heads, preferred_element_type=jnp.float32)
            * 0.125
        )
        value_grad = value_grad + jnp.einsum(
            "hqk,qhd->khd",
            probs.astype(jnp.bfloat16),
            grad_heads,
            preferred_element_type=jnp.float32,
        )
        return ((key_grad, value_grad), query_grad)

    zeros = jnp.zeros(key_heads.shape, jnp.float32)
    (key_grad, value_grad), query_grads = lax.scan(
        one_block, (zeros, zeros), jnp.arange(row_count // block_rows, dtype=jnp.int32)
    )
    key_count = key_heads.shape[0]
    return (
        query_grads.reshape(row_count, HEADS * HEAD),
        key_grad.reshape(key_count, HEADS * HEAD),
        value_grad.reshape(key_count, HEADS * HEAD),
    )


def clip_window(whole, rows_here, seq_length, own_index):
    neighbours = (WINDOW // 2 + rows_here - 1) // rows_here
    key_span = min((2 * neighbours + 1) * rows_here, seq_length)
    first_key = jnp.clip((own_index - neighbours) * rows_here, 0, seq_length - key_span)
    window = tuple((lax.dynamic_slice_in_dim(member, first_key, key_span, 0) for member in whole))
    return (window, first_key)


def window_keys(items, rows_here, seq_length, own_index):
    whole = (
        lax.all_gather(items[0], "ctx", axis=0, tiled=True),
        lax.all_gather(items[1], "ctx", axis=0, tiled=True),
        lax.all_gather(items[2], "ctx", axis=0, tiled=True),
    )
    return clip_window(whole, rows_here, seq_length, own_index)


def window_keys_again(items, rows_here, seq_length, own_index):
    whole = (
        lax.all_gather(items[0], "ctx", axis=0, tiled=True),
        lax.all_gather(items[1], "ctx", axis=0, tiled=True),
        lax.all_gather(items[2], "ctx", axis=0, tiled=True),
    )
    return clip_window(whole, rows_here, seq_length, own_index)


def return_key_grads(key_grad, value_grad, rows_here, first_key):
    width = key_grad.shape[1]
    joined = jnp.concatenate([key_grad, value_grad], axis=1)
    key_span = joined.shape[0]
    count = rows_here * lax.axis_size("ctx")
    padding = jnp.zeros((count, 2 * width), jnp.float32)
    padded = jnp.concatenate([padding, joined, padding], axis=0)
    offset = jnp.clip(jnp.int32(0) - first_key + count, 0, key_span + count)
    summed = lax.psum_scatter(
        lax.dynamic_slice_in_dim(padded, offset, count, 0), "ctx", scatter_dimension=0, tiled=True
    )
    return (summed[:, :width], summed[:, width:])


def general_body(
    tokens,
    w_qkv,
    b_query,
    b_value,
    w_out,
    b_out,
    ln1_gain,
    ln1_bias,
    w_up,
    b_up,
    w_down,
    b_down,
    ln2_gain,
    ln2_bias,
    segment_ids,
    pad_mask,
    cotangent,
):
    weight_shards = (
        w_qkv,
        b_query,
        b_value,
        w_out,
        b_out,
        ln1_gain,
        ln1_bias,
        w_up,
        b_up,
        w_down,
        b_down,
        ln2_gain,
        ln2_bias,
    )
    gathered = (
        lax.all_gather(weight_shards[0], ("dp", "ctx"), axis=0, tiled=True),
        lax.all_gather(weight_shards[1], ("dp", "ctx"), axis=0, tiled=True),
        lax.all_gather(weight_shards[2], ("dp", "ctx"), axis=0, tiled=True),
        lax.all_gather(weight_shards[3], ("dp", "ctx"), axis=0, tiled=True),
        lax.all_gather(weight_shards[4], ("dp", "ctx"), axis=0, tiled=True),
        lax.all_gather(weight_shards[5], ("dp", "ctx"), axis=0, tiled=True),
        lax.all_gather(weight_shards[6], ("dp", "ctx"), axis=0, tiled=True),
        lax.all_gather(weight_shards[7], ("dp", "ctx"), axis=0, tiled=True),
        lax.all_gather(weight_shards[8], ("dp", "ctx"), axis=0, tiled=True),
        lax.all_gather(weight_shards[9], ("dp", "ctx"), axis=0, tiled=True),
        lax.all_gather(weight_shards[10], ("dp", "ctx"), axis=0, tiled=True),
        lax.all_gather(weight_shards[11], ("dp", "ctx"), axis=0, tiled=True),
        lax.all_gather(weight_shards[12], ("dp", "ctx"), axis=0, tiled=True),
    )
    (
        full_qkv,
        full_bquery,
        full_bvalue,
        full_out,
        full_bout,
        full_gain_one,
        full_bias_one,
        full_up,
        full_bup,
        full_down,
        full_bdown,
        full_gain_two,
        full_bias_two,
    ) = gathered
    rows_here = tokens.shape[1]
    seq_length = rows_here * lax.axis_size("ctx")
    own_index = lax.axis_index("ctx")
    inputs = tokens[0]
    inputs_wide = inputs.astype(jnp.float32)
    model_width = inputs.shape[1]
    token_tags = 2 * (segment_ids[0] + 1) + pad_mask[0]
    query_place = own_index * rows_here + jnp.arange(rows_here, dtype=jnp.int32)
    mixed = matmul(inputs, full_qkv)
    queries = (mixed[:, :model_width] + full_bquery.astype(jnp.float32)).astype(jnp.bfloat16)
    keys = mixed[:, model_width : 2 * model_width].astype(jnp.bfloat16)
    values = (mixed[:, 2 * model_width :] + full_bvalue.astype(jnp.float32)).astype(jnp.bfloat16)
    (key_window, value_window, tag_window), first_key = window_keys(
        (keys, values, token_tags), rows_here, seq_length, own_index
    )
    key_place = first_key + jnp.arange(key_window.shape[0], dtype=jnp.int32)
    attended, totals = attend_forward(
        split_heads(queries),
        split_heads(key_window),
        split_heads(value_window),
        token_tags,
        query_place,
        tag_window,
        key_place,
    )
    attended_low = attended.astype(jnp.bfloat16)
    first = inputs_wide + matmul(attended_low, full_out) + full_bout.astype(jnp.float32)
    normed, first_pull = jax.vjp(
        layer_norm, first, full_gain_one.astype(jnp.float32), full_bias_one.astype(jnp.float32)
    )
    normed_low = normed.astype(jnp.bfloat16)
    hidden = matmul(normed_low, full_up) + full_bup.astype(jnp.float32)
    active, gelu_pull = jax.vjp(partial(jax.nn.gelu, approximate=False), hidden)
    active_low = active.astype(jnp.bfloat16)
    second = normed + matmul(active_low, full_down) + full_bdown.astype(jnp.float32)
    result, second_pull = jax.vjp(
        layer_norm, second, full_gain_two.astype(jnp.float32), full_bias_two.astype(jnp.float32)
    )
    gathered = (
        lax.all_gather(weight_shards[0], ("dp", "ctx"), axis=0, tiled=True),
        lax.all_gather(weight_shards[1], ("dp", "ctx"), axis=0, tiled=True),
        lax.all_gather(weight_shards[2], ("dp", "ctx"), axis=0, tiled=True),
        lax.all_gather(weight_shards[3], ("dp", "ctx"), axis=0, tiled=True),
        lax.all_gather(weight_shards[4], ("dp", "ctx"), axis=0, tiled=True),
        lax.all_gather(weight_shards[5], ("dp", "ctx"), axis=0, tiled=True),
        lax.all_gather(weight_shards[6], ("dp", "ctx"), axis=0, tiled=True),
        lax.all_gather(weight_shards[7], ("dp", "ctx"), axis=0, tiled=True),
        lax.all_gather(weight_shards[8], ("dp", "ctx"), axis=0, tiled=True),
        lax.all_gather(weight_shards[9], ("dp", "ctx"), axis=0, tiled=True),
        lax.all_gather(weight_shards[10], ("dp", "ctx"), axis=0, tiled=True),
        lax.all_gather(weight_shards[11], ("dp", "ctx"), axis=0, tiled=True),
        lax.all_gather(weight_shards[12], ("dp", "ctx"), axis=0, tiled=True),
    )
    back_qkv = gathered[0]
    back_out = gathered[3]
    back_up = gathered[7]
    back_down = gathered[9]
    grad_second, grad_gain_two, grad_bias_two = second_pull(cotangent[0].astype(jnp.float32))
    grad_outcome = grad_second.astype(jnp.bfloat16)
    grad_wdown = rows_product(active_low, grad_outcome)
    grad_bdown = jnp.sum(grad_outcome.astype(jnp.float32), axis=0)
    (grad_active,) = gelu_pull(cols_product(grad_outcome, back_down))
    grad_hidden = grad_active.astype(jnp.bfloat16)
    grad_wup = rows_product(normed_low, grad_hidden)
    grad_bup = jnp.sum(grad_hidden.astype(jnp.float32), axis=0)
    grad_normed = grad_second + cols_product(grad_hidden, back_up)
    grad_first, grad_gain_one, grad_bias_one = first_pull(grad_normed)
    grad_branch = grad_first.astype(jnp.bfloat16)
    grad_wout = rows_product(attended_low, grad_branch)
    grad_bout = jnp.sum(grad_branch.astype(jnp.float32), axis=0)
    grad_attended = cols_product(grad_branch, back_out).astype(jnp.bfloat16)
    deltas = jnp.sum(
        (grad_attended.astype(jnp.float32) * attended).reshape(rows_here, HEADS, HEAD), axis=2
    ).T
    (key_again, value_again, tag_again), first_again = window_keys_again(
        (keys, values, token_tags), rows_here, seq_length, own_index
    )
    place_again = first_again + jnp.arange(key_again.shape[0], dtype=jnp.int32)
    grad_queries, key_grad, value_grad = attend_backward(
        split_heads(queries),
        split_heads(key_again),
        split_heads(value_again),
        split_heads(grad_attended),
        deltas,
        totals,
        token_tags,
        query_place,
        tag_again,
        place_again,
    )
    key_total, value_total = return_key_grads(key_grad, value_grad, rows_here, first_again)
    grad_query_low = grad_queries.astype(jnp.bfloat16)
    grad_value_low = value_total.astype(jnp.bfloat16)
    grad_mixed = jnp.concatenate(
        [grad_query_low, key_total.astype(jnp.bfloat16), grad_value_low], axis=1
    )
    grad_wqkv = rows_product(inputs, grad_mixed)
    grad_bquery = jnp.sum(grad_query_low.astype(jnp.float32), axis=0)
    grad_bvalue = jnp.sum(grad_value_low.astype(jnp.float32), axis=0)
    grad_inputs = grad_first + cols_product(grad_mixed, back_qkv)
    summed = (
        lax.psum_scatter(grad_wqkv, ("dp", "ctx"), scatter_dimension=0, tiled=True),
        lax.psum_scatter(grad_bquery, ("dp", "ctx"), scatter_dimension=0, tiled=True),
        lax.psum_scatter(grad_bvalue, ("dp", "ctx"), scatter_dimension=0, tiled=True),
        lax.psum_scatter(grad_wout, ("dp", "ctx"), scatter_dimension=0, tiled=True),
        lax.psum_scatter(grad_bout, ("dp", "ctx"), scatter_dimension=0, tiled=True),
        lax.psum_scatter(grad_gain_one, ("dp", "ctx"), scatter_dimension=0, tiled=True),
        lax.psum_scatter(grad_bias_one, ("dp", "ctx"), scatter_dimension=0, tiled=True),
        lax.psum_scatter(grad_wup, ("dp", "ctx"), scatter_dimension=0, tiled=True),
        lax.psum_scatter(grad_bup, ("dp", "ctx"), scatter_dimension=0, tiled=True),
        lax.psum_scatter(grad_wdown, ("dp", "ctx"), scatter_dimension=0, tiled=True),
        lax.psum_scatter(grad_bdown, ("dp", "ctx"), scatter_dimension=0, tiled=True),
        lax.psum_scatter(grad_gain_two, ("dp", "ctx"), scatter_dimension=0, tiled=True),
        lax.psum_scatter(grad_bias_two, ("dp", "ctx"), scatter_dimension=0, tiled=True),
    )
    return (
        result.astype(jnp.bfloat16)[None],
        grad_inputs.astype(jnp.bfloat16)[None],
        summed[0],
        summed[1],
        summed[2],
        summed[3],
        summed[4],
        summed[5],
        summed[6],
        summed[7],
        summed[8],
        summed[9],
        summed[10],
        summed[11],
        summed[12],
    )


GROUP = ("y", "core", "x")
CTX = ("z", "x")
DP = ("y", "core")
EVERY = ("y", "core", "z", "x")
bf16, f32 = jnp.bfloat16, jnp.float32


def swap(member, axes, code):
    count = 1
    for axis in axes:
        count *= lax.axis_size(axis)
    return lax.ppermute(member, axes, [(place, place ^ code) for place in range(count)])


def after(member, *events):
    return lax.optimization_barrier((member,) + events)[0]


class Turns:
    def __init__(self, last):
        self.last = last

    def take(self, *members):
        return lax.optimization_barrier((*members, self.last))[:-1]


def like(shape, kind):
    return jax.ShapeDtypeStruct(shape, kind)


def staged(kernel, groups, results, lazy, place, *refs):
    count = sum(groups)
    given, refs = refs[:count], refs[count:]
    out, refs = list(refs[: len(results)]), refs[len(results) :]
    held, refs = refs[: len(groups)], refs[len(groups) :]
    staging, refs = refs[: sum(results)], refs[sum(results) :]
    (arrived, left), refs = refs[:2], refs[2:]
    copies, index, first = [], 0, []
    for size, target in zip(groups, held):
        first.append(index)
        rows = target.shape[0] // size
        for member in range(size):
            part = target if size == 1 else target.at[pl.ds(member * rows, rows)]
            copies.append(pltpu.make_async_copy(given[index], part, arrived.at[index]))
            index += 1
    for copy in copies:
        copy.start()
    if lazy:
        arrivals = copies
        kernel = partial(kernel, lambda group, member=0: arrivals[first[group] + member].wait())
    else:
        for copy in copies:
            copy.wait()
    copies, index = [], 0
    for i, far in enumerate(results):
        if far:
            copies.append(pltpu.make_async_copy(staging[index], out[i], left.at[index]))
            out[i] = staging[index]
            index += 1
    kernel(place, *held, *out, *refs)
    for copy in copies:
        copy.start()
    for copy in copies:
        copy.wait()


def bytes_of(v):
    return math.prod(v.shape) * jnp.dtype(v.dtype).itemsize


def local(kernel, outs, place, *operands, scratch=(), far=False, keep=(), lazy=False, cost=0):
    near = pl.BlockSpec(memory_space=pltpu.VMEM)
    groups = [v if isinstance(v, (tuple, list)) else (v,) for v in operands]
    operands = [v for group in groups for v in group]
    size = sum(bytes_of(v) for v in (*operands, *outs, *scratch))
    results = [far and i not in keep for i in range(len(outs))]
    if far:
        kernel = partial(staged, kernel, [len(group) for group in groups], results, lazy)
        held = [
            pltpu.VMEM((len(g) * g[0].shape[0],) + g[0].shape[1:], g[0].dtype) for g in groups
        ]
        held += [pltpu.VMEM(v.shape, v.dtype) for v, out in zip(outs, results) if out]
        held += [pltpu.SemaphoreType.DMA((len(operands),))]
        held += [pltpu.SemaphoreType.DMA((max(sum(results), 1),))]
        scratch = held + list(scratch)
        operands = [pltpu.with_memory_space_constraint(v, pltpu.HBM) for v in operands]
        outs = [pltpu.HBM(v.shape, v.dtype) if out else v for v, out in zip(outs, results)]
    hbm = pl.BlockSpec(memory_space=pltpu.HBM)
    return pl.pallas_call(
        kernel,
        out_shape=list(outs),
        in_specs=[pl.BlockSpec(memory_space=pltpu.SMEM)] + [hbm if far else near] * len(operands),
        out_specs=[hbm if out else near for out in results],
        scratch_shapes=list(scratch),
        cost_estimate=pl.CostEstimate(flops=cost * 10**9, bytes_accessed=0, transcendentals=0),
        compiler_params=pltpu.CompilerParams(vmem_limit_bytes=size + ((24 if cost > 8 else 6) << 20)),
    )(place, *operands)


def pair_product(left, right):
    return lax.dot_general(
        left, right, (((0,), (0,)), ((), ())), preferred_element_type=jnp.float32
    )


def plane_gather(block):
    return [block] + [swap(block, ("y", "x"), code) for code in range(1, 4)]


def group_gather(block):
    plane = plane_gather(block)
    return plane + [swap(member, ("core",), 1) for member in plane]


def merge_kernel(place, near, far, own, *sent):
    rows = own.shape[0]
    for code in range(4):
        part = pl.ds(code * rows, rows)
        total = near[part, :].astype(f32) + far[part, :].astype(f32)
        if code == 0:
            own[...] = total
        else:
            sent[code - 1][...] = total.astype(bf16)


def group_scatter(near, far, place, event=None):
    crossed = swap(far, ("core",), 1)
    if event is not None:
        crossed = after(crossed, event)
    return plane_scatter(near, crossed, place)


def plane_scatter(near, crossed, place):
    rows, width = near.shape[0] // 4, near.shape[1]
    outs = [like((rows, width), f32)] + [like((rows, width), bf16)] * 3
    own, *sent = local(merge_kernel, outs, place, near, crossed)
    parts = [own] + [swap(sent[code - 1], ("y", "x"), code) for code in range(1, 4)]
    return parts


def ctx_gather(block):
    two, one = swap(block, ("z",), 2), swap(block, ("z",), 1)
    line = [block, one, two, swap(two, ("z",), 1)]
    blocks = [piece for member in line[:3] for piece in (member, swap(member, ("x",), 1))]
    return blocks + [line[3]]


def pack_kernel(place, w_qkv, w_up, *refs):
    vectors, (b_up, segments, pads, qkv_ref, up_ref) = refs[:8], refs[8:]
    groups, _, wide = qkv_ref.shape
    shard, cols = w_qkv.shape[0], wide // 3
    tags = (2 * (segments[...] + 1) + pads[...]).astype(f32)
    lone = jnp.concatenate([v[...].astype(f32) for v in vectors], axis=0)
    lone = jnp.concatenate([lone, jnp.zeros((8, 128 - shard), f32)], axis=1)
    small = jnp.concatenate([lone, b_up[...].astype(f32), tags, jnp.zeros((6, 128), f32)], axis=0)
    small = jnp.concatenate([small, jnp.zeros((16, wide - 128), f32)], axis=1).astype(bf16)
    for c in range(groups):
        for kind in range(3):
            at = (kind * groups + c) * cols
            qkv_ref[c, :shard, kind * cols : (kind + 1) * cols] = w_qkv[:, at : at + cols]
        qkv_ref[c, shard:, :] = small
    units = b_up.shape[1]
    for g in range(8):
        for z in range(4):
            at = ((g // 2 * 4 + z) * 2 + g % 2) * units
            up_ref[g, :, z * units : (z + 1) * units] = w_up[:, at : at + units]


def out_gather(block, *events):
    pair = after(jnp.stack([block, swap(block, ("z",), 1)]), events[0])
    line = after(jnp.concatenate([pair, swap(pair, ("z",), 2)]), events[1])
    both = after(jnp.stack([line, swap(line, ("y",), 1)]), events[2])
    far = swap(both, ("x",), 1)
    both, far = after(both, events[3]), after(far, events[3])
    return [both, far, swap(both, ("core",), 1), swap(far, ("core",), 1)]


def order_out_kernel(place, p00, p01, p10, p11, out_ref):
    rows = p00.shape[2]
    own = place[0]
    for core in range(2):
        for x in range(2):
            piece = ((p00, p01), (p10, p11))[core][x]
            for y in range(2):
                for z in range(4):
                    at = own ^ (y * 16 + core * 8 + z * 2 + x)
                    out_ref[pl.ds(at * rows, rows), :] = piece[y, z]


def order_kernel(place, *refs):
    up_refs, down_refs, (up_out, down_out) = refs[:4], refs[4:8], refs[8:]
    rows, units = up_out.shape[0] // 32, down_refs[0].shape[0]
    own_z = place[3]
    for z in range(4):
        down_out[pl.ds((own_z ^ z) * units, units), :] = down_refs[z][...]
        for j in range(8):
            at = (j // 2 * 4 + (own_z ^ z)) * 2 + j % 2
            up_out[pl.ds(at * rows, rows), :] = up_refs[z][pl.ds(j * rows, rows), :]


def allowed_here(query_tags, query_place, key_tags, key_place):
    same_doc = (query_tags >> 1) == (key_tags >> 1)
    distance = jnp.abs(query_place - key_place)
    usable = ((key_tags & 1) == 1) | (distance == 0)
    return same_doc & (distance <= WINDOW // 2) & usable


def places(own_ctx, rows, shape, axis, start=0):
    index = lax.broadcasted_iota(jnp.int32, shape, axis) + start
    return ((index // rows) ^ own_ctx) * rows + index % rows


def attend_kernel(ready, place, *refs, n_blocks, rows, cols):
    pieces, refs = refs[:4], refs[4:]
    bias, tags_row, lines, q_ref, k_ref, v_ref, att_ref, msg_ref, lse_ref, qkv_ref = refs
    own_dp, own_ctx = place[1], place[2]
    shard = 32
    for m, piece in enumerate(pieces):
        ready(m)
        for c in range(n_blocks):
            at = ((own_dp ^ m) * n_blocks + c) * shard
            qkv_ref[pl.ds(at, shard), :] = piece[c, :shard, :]
    ready(4)
    ready(5)
    for j in range(n_blocks // 2):
        part = pl.ds(j * 2 * rows, 2 * rows)
        ready(6, 2 * j)
        ready(6, 2 * j + 1)
        mixed = matmul(lines[part, :], qkv_ref[...]) + bias[...]
        q_ref[part, :] = mixed[:, :cols].astype(bf16)
        k_ref[part, :] = mixed[:, cols : 2 * cols].astype(bf16)
        v_ref[part, :] = mixed[:, 2 * cols :].astype(bf16)
    length = n_blocks * rows
    chunk = 2 * rows

    def step(index, carry):
        part = pl.ds(index * chunk, chunk)
        allowed = allowed_here(
            jnp.broadcast_to(tags_row[:, part], (128, chunk)).T[:, :1],
            places(own_ctx, rows, (chunk, 1), 0, index * chunk),
            tags_row[...],
            places(own_ctx, rows, (1, length), 1),
        )
        found = []
        for head in range(cols // HEAD):
            lanes = slice(head * HEAD, (head + 1) * HEAD)
            scores = cols_product(q_ref[part, lanes], k_ref[:, lanes]) * 0.125
            scores = jnp.where(allowed, scores, MASKED)
            top = jnp.max(scores, axis=1, keepdims=True)
            weights = jnp.exp(scores - top)
            mass = jnp.sum(weights, axis=1, keepdims=True)
            found.append(matmul(weights.astype(bf16), v_ref[:, lanes]) / mass)
            total = top + jnp.log(mass)
            lse_ref[pl.ds(head, 1), part] = jnp.broadcast_to(total, (chunk, 128)).T[:1, :]
        attended = jnp.concatenate(found, axis=1)
        att_ref[part, :] = attended
        for half in range(2):
            at = ((index * 2 + half) ^ own_ctx) * rows
            msg_ref[pl.ds(at, rows), :] = attended[half * rows : (half + 1) * rows].astype(bf16)
        return carry

    lax.fori_loop(0, length // chunk, step, 0, unroll=True)


def branch_kernel(
    place, moved, w_out, inputs, vectors, normed_ref, low_ref, hat_ref, rate_ref
):
    groups, rows, cols = moved.shape
    total = inputs[...].astype(f32) + vectors[2:3, :]
    for c in range(groups):
        total = total + matmul(moved[c], w_out[pl.ds(c * cols, cols), :])
    centred = total - jnp.mean(total, axis=1, keepdims=True)
    rate = lax.rsqrt(jnp.mean(centred * centred, axis=1, keepdims=True) + EPSILON)
    hat = centred * rate
    normed = hat * vectors[3:4, :] + vectors[4:5, :]
    normed_ref[...] = normed
    low_ref[...] = normed.astype(bf16)
    hat_ref[...] = hat
    rate_ref[...] = jnp.broadcast_to(rate, rate_ref.shape)


def forward_kernel(ready, place, up, bias, lines, down, hidden_ref, active_ref, near, far):
    rows = lines.shape[0] // 4
    ready(0)
    ready(1)
    for quarter in range(4):
        part = pl.ds(quarter * rows, rows)
        ready(2, 2 * quarter)
        ready(2, 2 * quarter + 1)
        hidden = matmul(lines[part, :], up[...]) + bias[...]
        hidden_ref[part, :] = hidden
        active = (0.5 * hidden * (1 + lax.erf(hidden * 0.7071067811865476))).astype(bf16)
        active_ref[part, :] = active
        if quarter == 0:
            ready(3)
        target = near if quarter < 2 else far
        target[pl.ds(quarter % 2 * rows, rows), :] = matmul(active, down[...]).astype(bf16)


def second_kernel(
    place, normed, own, p1, p2, p3, vectors, cotangent, result_ref, grad_ref, low_ref, sums_ref
):
    second = normed[...] + own[...] + p1[...].astype(f32) + p2[...].astype(f32)
    second = second + p3[...].astype(f32) + vectors[5:6, :]
    centred = second - jnp.mean(second, axis=1, keepdims=True)
    rate = lax.rsqrt(jnp.mean(centred * centred, axis=1, keepdims=True) + EPSILON)
    hat = centred * rate
    gain = vectors[6:7, :]
    result_ref[...] = (hat * gain + vectors[7:8, :]).astype(bf16)
    grad = cotangent[...].astype(f32)
    scaled = grad * gain
    mean_scaled = jnp.mean(scaled, axis=1, keepdims=True)
    mean_hat = jnp.mean(scaled * hat, axis=1, keepdims=True)
    grad_second = rate * (scaled - mean_scaled - hat * mean_hat)
    grad_ref[...] = grad_second
    low = grad_second.astype(bf16)
    low_ref[...] = low
    sums_ref[0:1, :] = jnp.sum(low.astype(f32), axis=0, keepdims=True)
    sums_ref[1:2, :] = jnp.sum(grad * hat, axis=0, keepdims=True)
    sums_ref[2:3, :] = jnp.sum(grad, axis=0, keepdims=True)


def backward_kernel(place, *refs):
    blocks = refs[:8]
    up, down, slope, grad_ref, near, far = refs[8:]
    rows = blocks[0].shape[0]
    for pair in range(4):
        lines = jnp.concatenate([blocks[2 * pair][...], blocks[2 * pair + 1][...]], axis=0)
        part = pl.ds(pair * 2 * rows, 2 * rows)
        grad = (slope[part, :] * cols_product(lines, down[...])).astype(bf16)
        grad_ref[part, :] = grad
        target = near if pair < 2 else far
        target[pl.ds(pair % 2 * 2 * rows, 2 * rows), :] = cols_product(grad, up[...]).astype(bf16)


def down_grad_kernel(place, lines, active, grad_hidden, near, far, parts):
    width = lines.shape[1]
    shard = active.shape[1] // 4
    total = jnp.sum(grad_hidden[...].astype(f32), axis=0, keepdims=True)
    for z in range(4):
        part = slice(z * shard, (z + 1) * shard)
        at = place[3] ^ z
        parts[at, :shard, :] = pair_product(active[:, part], lines[...]).astype(bf16)
        parts[at, shard:, :shard] = jnp.broadcast_to(total[:, part], (16, shard)).astype(bf16)
        parts[at, shard:, shard:] = jnp.zeros((16, width - shard), bf16)
    for half in range(2):
        near[half], far[half] = parts[2 * half], parts[2 * half + 1]


def up_grad_kernel(place, lines, grad_hidden, near, far, parts):
    own_z = place[3]
    for quarter in range(4):
        span = 8 * 32
        part = slice(quarter * span, (quarter + 1) * span)
        found = pair_product(lines[:, part], grad_hidden[...]).astype(bf16)
        for z in range(4):
            for x in range(2):
                piece = found[(z * 2 + x) * 32 : (z * 2 + x + 1) * 32]
                parts[own_z ^ z, pl.ds((quarter * 2 + x) * 32, 32), :] = piece
    for half in range(2):
        near[half], far[half] = parts[2 * half], parts[2 * half + 1]


def first_kernel(
    place, grad_second, own, p1, p2, p3, vectors, hat_ref, rate_ref, w_out, grad_ref, low_ref,
    msg_ref, sums_ref,
):
    grad = grad_second[...] + own[...] + p1[...].astype(f32) + p2[...].astype(f32)
    grad = grad + p3[...].astype(f32)
    hat = hat_ref[...]
    scaled = grad * vectors[3:4, :]
    mean_scaled = jnp.mean(scaled, axis=1, keepdims=True)
    mean_hat = jnp.mean(scaled * hat, axis=1, keepdims=True)
    grad_first = rate_ref[:, :1] * (scaled - mean_scaled - hat * mean_hat)
    grad_ref[...] = grad_first
    low = grad_first.astype(bf16)
    low_ref[...] = low
    groups, rows, cols = msg_ref.shape
    for c in range(groups):
        msg_ref[c] = cols_product(low, w_out[pl.ds(c * cols, cols), :]).astype(bf16)
    sums_ref[0:1, :] = jnp.sum(low.astype(f32), axis=0, keepdims=True)
    sums_ref[1:2, :] = jnp.sum(grad * hat, axis=0, keepdims=True)
    sums_ref[2:3, :] = jnp.sum(grad, axis=0, keepdims=True)


def out_grad_kernel(place, moved, low, sums_one, sums_two, near, far, parts):
    groups, rows, cols = moved.shape
    high, width = parts.shape[1:]
    own_y, own_core, own_x = place[4], place[5], place[6]
    sums = [sums_one[0:3, :], sums_two[0:3, :], jnp.zeros((high - rows - 6, width), f32)]
    sums = jnp.concatenate(sums, axis=0).astype(bf16)
    for c in range(groups):
        found = pair_product(moved[c], low[...]).astype(bf16)
        for m in range(4):
            y, core, z, x = c // 4, c // 2 % 2, c % 2 * 2 + m // 2, m % 2
            code = (core ^ own_core) * 4 + (y ^ own_y) * 2 + (x ^ own_x)
            parts[code, pl.ds(z * 32, 32), :] = found[m * 32 : (m + 1) * 32]
            lanes = slice((c * 4 + m) * 32, (c * 4 + m + 1) * 32)
            parts[code, rows:, z * 32 : (z + 1) * 32] = sums[:, lanes]
    for code in range(4):
        near[pl.ds(code * high, high), :] = parts[code]
        far[pl.ds(code * high, high), :] = parts[code + 4]


def out_line_kernel(place, own, p1, p2, p3, near, far, parts):
    total = own[...] + p1[...].astype(f32) + p2[...].astype(f32) + p3[...].astype(f32)
    own_z = place[3]
    parts[...] = jnp.zeros(parts.shape, f32)
    for z in range(4):
        at = own_z ^ z
        parts[at, :32, :] = total[z * 32 : (z + 1) * 32]
        parts[at, 32:, :32] = total[128:, z * 32 : (z + 1) * 32]
    for half in range(2):
        near[half], far[half] = parts[2 * half], parts[2 * half + 1].astype(bf16)


def attend_grad_kernel(
    place, *refs,
):
    moved, q_ref, k_ref, v_ref, att_ref, lse_ref, tags_row, *refs = refs
    mixed_ref, key_grad, value_grad, back = refs
    groups, rows, cols = moved.shape
    length = groups * rows
    own_ctx = place[2]
    for j in range(groups):
        back[pl.ds(j * rows, rows), :] = moved[own_ctx ^ j]
    key_grad[...] = jnp.zeros(key_grad.shape, f32)
    value_grad[...] = jnp.zeros(value_grad.shape, f32)
    chunk = 2 * rows
    tags_col = jnp.broadcast_to(tags_row[...], (128, length)).T[:, :1]

    def step(index, carry):
        part = pl.ds(index * chunk, chunk)
        allowed = allowed_here(
            tags_row[:, part],
            places(own_ctx, rows, (1, chunk), 1, index * chunk),
            tags_col,
            places(own_ctx, rows, (length, 1), 0),
        )
        weighted = (back[part, :].astype(f32) * att_ref[part, :]).T
        found = []
        for head in range(cols // HEAD):
            lanes = slice(head * HEAD, (head + 1) * HEAD)
            delta = jnp.sum(weighted[lanes, :], axis=0, keepdims=True)
            scores = cols_product(k_ref[:, lanes], q_ref[part, lanes]) * 0.125
            probs = jnp.where(allowed, jnp.exp(scores - lse_ref[pl.ds(head, 1), part]), 0.0)
            grads = cols_product(v_ref[:, lanes], back[part, lanes])
            grads = (probs * (grads - delta)).astype(bf16)
            value_grad[:, lanes] += matmul(probs.astype(bf16), back[part, lanes])
            key_grad[:, lanes] += matmul(grads, q_ref[part, lanes])
            found.append(pair_product(grads, k_ref[:, lanes]) * 0.125)
        mixed_ref[part, :cols] = jnp.concatenate(found, axis=1).astype(bf16)
        return carry

    lax.fori_loop(0, length // chunk, step, 0, unroll=True)
    mixed_ref[:, cols : 2 * cols] = (key_grad[...] * 0.125).astype(bf16)
    mixed_ref[:, 2 * cols :] = value_grad[...].astype(bf16)


def leave_kernel(ready, place, mixed_ref, qkv_ref, lines, *refs):
    even_near, even_far, odd_near, odd_far, near, far = refs
    messages = ((even_near, even_far), (odd_near, odd_far))
    groups, rows = 8, mixed_ref.shape[0] // 8
    ready(0)
    ready(1)
    for j in range(groups):
        part = cols_product(mixed_ref[pl.ds(j * rows, rows), :], qkv_ref[...])
        target = messages[j // 2 % 2][j % 2]
        target[pl.ds(j // 4 * rows, rows), :] = part.astype(bf16)
    own_dp = place[1]
    cols = mixed_ref.shape[1] // 3
    sums = jnp.sum(mixed_ref[...].astype(f32), axis=0, keepdims=True)
    sums = jnp.broadcast_to(sums, (16, 3 * cols)).astype(bf16)
    span = lines.shape[1] // 4
    for j in range(groups):
        ready(2, j)
    for ky in range(2):
        for kc in range(2):
            start = pl.multiple_of((own_dp ^ (ky * 2 + kc)) * span, span)
            found = pair_product(lines[:, pl.ds(start, span)], mixed_ref[...]).astype(bf16)
            target = far if kc else near
            target[ky, :span, :] = found
            target[ky, span:, :] = sums


def up_final_kernel(place, moved, out):
    groups, shard, wide = moved.shape
    units = wide // 4
    for g in range(groups):
        for z in range(4):
            at = ((g // 2 * 4 + z) * 2 + g % 2) * units
            out[:, at : at + units] = moved[g, :, z * units : (z + 1) * units].astype(f32)


def qkv_final_kernel(place, moved, out):
    groups, _, wide = moved.shape
    shard, cols = out.shape[0], wide // 3
    for c in range(groups):
        for kind in range(3):
            at = (kind * groups + c) * cols
            out[:, at : at + cols] = moved[c, :shard, kind * cols : (kind + 1) * cols].astype(f32)


def heads_body(
    tokens, w_qkv, b_query, b_value, w_out, b_out, ln1_gain, ln1_bias, w_up, b_up, w_down, b_down,
    ln2_gain, ln2_bias, segment_ids, pad_mask, cotangent,
):
    inputs = tokens[0]
    rows, width = inputs.shape
    n_ctx = lax.axis_size(CTX)
    n_dp = lax.axis_size(DP)
    n_z = lax.axis_size("z")
    length = rows * n_ctx
    cols = width // n_ctx
    shard = w_qkv.shape[0]
    units = w_down.shape[0]
    wide = n_z * units
    own_ctx = lax.axis_index(CTX)
    own_dp = lax.axis_index(DP)
    own = lax.axis_index(EVERY)
    place = jnp.stack(
        [own, own_dp, own_ctx, lax.axis_index("z")] + [lax.axis_index(a) for a in GROUP]
    ).astype(jnp.int32)

    vectors = (b_query, b_value, b_out, ln1_gain, ln1_bias, b_down, ln2_gain, ln2_bias)
    qkv_parts, up_parts = local(
        pack_kernel,
        [like((n_ctx, shard + 16, 3 * cols), bf16), like((8, shard, wide), bf16)],
        place, w_qkv, w_up, *[v[None] for v in vectors], b_up[None], segment_ids, pad_mask,
        far=True,
    )
    blocks = ctx_gather(inputs)
    qkv = after(qkv_parts, blocks[1], blocks[2])
    qkv = lax.all_to_all(qkv, CTX, 0, 0, tiled=True)
    blocks.append(swap(blocks[6], ("x",), 1))
    qkv_y = swap(after(qkv, blocks[6]), ("y",), 1)
    qkv_c, qkv_y = after(qkv, blocks[5]), after(qkv_y, blocks[5])
    pieces = [qkv, swap(qkv_c, ("core",), 1), qkv_y, swap(qkv_y, ("core",), 1)]
    up = after(up_parts.reshape(8 * shard, wide), qkv)
    up = lax.all_to_all(up, GROUP, 0, 0, tiled=True)
    small = jnp.stack([piece[:, shard : shard + 10, :128] for piece in pieces])
    small = jnp.take(small, own_dp ^ jnp.arange(n_dp), axis=0).reshape(n_dp * n_ctx, 10, 128)
    vectors = small[:, :8, :shard].transpose(1, 0, 2).reshape(8, width).astype(f32)
    bias_up = small[:, 8].reshape(n_dp, n_z, 2, units)
    bias_up = lax.dynamic_slice(bias_up, (own_dp, 0, lax.axis_index("x"), 0), (1, n_z, 1, units))
    bias_up = bias_up.reshape(1, wide).astype(f32)
    tags = lax.dynamic_slice(small[:, 9], (own_dp * n_ctx, 0), (n_ctx, rows)).astype(jnp.int32)
    tags_row = jnp.take(tags, own_ctx ^ jnp.arange(n_ctx), axis=0).reshape(1, length)
    bias = lax.dynamic_slice(vectors, (0, own_ctx * cols), (2, cols))
    bias = jnp.concatenate([bias[:1], jnp.zeros((1, cols), f32), bias[1:]], axis=1)

    down = after(w_down, blocks[6])
    down_z = swap(down, ("z",), 2)
    down_lines = [down, swap(down, ("z",), 1), down_z, swap(down_z, ("z",), 1)]
    queries, keys, values, attended, message, totals, full_qkv = local(
        partial(attend_kernel, n_blocks=n_ctx, rows=rows, cols=cols),
        [like((length, cols), bf16)] * 3
        + [
            like((length, cols), f32),
            like((length, cols), bf16),
            like((8, length), f32),
            like((width, 3 * cols), bf16),
        ],
        place, *pieces, after(bias, down_z, down_lines[1]), tags_row, blocks, far=True, lazy=True,
        cost=10,
    )
    up_z = swap(up, ("z",), 2)
    up_lines = [up, swap(up, ("z",), 1), up_z, swap(up_z, ("z",), 1)]
    (full_out,) = local(
        order_out_kernel, [like((width, width), bf16)], place,
        *out_gather(after(w_out, blocks[2]), blocks[4], qkv, blocks[7], message), far=True,
        keep=(0,),
    )
    moved = lax.all_to_all(message, CTX, 0, 0, tiled=True).reshape(n_ctx, rows, cols)
    normed, normed_low, hat, rate = local(
        branch_kernel,
        [like((rows, width), f32), like((rows, width), bf16), like((rows, width), f32)]
        + [like((rows, 128), f32)],
        place, moved, full_out, inputs, vectors,
    )
    normed_all = group_gather(normed_low)
    full_up, down = local(
        order_kernel, [like((width, wide), bf16), like((wide, width), bf16)], place,
        after(up_lines[0], normed_all[1]), *up_lines[1:], *down_lines, far=True,
    )
    hidden, active, near, far = local(
        forward_kernel,
        [like((8 * rows, wide), f32), like((8 * rows, wide), bf16)]
        + [like((4 * rows, width), bf16)] * 2,
        place, full_up, bias_up, normed_all, down, far=True, keep=(0, 2, 3), lazy=True,
    )
    parts = group_scatter(near, far, place)
    hidden = after(hidden, parts[1])
    result, grad_second, grad_z, sums_two = local(
        second_kernel,
        [like((rows, width), bf16), like((rows, width), f32), like((rows, width), bf16)]
        + [like((8, width), f32)],
        place, normed, *parts, vectors, cotangent[0],
    )

    slope = 0.5 * (1 + lax.erf(hidden * 0.7071067811865476)) + hidden * (
        jnp.exp(-0.5 * hidden * hidden) * 0.3989422804014327
    )
    grad_z_all = group_gather(grad_z)
    grad_hidden, near, far = local(
        backward_kernel,
        [like((8 * rows, wide), bf16)] + [like((4 * rows, width), bf16)] * 2,
        place, *grad_z_all, full_up, down, slope,
    )
    down_near, down_far = local(
        down_grad_kernel, [like((2, units + 16, width), bf16)] * 2,
        place, grad_z_all, active, grad_hidden, far=True,
        scratch=[pltpu.VMEM((4, units + 16, width), bf16)],
    )
    parts = group_scatter(near, far, place, down_near)
    down_far = swap(down_far, ("z",), 1)
    up_near, up_far = local(
        up_grad_kernel, [like((2, 8 * shard, wide), bf16)] * 2,
        place, normed_all, after(grad_hidden, parts[1]), far=True,
        scratch=[pltpu.VMEM((4, 8 * shard, wide), bf16)],
    )
    grad_first, grad_branch, message, sums_one = local(
        first_kernel,
        [like((rows, width), f32), like((rows, width), bf16), like((n_ctx, rows, cols), bf16)]
        + [like((8, width), f32)],
        place, after(grad_second, up_near), *parts, vectors, hat, rate, full_out,
    )
    grad_moved = lax.all_to_all(message, CTX, 0, 0, tiled=True)
    high = rows + 16
    near, far = local(
        out_grad_kernel, [like((4 * high, width), bf16)] * 2, place, moved, grad_branch, sums_one,
        sums_two, far=True, scratch=[pltpu.VMEM((8, high, width), bf16)],
    )
    out_near, out_far = near, swap(far, ("core",), 1)
    turns = Turns(near)
    (down_far,) = turns.take(down_far)
    turns.last = down_sent = (down_near[1].astype(f32) + down_far[1].astype(f32)).astype(bf16)
    (grad_moved,) = turns.take(grad_moved)
    (mixed,) = local(
        attend_grad_kernel, [like((length, 3 * cols), bf16)],
        place, grad_moved, queries, keys, values, attended, totals, tags_row,
        far=True, cost=14,
        scratch=[
            pltpu.VMEM((length, cols), f32),
            pltpu.VMEM((length, cols), f32),
            pltpu.VMEM((length, cols), bf16),
        ],
    )
    up_far = swap(after(up_far, grad_moved), ("z",), 1)
    mixed = after(mixed, out_far)
    even_near, even_far, odd_near, odd_far, near, far = local(
        leave_kernel,
        [like((2 * rows, width), bf16)] * 4 + [like((2, width // 4 + 16, 3 * cols), bf16)] * 2,
        place, mixed, full_qkv, blocks, far=True, lazy=True, cost=4,
    )

    odd_far, far, down_last = swap(odd_far, ("x",), 1), swap(far, ("core",), 1), swap(down_sent, ("z",), 2)
    turns = Turns(near)
    down_last, up_far = turns.take(down_last, up_far)
    up_sent = (up_near[1].astype(f32) + up_far[1].astype(f32)).astype(bf16)
    up_last = swap(up_sent, ("z",), 2)
    down_sum = down_near[0].astype(f32) + down_far[0].astype(f32) + down_last.astype(f32)
    turns.last = up_sent
    (far,) = turns.take(far)
    qkv_sent = (near[1].astype(f32) + far[1].astype(f32)).astype(bf16)
    qkv_last = swap(qkv_sent, ("y",), 1)
    turns.last = qkv_sent
    (odd_far,) = turns.take(odd_far)
    even_far = swap(after(even_far, odd_far), ("x",), 1)
    odd = (odd_near.astype(f32) + odd_far.astype(f32)).astype(bf16)
    odd_last = swap(odd, ("z",), 1)
    turns.last = odd
    (up_last,) = turns.take(up_last)
    up_sum = up_near[0].astype(f32) + up_far[0].astype(f32) + up_last.astype(f32)
    turns.last = up_sum = up_sum.astype(bf16)
    up_sum = lax.all_to_all(up_sum, GROUP, 0, 0, tiled=True).reshape(8, shard, wide)
    (qkv_last,) = turns.take(qkv_last)
    qkv_sum = near[0].astype(f32) + far[0].astype(f32) + qkv_last.astype(f32)
    qkv_sum = qkv_sum.astype(bf16)
    qkv_rows = qkv_sum[: n_ctx * shard].reshape(n_ctx, shard, 3 * cols)
    qkv_bias = jnp.broadcast_to(qkv_sum[n_ctx * shard :], (n_ctx, 16, 3 * cols))
    turns.last = qkv_sum = jnp.concatenate([qkv_rows, qkv_bias], axis=1)
    (out_far,) = turns.take(out_far)
    out_parts = plane_scatter(out_near, out_far, place)
    turns.last = out_parts[0]
    even_far, odd_last = turns.take(even_far, odd_last)
    even = even_near.astype(f32) + even_far.astype(f32) + odd_last.astype(f32)
    final = swap(even[rows:].astype(bf16), ("z",), 2)
    turns.last = even
    up_sum, qkv_sum = turns.take(up_sum, qkv_sum)
    qkv_sum = lax.all_to_all(qkv_sum, CTX, 0, 0, tiled=True)
    (grad_wup,) = local(
        up_final_kernel, [like((shard, w_up.shape[1]), f32)], place, up_sum
    )
    turns.last = grad_wup
    out_parts = turns.take(*out_parts)
    line_near, line_far = local(
        out_line_kernel, [like((2, shard + 16, width), f32), like((2, shard + 16, width), bf16)],
        place, *out_parts,
        scratch=[pltpu.VMEM((4, shard + 16, width), f32)],
    )
    line_far = swap(line_far, ("z",), 1)
    turns.last = line_near
    (final,) = turns.take(final)
    turns.last = grad_inputs = (grad_first + even[:rows] + final.astype(f32)).astype(bf16)
    (line_far,) = turns.take(line_far)
    turns.last = line_sent = (line_near[1] + line_far[1].astype(f32)).astype(bf16)
    line_last = swap(line_sent, ("z",), 2)
    (qkv_sum,) = turns.take(qkv_sum)
    (grad_wqkv,) = local(
        qkv_final_kernel, [like((shard, 3 * width), f32)], place, qkv_sum
    )
    bias_sum = qkv_sum[:, shard].reshape(n_ctx, 3, cols).transpose(1, 0, 2).reshape(3, width)
    bias_own = lax.dynamic_slice(bias_sum, (0, own * shard), (3, shard)).astype(f32)
    turns.last = grad_wqkv
    (line_last,) = turns.take(line_last)
    out_sum = line_near[0] + line_far[0].astype(f32) + line_last.astype(f32)
    thin = out_sum[shard:, :shard]

    return (
        result[None],
        grad_inputs[None],
        grad_wqkv,
        bias_own[0],
        bias_own[2],
        out_sum[:shard],
        thin[0],
        thin[1],
        thin[2],
        grad_wup,
        down_sum[units, :units],
        down_sum[:units],
        thin[3],
        thin[4],
        thin[5],
    )


def call_heads(mesh, *arrays):
    grid = Mesh(mesh.devices.reshape(2, 2, 4, 2), EVERY)
    lines, lone, block = P(EVERY, None), P(EVERY), P(DP, CTX, None)
    in_specs = (
        block, lines, lone, lone, lines, lone, lone, lone, lines, lone, lines, lone, lone, lone,
        P(DP, CTX), P(DP, CTX), block,
    )
    out_specs = (
        block, block, lines, lone, lone, lines, lone, lone, lone, lines, lone, lines, lone, lone,
        lone,
    )
    return jax.shard_map(
        heads_body, mesh=grid, in_specs=in_specs, out_specs=out_specs, check_vma=False
    )(*arrays)


def call(mesh, *arrays):
    if mesh.shape["dp"] == 4 and mesh.shape["ctx"] == 8 and arrays[0].shape[1] == 1024:
        return call_heads(mesh, *arrays)
    return general_call(mesh)(*arrays)


def general_call(mesh):
    in_specs = (
        P("dp", "ctx", None),
        P(("dp", "ctx"), None),
        P(("dp", "ctx")),
        P(("dp", "ctx")),
        P(("dp", "ctx"), None),
        P(("dp", "ctx")),
        P(("dp", "ctx")),
        P(("dp", "ctx")),
        P(("dp", "ctx"), None),
        P(("dp", "ctx")),
        P(("dp", "ctx"), None),
        P(("dp", "ctx")),
        P(("dp", "ctx")),
        P(("dp", "ctx")),
        P("dp", "ctx"),
        P("dp", "ctx"),
        P("dp", "ctx", None),
    )
    out_specs = (
        P("dp", "ctx", None),
        P("dp", "ctx", None),
        P(("dp", "ctx"), None),
        P(("dp", "ctx")),
        P(("dp", "ctx")),
        P(("dp", "ctx"), None),
        P(("dp", "ctx")),
        P(("dp", "ctx")),
        P(("dp", "ctx")),
        P(("dp", "ctx"), None),
        P(("dp", "ctx")),
        P(("dp", "ctx"), None),
        P(("dp", "ctx")),
        P(("dp", "ctx")),
        P(("dp", "ctx")),
    )
    return jax.shard_map(general_body, mesh=mesh, in_specs=in_specs, out_specs=out_specs, check_vma=False)


def solution(mesh):
    return partial(call, mesh)
```
